32 devices in a mesh: ens: 2 (over y), dom: 16 (over z, x, core).
Axes of the slice: x: 2, y: 2, z: 4, core: 2. Of those that a mesh axis runs over, the one named last changes fastest.
Arguments:
- grid_feat: bfloat16 [32768, 227], P(('ens', 'dom')), parts along dimension 0, may hold values from -6 to 6
- mesh_latent: bfloat16 [16384, 512], P(('ens', 'dom')), parts along dimension 0, may hold values from -6 to 6
- cotangent: bfloat16 [16384, 512], P(('ens', 'dom')), parts along dimension 0, may hold values from -0.15625 to 0.15625
- row_pack: int32 [1024], P('dom'), may hold values from -1 to 1023, as said below
- edge_src: int32 [64, 1024], P('dom'), may hold values from 0 to 1087, as said below
- edge_dst: int32 [64, 1024], P('dom'), may hold values from 0 to 127
- edge_count: int32 [64], P('dom'), may hold values from 512 to 1024
- w_embed: bfloat16 [227, 512], replicated, may hold values from -0.375 to 0.375
- b_embed: bfloat16 [512], replicated, may hold values from -4 to 4
- w_src: bfloat16 [512, 512], replicated, may hold values from -0.25 to 0.25
- w_dst: bfloat16 [512, 512], replicated, may hold values from -0.25 to 0.25
- b_hidden: bfloat16 [512], replicated, may hold values from -4 to 4
- w_out: bfloat16 [512, 512], replicated, may hold values from -0.25 to 0.25
Outputs:
- mesh_out: bfloat16 [16384, 512], P(('ens', 'dom')), parts along dimension 0
- grad_embed: float32 [454, 512], P('ens'), parts along dimension 0
- grad_src: float32 [1024, 512], P('ens'), parts along dimension 0
- grad_dst: float32 [1024, 512], P('ens'), parts along dimension 0
- grad_out: float32 [1024, 512], P('ens'), parts along dimension 0
- grad_biases: float32 [4, 512], P('ens'), parts along dimension 0
The draws below stay inside these ranges and needn't reach their ends.
There are 2 independent parts, one for each index of `ens`. The reference program is written for one: setup_inputs(seed, part) draws one part's arguments, and reference() takes and returns one part's arrays. A program takes and returns all parts, laid end to end along the dimension named above; an argument that names none is the same for every part. Nothing has to cross between parts.
Inputs may be any that keep to these rules, and one draw needn't show every extreme that they name: `row_pack`: entries of band s, in order of partition d and slot k: the local row of s that goes to d, or -1; filled slots of a pair come first; no row is named twice; a band sends nothing to itself. `edge_src`: edges name only filled buffer rows, and never a home row that its band sends away.
All inputs are finite; a program needn't handle non-finite values.
Results may differ from the reference program's by a relative error of at most 0.0062.
Values may be sent and summed in bfloat16 or wider, within the bound.
No kernel may reach another device: no remote copies, remote signals or barrier semaphores. Data moves between devices by JAX's collectives and lax.ppermute only.
A program may use at most 128 MiB of HBM per device.

```python
import jax
import jax.numpy as jnp
from jax import lax

C = 227
L = 512
G_DEV = 1024
PEER = 4
MB = 4
BLOCK = 128
EMAX = 1024
GRID = 16384
BLOCKS = 64
NODES = 8192
N_DOM = 16


def permute_rows(one_key):
    return jax.random.permutation(one_key, G_DEV)


def shared_tables(key):
    order_key = jax.random.fold_in(key, 11)
    count_key = jax.random.fold_in(key, 12)
    orders = jax.vmap(permute_rows)(jax.random.split(order_key, N_DOM)).astype(jnp.int32)
    source = jnp.arange(N_DOM, dtype=jnp.int32)[:, None]
    target = jnp.arange(N_DOM, dtype=jnp.int32)[None, :]
    counts = jax.random.randint(count_key, (N_DOM, N_DOM), 0, PEER + 1, dtype=jnp.int32)
    counts = jnp.where(source == target, 0, counts)
    counts = jnp.where(target == (source + 1) % N_DOM, PEER, counts)
    band_ids = jnp.arange(N_DOM, dtype=jnp.int32)
    marked = orders[band_ids, (band_ids + 1) % N_DOM * PEER]
    shifts = (G_DEV - 1 - marked) % G_DEV
    rows_table = (orders + shifts[:, None]) % G_DEV
    zero_pos = jnp.argmax(rows_table == 0, axis=1).astype(jnp.int32)
    last_vals = rows_table[:, G_DEV - 1]
    rows_table = rows_table.at[band_ids, zero_pos].set(last_vals)
    rows_table = rows_table.at[:, G_DEV - 1].set(0)
    return (rows_table.astype(jnp.int32), counts)


def draw_row_pack(key, part):
    rows_table, counts = shared_tables(key)
    chosen = rows_table[:, :N_DOM * PEER].reshape(N_DOM, N_DOM, PEER)
    slot_index = jnp.arange(PEER, dtype=jnp.int32)
    filled = slot_index[None, None, :] < counts[:, :, None]
    return jnp.where(filled, chosen, -1).reshape(-1).astype(jnp.int32)


def draw_edge_src(key, part):
    rows_table, counts = shared_tables(key)
    key = jax.random.fold_in(key, 3)
    key_list = jax.random.split(key, 4)
    block_total = MB * N_DOM
    shape = (block_total, EMAX)
    device = jnp.broadcast_to((jnp.arange(block_total, dtype=jnp.int32) // MB)[:, None], shape)
    own_pick = jax.random.randint(key_list[0], shape, N_DOM * PEER, G_DEV, dtype=jnp.int32)
    own_row = rows_table[device, own_pick]
    source = jax.random.randint(key_list[1], shape, 0, N_DOM, dtype=jnp.int32)
    slot_k = jax.random.randint(key_list[2], shape, 0, PEER, dtype=jnp.int32)
    choose_own = jax.random.randint(key_list[3], shape, 0, 10, dtype=jnp.int32) < 7
    usable = slot_k < counts[source, device]
    incoming = G_DEV + source * PEER + slot_k
    result = jnp.where(choose_own | ~usable, own_row, incoming)
    result = result.at[0, 0].set(G_DEV + N_DOM * PEER - 1)
    result = result.at[0, 1].set(rows_table[0, G_DEV - 1])
    return result.astype(jnp.int32)


def with_ends(array, key, smallest, largest):
    longest = array.shape.index(max(array.shape))
    spots = []
    for shift in (0, 1):
        where = [jax.random.randint(jax.random.fold_in(key, axis), (), 0, length) for axis, length in enumerate(array.shape)]
        where[longest] = (where[longest] + shift) % array.shape[longest]
        spots.append(tuple(where))
    return array.at[spots[0]].set(smallest).at[spots[1]].set(largest)


def steps_of(rng, extent, pieces, least, largest):
    def one(position, blocks):
        heights = jax.random.uniform(jax.random.fold_in(jax.random.fold_in(rng, 6), position), (blocks,), jnp.float32, least / len(pieces), largest / len(pieces))
        return jnp.repeat(jnp.exp(heights), extent[position] // blocks).reshape((-1,) + (1,) * (len(extent) - position - 1))

    loudness = one(*pieces[0])
    for cut in pieces[1:]:
        loudness = loudness * one(*cut)
    return loudness


def gaussian(key, extent, deviation, limit, shards=(), kind=jnp.bfloat16):
    gain = steps_of(key, extent, shards, -0.22, 0.18) if shards else 1.0
    array = jax.random.normal(key, extent, jnp.float32) * deviation * gain
    return jnp.minimum(jnp.maximum(array, -limit), limit).astype(kind)


def setup_inputs(seed: int = 0, part: int = 0) -> dict:
    keys = jax.random.split(jax.random.key(seed), 14)
    part_splits = jax.random.split(jax.random.fold_in(keys[13], part), 14)
    grid_feat = gaussian(part_splits[0], (GRID, C), 1.0, 6.0, ((0, 16),))
    mesh_latent = gaussian(part_splits[1], (NODES, L), 1.0, 6.0, ((0, 16),))
    cotangent = gaussian(part_splits[2], (NODES, L), (1.0 / (MB * BLOCK * N_DOM) ** 0.5), 0.15625, ((0, 16),))
    row_pack = draw_row_pack(jax.random.fold_in(keys[13], 71), part)
    edge_src = draw_edge_src(jax.random.fold_in(keys[13], 71), part)
    edge_dst = with_ends(jax.random.randint(keys[5], (BLOCKS, EMAX), 0, BLOCK), jax.random.fold_in(keys[5], 1), 0, BLOCK - 1).astype(jnp.int32)
    edge_count = with_ends(jax.random.randint(keys[6], (BLOCKS,), EMAX // 2, EMAX + 1), jax.random.fold_in(keys[6], 1), EMAX // 2, EMAX).astype(jnp.int32)
    w_embed = gaussian(keys[7], (C, L), C ** -0.5, 0.375)
    b_embed = gaussian(keys[8], (L,), 1.0, 4.0)
    w_src = gaussian(keys[9], (L, L), L ** -0.5, 0.25)
    w_dst = gaussian(keys[10], (L, L), L ** -0.5, 0.25)
    b_hidden = gaussian(keys[11], (L,), 1.0, 4.0)
    w_out = gaussian(keys[12], (L, L), L ** -0.5, 0.25)
    return dict(grid_feat=grid_feat, mesh_latent=mesh_latent, cotangent=cotangent, row_pack=row_pack, edge_src=edge_src, edge_dst=edge_dst, edge_count=edge_count, w_embed=w_embed, b_embed=b_embed, w_src=w_src, w_dst=w_dst, b_hidden=b_hidden, w_out=w_out)


def silu_slope(values):
    sig = jax.nn.sigmoid(values)
    return sig * (1.0 + values * (1.0 - sig))


def reference(grid_feat, mesh_latent, cotangent, row_pack, edge_src, edge_dst, edge_count, w_embed, b_embed, w_src, w_dst, b_hidden, w_out):
    pre_embed = jnp.dot(grid_feat, w_embed, preferred_element_type=jnp.float32) + b_embed.astype(jnp.float32)
    latent = jax.nn.silu(pre_embed).astype(jnp.bfloat16)
    packs = row_pack.reshape(N_DOM, N_DOM, PEER)
    sources = jnp.arange(N_DOM, dtype=jnp.int32)
    node_total = MB * BLOCK

    def device_step(carry_state, device):
        latent_grad, grad_src, grad_dst, grad_out, grad_bias = carry_state
        own_rows = lax.dynamic_slice_in_dim(latent, device * G_DEV, G_DEV, 0)
        pack_column = lax.dynamic_index_in_dim(packs, device, 1, keepdims=False)
        filled = (pack_column >= 0).reshape(-1)
        row_ids = (sources[:, None] * G_DEV + jnp.maximum(pack_column, 0)).reshape(-1).astype(jnp.int32)
        incoming = jnp.where(filled[:, None], latent[row_ids], jnp.zeros((), jnp.bfloat16))
        buffer = jnp.concatenate([own_rows, incoming], axis=0)
        proj_src = jnp.dot(buffer, w_src, preferred_element_type=jnp.float32).astype(jnp.bfloat16)
        node_rows = lax.dynamic_slice_in_dim(mesh_latent, device * node_total, node_total, 0)
        cot_rows = lax.dynamic_slice_in_dim(cotangent, device * node_total, node_total, 0)
        proj_dst = jnp.dot(node_rows, w_dst, preferred_element_type=jnp.float32).astype(jnp.bfloat16)
        src_slots = lax.dynamic_slice_in_dim(edge_src, device * MB, MB, 0)
        dst_nodes = lax.dynamic_slice_in_dim(edge_dst, device * MB, MB, 0)
        live_count = lax.dynamic_slice_in_dim(edge_count, device * MB, MB, 0)
        target_node = (jnp.arange(MB, dtype=jnp.int32)[:, None] * BLOCK + dst_nodes).reshape(-1)
        live_edge = (jnp.arange(EMAX, dtype=jnp.int32)[None, :] < live_count[:, None]).reshape(-1)
        flat_src = src_slots.reshape(-1)
        pre_edge = proj_src[flat_src].astype(jnp.float32) + proj_dst[target_node].astype(jnp.float32) + b_hidden.astype(jnp.float32)
        hidden = jax.nn.silu(pre_edge).astype(jnp.bfloat16)
        message = jnp.dot(hidden, w_out, preferred_element_type=jnp.float32) * live_edge[:, None].astype(jnp.float32)
        summed = jax.ops.segment_sum(message, target_node, num_segments=node_total)
        out_rows = (node_rows.astype(jnp.float32) + summed).astype(jnp.bfloat16)
        msg_grad = jnp.where(live_edge[:, None], cot_rows[target_node], jnp.zeros((), jnp.bfloat16))
        grad_out = grad_out + jnp.dot(hidden.T, msg_grad, preferred_element_type=jnp.float32)
        hidden_grad = jnp.dot(msg_grad, w_out.T, preferred_element_type=jnp.float32)
        pre_grad = (hidden_grad * silu_slope(pre_edge)).astype(jnp.bfloat16)
        grad_bias = grad_bias + jnp.sum(pre_grad.astype(jnp.float32), axis=0)
        node_grad = jax.ops.segment_sum(pre_grad.astype(jnp.float32), target_node, num_segments=node_total).astype(jnp.bfloat16)
        grad_dst = grad_dst + jnp.dot(node_rows.T, node_grad, preferred_element_type=jnp.float32)
        slot_grad = jax.ops.segment_sum(pre_grad.astype(jnp.float32), flat_src, num_segments=G_DEV + N_DOM * PEER).astype(jnp.bfloat16)
        grad_src = grad_src + jnp.dot(buffer.T, slot_grad, preferred_element_type=jnp.float32)
        buffer_grad = jnp.dot(slot_grad, w_src.T, preferred_element_type=jnp.float32)
        home_part = lax.dynamic_slice_in_dim(latent_grad, device * G_DEV, G_DEV, 0) + buffer_grad[:G_DEV]
        latent_grad = lax.dynamic_update_slice_in_dim(latent_grad, home_part, device * G_DEV, 0)
        latent_grad = latent_grad.at[row_ids].add(jnp.where(filled[:, None], buffer_grad[G_DEV:], jnp.float32(0.0)))
        return (latent_grad, grad_src, grad_dst, grad_out, grad_bias), out_rows

    width = w_src.shape[1]
    start_state = (jnp.zeros((G_DEV * N_DOM, width), jnp.float32), jnp.zeros((width, width), jnp.float32), jnp.zeros((width, width), jnp.float32), jnp.zeros((width, width), jnp.float32), jnp.zeros((width,), jnp.float32))
    final_state, out_blocks = lax.scan(device_step, start_state, sources)
    latent_grad, grad_src, grad_dst, grad_out, grad_bias = final_state
    mesh_out = out_blocks.reshape(N_DOM * node_total, width)
    embed_grad = (latent_grad * silu_slope(pre_embed)).astype(jnp.bfloat16)
    grad_embed = jnp.dot(grid_feat.T, embed_grad, preferred_element_type=jnp.float32)
    grad_biases = jnp.stack([jnp.sum(embed_grad.astype(jnp.float32), axis=0), grad_bias])
    return (mesh_out, grad_embed, grad_src, grad_dst, grad_out, grad_biases)
```

```python
import functools

import jax
import jax.numpy as jnp
from jax import lax
from jax.experimental import pallas as pl
from jax.experimental.pallas import tpu as pltpu
from jax.sharding import PartitionSpec as P

BF16 = jnp.bfloat16
F32 = jnp.float32
VMEM_BYTES = 60 * 1024 * 1024


def mm(left, right, left_dim=1, right_dim=0):
    return lax.dot_general(
        left, right, (((left_dim,), (right_dim,)), ((), ())), preferred_element_type=F32
    )


def sigmoid(values):
    return 0.5 * jnp.tanh(0.5 * values) + 0.5


def round_up(value, step):
    return -(-value // step) * step


def own_kernel(feat, w_embed, w_src, mesh, w_dst, cot, w_out, latent, proj, near, back):
    rows = feat.shape[0]
    step = 256

    def body(i, carry):
        part = pl.ds(pl.multiple_of(i * step, step), step)
        pre = mm(feat[part, :], w_embed[...])
        lat = (pre * sigmoid(pre)).astype(BF16)
        latent[part, :] = lat
        proj[part, :] = mm(lat, w_src[...]).astype(BF16)
        return carry

    lax.fori_loop(0, rows // step, body, 0)
    near[...] = mm(mesh[...], w_dst[...]).astype(BF16)
    back[...] = mm(cot[...], w_out[...], 1, 1).astype(BF16)


def edge_kernel(
    channels,
    count,
    src,
    dst,
    feat_in,
    feat_own,
    w_embed,
    w_src,
    w_out,
    b_hidden,
    latent_own,
    proj_own,
    near,
    back,
    mesh,
    cot,
    mesh_out,
    grads,
    table,
    latent,
    feat,
    one_hot,
    one_hot_t,
    hid,
    pgrad,
    slot_sum,
    node_sum,
    hid_sum,
    bias_sum,
):
    own = feat_own.shape[0]
    more = feat_in.shape[0]
    slots = own + more
    blocks, edges = src.shape
    width = w_src.shape[0]
    block = mesh.shape[0] // blocks
    depth = table.shape[0]
    step = 256

    feat[0:own, :] = feat_own[...]
    feat[own:slots, :] = feat_in[...]
    latent[0:own, :] = latent_own[...]
    pre_in = mm(feat_in[...], w_embed[...])
    lat_in = (pre_in * sigmoid(pre_in)).astype(BF16)
    latent[own:slots, :] = lat_in
    table[0:own, :] = proj_own[...]
    table[own:slots, :] = mm(lat_in, w_src[...]).astype(BF16)
    tail = depth - slots - block
    tail_row = lax.broadcasted_iota(jnp.int32, (tail, width), 0)
    table[slots + block : depth, :] = jnp.where(
        tail_row == 0, jnp.broadcast_to(b_hidden[...], (tail, width)).astype(F32), 0.0
    ).astype(BF16)
    slot_sum[...] = jnp.zeros_like(slot_sum)
    bias_sum[...] = jnp.zeros_like(bias_sum)

    edge_lane = lax.broadcasted_iota(jnp.int32, (blocks, edges), 1)
    block_row = lax.broadcasted_iota(jnp.int32, (blocks, 1), 0)
    counts = jnp.zeros((blocks, 1), jnp.int32)
    for b in range(blocks):
        counts = jnp.where(block_row == b, count[b], counts)
    src_all = src[...]
    dst_all = jnp.where(edge_lane < counts, dst[...] + slots, -1)
    columns = jnp.transpose(jnp.concatenate([src_all, dst_all], axis=0))

    for b in range(blocks):
        rows = slice(b * block, (b + 1) * block)
        table[slots : slots + block, :] = near[rows, :]
        src_row = src_all[b : b + 1, :]
        dst_row = dst_all[b : b + 1, :]
        back_b = back[rows, :]
        for e in range(0, edges, step):
            src_col = columns[e : e + step, b : b + 1]
            dst_col = columns[e : e + step, blocks + b : blocks + b + 1]
            lane = lax.broadcasted_iota(jnp.int32, (step, depth), 1)
            hot = (lane == src_col) | (lane == dst_col) | (lane == slots + block)
            hot = jnp.where(hot, 1.0, 0.0).astype(BF16)
            one_hot[e : e + step, :] = hot
            pre = mm(hot, table[...])
            grad = mm(hot[:, slots : slots + block], back_b)
            sig = sigmoid(pre)
            act = pre * sig
            hid[e : e + step, :] = act.astype(BF16)
            pgrad[e : e + step, :] = (grad * (sig + act * (1.0 - sig))).astype(BF16)
        for r in range(0, depth, 128):
            sub = lax.broadcasted_iota(jnp.int32, (128, edges), 0) + r
            hot_t = (sub == src_row) | (sub == dst_row) | (sub == slots + block)
            one_hot_t[r : r + 128, :] = jnp.where(hot_t, 1.0, 0.0).astype(BF16)
        slot_sum[...] += mm(one_hot_t[0:slots, :], pgrad[...])
        node = mm(one_hot_t[slots:depth, :], pgrad[...])
        node_sum[rows, :] = node[0:block, :].astype(BF16)
        bias_sum[...] += node[block : block + 8, :]
        hid_sum[rows, :] = mm(one_hot_t[slots : slots + block, :], hid[...]).astype(BF16)

    total = hid_sum[...]
    mesh_out[...] = (mesh[...].astype(F32) + mm(total, w_out[...])).astype(BF16)
    grads[0:width, :] = mm(total, cot[...], 0, 0).astype(BF16)
    grads[width : 2 * width, :] = mm(mesh[...], node_sum[...], 0, 0).astype(BF16)
    slot_grad = slot_sum[...].astype(BF16)
    grads[2 * width : 3 * width, :] = mm(latent[...], slot_grad, 0, 0).astype(BF16)
    buffer_grad = mm(slot_grad, w_src[...], 1, 1)
    pre = mm(feat[...], w_embed[...])
    sig = sigmoid(pre)
    embed = (buffer_grad * (sig * (1.0 + pre * (1.0 - sig)))).astype(BF16)
    padded = feat.shape[1]
    grad_embed = mm(feat[...], embed, 0, 0)
    bias_row = lax.broadcasted_iota(jnp.int32, (padded, width), 0)
    grad_embed = jnp.where(bias_row == channels + 1, bias_sum[0:1, :], grad_embed)
    grads[3 * width : 3 * width + padded, :] = grad_embed.astype(BF16)
    if grads.shape[0] > 3 * width + padded:
        rest = grads.shape[0] - 3 * width - padded
        grads[3 * width + padded :, :] = jnp.zeros((rest, width), BF16)


def shards(
    grid_feat,
    mesh_latent,
    cotangent,
    row_pack,
    edge_src,
    edge_dst,
    edge_count,
    w_embed,
    b_embed,
    w_src,
    w_dst,
    b_hidden,
    w_out,
):
    device_count = lax.axis_size("dom")
    me = lax.axis_index("dom")
    own, channels = grid_feat.shape
    width = w_src.shape[0]
    peer_slots = row_pack.shape[0] // device_count
    more = device_count * peer_slots
    slots = own + more
    blocks, edges = edge_src.shape
    nodes = mesh_latent.shape[0]
    block = nodes // blocks
    padded = round_up(channels + 2, 128)
    depth = round_up(slots + block + 1, 256)
    grad_rows = round_up(3 * width + padded, 16 * device_count)

    feat = jnp.concatenate(
        [grid_feat, jnp.ones((own, 1), BF16), jnp.zeros((own, padded - channels - 1), BF16)], axis=1
    )
    w_pad = jnp.concatenate(
        [w_embed, b_embed[None, :], jnp.zeros((padded - channels - 1, width), BF16)], axis=0
    )
    pick = (row_pack[:, None] == lax.broadcasted_iota(jnp.int32, (1, own), 1)).astype(BF16)
    send = jnp.dot(pick, feat, preferred_element_type=F32).astype(BF16)
    feat_in = lax.all_to_all(
        send.reshape(device_count, peer_slots, padded), "dom", split_axis=0, concat_axis=0, tiled=True
    ).reshape(more, padded)

    vmem = pl.BlockSpec(memory_space=pltpu.VMEM)
    smem = pl.BlockSpec(memory_space=pltpu.SMEM)
    params = pltpu.CompilerParams(vmem_limit_bytes=VMEM_BYTES)
    own_macs = own * width * (padded + width) + 2 * nodes * width * width
    latent, proj, near, back = pl.pallas_call(
        own_kernel,
        out_shape=(
            jax.ShapeDtypeStruct((own, width), BF16),
            jax.ShapeDtypeStruct((own, width), BF16),
            jax.ShapeDtypeStruct((nodes, width), BF16),
            jax.ShapeDtypeStruct((nodes, width), BF16),
        ),
        in_specs=[vmem] * 7,
        out_specs=(vmem,) * 4,
        compiler_params=params,
        cost_estimate=pl.CostEstimate(
            flops=2 * own_macs, bytes_accessed=8 * own * width, transcendentals=own * width
        ),
        name="own_rows",
    )(feat, w_pad, w_src, mesh_latent, w_dst, cotangent, w_out)

    edge_macs = blocks * edges * width * (2 * depth + 2 * block)
    mesh_out, grads = pl.pallas_call(
        functools.partial(edge_kernel, channels),
        out_shape=(
            jax.ShapeDtypeStruct((nodes, width), BF16),
            jax.ShapeDtypeStruct((grad_rows, width), BF16),
        ),
        in_specs=[smem] + [vmem] * 14,
        out_specs=(vmem,) * 2,
        scratch_shapes=[
            pltpu.VMEM((depth, width), BF16),
            pltpu.VMEM((slots, width), BF16),
            pltpu.VMEM((slots, padded), BF16),
            pltpu.VMEM((edges, depth), BF16),
            pltpu.VMEM((depth, edges), BF16),
            pltpu.VMEM((edges, width), BF16),
            pltpu.VMEM((edges, width), BF16),
            pltpu.VMEM((slots, width), F32),
            pltpu.VMEM((nodes, width), BF16),
            pltpu.VMEM((nodes, width), BF16),
            pltpu.VMEM((8, width), F32),
        ],
        compiler_params=params,
        cost_estimate=pl.CostEstimate(
            flops=2 * edge_macs, bytes_accessed=8 * own * width, transcendentals=blocks * edges * width
        ),
        name="edge_rows",
    )(
        edge_count,
        edge_src,
        edge_dst,
        feat_in,
        feat,
        w_pad,
        w_src,
        w_out,
        b_hidden[None, :],
        latent,
        proj,
        near,
        back,
        mesh_latent,
        cotangent,
    )

    core = me % 2
    swap = [(i, i ^ 1) for i in range(device_count)]
    half = grad_rows // 2
    chips = device_count // 2
    groups = [[2 * c + k for c in range(chips)] for k in range(2)]
    kept = lax.dynamic_slice_in_dim(grads, core * half, half, 0)
    sent = lax.dynamic_slice_in_dim(grads, (1 - core) * half, half, 0)
    got = lax.ppermute(sent, "dom", swap)
    pair = (kept.astype(F32) + got.astype(F32)).astype(BF16)
    parts = lax.all_to_all(
        pair.reshape(chips, half // chips, width),
        "dom",
        split_axis=0,
        concat_axis=0,
        axis_index_groups=groups,
        tiled=True,
    )
    mine = jnp.sum(parts.astype(F32), axis=0).astype(BF16)
    spread = lax.all_to_all(
        jnp.broadcast_to(mine[None], parts.shape),
        "dom",
        split_axis=0,
        concat_axis=0,
        axis_index_groups=groups,
        tiled=True,
    ).reshape(half, width)
    other = lax.ppermute(spread, "dom", swap)
    low = jnp.where(core == 0, spread, other)
    high = jnp.where(core == 0, other, spread)
    total = jnp.concatenate([low, high], axis=0).astype(F32)
    base = 3 * width
    return (
        mesh_out,
        total[base : base + channels],
        total[2 * width : base],
        total[width : 2 * width],
        total[0:width],
        total[base + channels : base + channels + 2],
    )


def solution(mesh):
    return jax.shard_map(
        shards,
        mesh=mesh,
        in_specs=(
            P(("ens", "dom"), None),
            P(("ens", "dom"), None),
            P(("ens", "dom"), None),
            P("dom"),
            P("dom", None),
            P("dom", None),
            P("dom"),
            P(),
            P(),
            P(),
            P(),
            P(),
            P(),
        ),
        out_specs=(
            P(("ens", "dom"), None),
            P("ens", None),
            P("ens", None),
            P("ens", None),
            P("ens", None),
            P("ens", None),
        ),
        check_vma=False,
    )
```

```python
import functools

import jax
import jax.numpy as jnp
from jax import lax
from jax.experimental import pallas as pl
from jax.experimental.pallas import tpu as pltpu
from jax.sharding import PartitionSpec as P

BF16 = jnp.bfloat16
F32 = jnp.float32
VMEM_BYTES = 60 * 1024 * 1024


def mm(left, right, left_dim=1, right_dim=0):
    return lax.dot_general(
        left, right, (((left_dim,), (right_dim,)), ((), ())), preferred_element_type=F32
    )


def sigmoid(values):
    return 0.5 * jnp.tanh(0.5 * values) + 0.5


def round_up(value, step):
    return -(-value // step) * step


def pick_kernel(row_pack, grid_feat, feat, send):
    own, channels = grid_feat.shape
    padded = feat.shape[1]
    peers, peer_slots = send.shape[0], send.shape[1]
    last = padded - 128
    lane = lax.broadcasted_iota(jnp.int32, (own, 128), 1) + last
    feat[:, last:padded] = jnp.where(lane == channels, 1.0, 0.0).astype(BF16)
    feat[:, 0:channels] = grid_feat[...]
    row = lax.broadcasted_iota(jnp.int32, (own, peers * peer_slots), 0)
    pick = jnp.where(row == row_pack[...], 1.0, 0.0).astype(BF16)
    rows = mm(pick, feat[...], 0, 0)
    for j in range(peers):
        send[j] = rows[j * peer_slots : (j + 1) * peer_slots, :].astype(BF16)


def own_kernel(
    feat, w_embed, b_embed, w_src, mesh, w_dst, cot, w_out, latent, proj, near, back, w_pad, wide
):
    rows = feat.shape[0]
    channels = w_embed.shape[0]
    step = 256
    wide[...] = jnp.zeros_like(wide)
    wide[0:channels, :] = w_embed[...].astype(F32)
    wide[channels : channels + 1, :] = b_embed[...].astype(F32)
    w_pad[...] = wide[...].astype(BF16)

    def body(i, carry):
        part = pl.ds(pl.multiple_of(i * step, step), step)
        pre = mm(feat[part, :], w_pad[...])
        lat = (pre * sigmoid(pre)).astype(BF16)
        latent[part, :] = lat
        proj[part, :] = mm(lat, w_src[...]).astype(BF16)
        return carry

    lax.fori_loop(0, rows // step, body, 0)
    near[...] = mm(mesh[...], w_dst[...]).astype(BF16)
    full = mm(cot[...], w_out[...], 1, 1)
    high = full.astype(BF16)
    back[0] = high
    back[1] = (full - high.astype(F32)).astype(BF16)


def stage_bits(device_count):
    bits = device_count.bit_length() - 1
    first = list(range(1, bits - 1))
    second = first[1::-1] + first[2:]
    return first, second, bits - 1


def position_mask(me, order):
    mask = 0
    for i, bit in enumerate(order):
        mask = mask + (lax.rem(me // (1 << bit), 2) << (len(order) - 1 - i))
    return mask


def edge_kernel(
    channels,
    device_count,
    count,
    src,
    dst,
    feat_in,
    feat_own,
    w_embed,
    w_src,
    w_out,
    b_hidden,
    latent_own,
    proj_own,
    near,
    back,
    mesh,
    cot,
    mesh_out,
    kept,
    sent,
    table,
    pair,
    latent,
    feat,
    incoming,
    one_hot,
    one_hot_t,
    hid,
    pgrad,
    slot_sum,
    node_sum,
    hid_sum,
    bias_sum,
    grads,
):
    own = feat_own.shape[0]
    peers, peer_slots, padded = feat_in.shape
    more = peers * peer_slots
    slots = own + more
    blocks, edges = src.shape
    width = w_src.shape[0]
    block = mesh.shape[0] // blocks
    depth = table.shape[0]
    step = 256

    feat[0:own, :] = feat_own[...]
    for j in range(peers):
        incoming[j * peer_slots : (j + 1) * peer_slots, :] = feat_in[j].astype(F32)
    feat[own:slots, :] = incoming[...].astype(BF16)
    latent[0:own, :] = latent_own[...]
    pre_in = mm(feat[own:slots, :], w_embed[...])
    lat_in = (pre_in * sigmoid(pre_in)).astype(BF16)
    latent[own:slots, :] = lat_in
    table[block : block + own, :] = proj_own[...]
    table[block + own : block + slots, :] = mm(lat_in, w_src[...]).astype(BF16)
    tail = depth - slots - block
    tail_row = lax.broadcasted_iota(jnp.int32, (tail, width), 0)
    table[slots + block : depth, :] = jnp.where(
        tail_row == 0, jnp.broadcast_to(b_hidden[...], (tail, width)).astype(F32), 0.0
    ).astype(BF16)
    slot_sum[...] = jnp.zeros_like(slot_sum)
    bias_sum[...] = jnp.zeros_like(bias_sum)

    edge_lane = lax.broadcasted_iota(jnp.int32, (blocks, edges), 1)
    block_row = lax.broadcasted_iota(jnp.int32, (blocks, 1), 0)
    counts = jnp.zeros((blocks, 1), jnp.int32)
    for b in range(blocks):
        counts = jnp.where(block_row == b, count[b], counts)
    src_all = src[...]
    dst_all = jnp.where(edge_lane < counts, dst[...], -1)
    columns = jnp.transpose(jnp.concatenate([src_all, dst_all], axis=0))

    for b in range(blocks):
        rows = slice(b * block, (b + 1) * block)
        table[0:block, :] = near[rows, :]
        pair[0:block, :] = back[0, rows, :]
        pair[block : 2 * block, :] = back[1, rows, :]
        src_row = src_all[b : b + 1, :]
        dst_row = dst_all[b : b + 1, :]
        for e in range(0, edges, step):
            src_col = columns[e : e + step, b : b + 1]
            dst_col = columns[e : e + step, blocks + b : blocks + b + 1]
            lane = lax.broadcasted_iota(jnp.int32, (step, block), 1)
            near_hot = jnp.where(lane == dst_col, 1.0, 0.0).astype(BF16)
            one_hot[e : e + step, 0:block] = near_hot
            one_hot[e : e + step, block : 2 * block] = near_hot
            for k in range(0, depth - block, 128):
                lane = lax.broadcasted_iota(jnp.int32, (step, 128), 1) + k
                hot = lane == src_col
                if k <= slots < k + 128:
                    hot = hot | (lane == slots)
                hot = jnp.where(hot, 1.0, 0.0).astype(BF16)
                one_hot[e : e + step, 2 * block + k : 2 * block + k + 128] = hot
            pre = mm(one_hot[e : e + step, block : block + depth], table[...])
            grad = mm(one_hot[e : e + step, 0 : 2 * block], pair[...])
            sig = sigmoid(pre)
            act = pre * sig
            hid[e : e + step, :] = act.astype(BF16)
            pgrad[e : e + step, :] = (grad * (sig + act * (1.0 - sig))).astype(BF16)
        sub = lax.broadcasted_iota(jnp.int32, (block, edges), 0)
        one_hot_t[0:block, :] = jnp.where(sub == dst_row, 1.0, 0.0).astype(BF16)
        for r in range(0, depth - block, 128):
            sub = lax.broadcasted_iota(jnp.int32, (128, edges), 0) + r
            hot = sub == src_row
            if r <= slots < r + 128:
                hot = hot | (sub == slots)
            one_hot_t[block + r : block + r + 128, :] = jnp.where(hot, 1.0, 0.0).astype(BF16)
        slot_sum[...] += mm(one_hot_t[block : block + slots, :], pgrad[...])
        bias_sum[...] += mm(one_hot_t[block + slots : block + slots + 16, :], pgrad[...])
        node_sum[rows, :] = mm(one_hot_t[0:block, :], pgrad[...]).astype(BF16)
        hid_sum[rows, :] = mm(one_hot_t[0:block, :], hid[...]).astype(BF16)

    total = hid_sum[...]
    mesh_out[...] = (mesh[...].astype(F32) + mm(total, w_out[...])).astype(BF16)
    grads[0:width, :] = mm(total, cot[...], 0, 0)
    grads[width : 2 * width, :] = mm(mesh[...], node_sum[...], 0, 0)
    slot_grad = slot_sum[...].astype(BF16)
    grads[2 * width : 3 * width, :] = mm(latent[...], slot_grad, 0, 0)
    buffer_grad = mm(slot_grad, w_src[...], 1, 1)
    pre = mm(feat[...], w_embed[...])
    sig = sigmoid(pre)
    embed = (buffer_grad * (sig * (1.0 + pre * (1.0 - sig)))).astype(BF16)
    base = 3 * width
    grads[base : base + padded, :] = mm(feat[...], embed, 0, 0)
    grads[base + channels + 1 : base + channels + 2, :] = bias_sum[0:1, :]
    if grads.shape[0] > base + padded:
        rest = grads.shape[0] - base - padded
        grads[base + padded :, :] = jnp.zeros((rest, width), F32)

    me = lax.axis_index("dom")
    core = lax.rem(me, 2)
    first, second, _ = stage_bits(device_count)
    masks = position_mask(me, first), position_mask(me, second)
    mine = jnp.where(core == 0, masks[0], masks[1])
    theirs = jnp.where(core == 0, masks[1], masks[0])
    pieces = 1 << len(first)
    piece = kept.shape[0] // pieces
    for p in range(pieces):
        at = pl.ds(pl.multiple_of((core * pieces + (mine ^ p)) * piece, 16), piece)
        kept[p * piece : (p + 1) * piece, :] = grads[at, :]
        at = pl.ds(pl.multiple_of(((1 - core) * pieces + (theirs ^ p)) * piece, 16), piece)
        sent[p * piece : (p + 1) * piece, :] = grads[at, :].astype(BF16)


def unpack_kernel(channels, device_count, total, grad_embed, grad_src, grad_dst, grad_out, biases):
    width = total.shape[1]
    me = lax.axis_index("dom")
    core = lax.rem(me, 2)
    first, second, _ = stage_bits(device_count)
    masks = position_mask(me, first), position_mask(me, second)
    pieces = 1 << len(first)
    piece = total.shape[0] // (2 * pieces)
    base = 3 * width
    bounds = (
        (0, width, grad_out),
        (width, 2 * width, grad_dst),
        (2 * width, base, grad_src),
        (base, base + channels, grad_embed),
        (base + channels, base + channels + 2, biases),
    )
    for c in range(2 * pieces):
        half = c // pieces
        slot = (half ^ core) * pieces + ((c % pieces) ^ masks[half])
        begin, end = c * piece, (c + 1) * piece
        if begin >= base + channels + 2:
            continue
        values = total[pl.ds(pl.multiple_of(slot * piece, 16), piece), :].astype(F32)
        for low, high, target in bounds:
            lo, hi = max(low, begin), min(high, end)
            if lo < hi:
                target[lo - low : hi - low, :] = values[lo - begin : hi - begin, :]


def shards(
    grid_feat,
    mesh_latent,
    cotangent,
    row_pack,
    edge_src,
    edge_dst,
    edge_count,
    w_embed,
    b_embed,
    w_src,
    w_dst,
    b_hidden,
    w_out,
):
    device_count = lax.axis_size("dom")
    own, channels = grid_feat.shape
    width = w_src.shape[0]
    peer_slots = row_pack.shape[0] // device_count
    more = device_count * peer_slots
    slots = own + more
    blocks, edges = edge_src.shape
    nodes = mesh_latent.shape[0]
    block = nodes // blocks
    padded = round_up(channels + 2, 128)
    depth = block + round_up(slots + 16, 128)
    first, second, last_bit = stage_bits(device_count)
    pieces = 1 << len(first)
    grad_rows = round_up(3 * width + padded, 32 * pieces)
    half = grad_rows // 2

    vmem = pl.BlockSpec(memory_space=pltpu.VMEM)
    smem = pl.BlockSpec(memory_space=pltpu.SMEM)
    params = pltpu.CompilerParams(vmem_limit_bytes=VMEM_BYTES)
    shape = jax.ShapeDtypeStruct
    feat, send = pl.pallas_call(
        pick_kernel,
        out_shape=(shape((own, padded), BF16), shape((device_count, peer_slots, padded), BF16)),
        in_specs=[vmem] * 2,
        out_specs=(vmem,) * 2,
        compiler_params=params,
        name="pick_rows",
    )(row_pack[None, :], grid_feat)
    feat_in = lax.all_to_all(send, "dom", split_axis=0, concat_axis=0, tiled=True)

    own_macs = own * width * (padded + width) + 2 * nodes * width * width
    latent, proj, near, back, w_pad = pl.pallas_call(
        own_kernel,
        out_shape=(
            shape((own, width), BF16),
            shape((own, width), BF16),
            shape((nodes, width), BF16),
            shape((2, nodes, width), BF16),
            shape((padded, width), BF16),
        ),
        in_specs=[vmem] * 8,
        out_specs=(vmem,) * 5,
        scratch_shapes=[pltpu.VMEM((padded, width), F32)],
        compiler_params=params,
        cost_estimate=pl.CostEstimate(
            flops=2 * own_macs, bytes_accessed=8 * own * width, transcendentals=own * width
        ),
        name="own_rows",
    )(feat, w_embed, b_embed[None, :], w_src, mesh_latent, w_dst, cotangent, w_out)

    edge_macs = blocks * edges * width * (2 * depth + 3 * block)
    mesh_out, kept, sent = pl.pallas_call(
        functools.partial(edge_kernel, channels, device_count),
        out_shape=(
            shape((nodes, width), BF16),
            shape((half, width), F32),
            shape((half, width), BF16),
        ),
        in_specs=[smem] + [vmem] * 14,
        out_specs=(vmem,) * 3,
        scratch_shapes=[
            pltpu.VMEM((depth, width), BF16),
            pltpu.VMEM((2 * block, width), BF16),
            pltpu.VMEM((slots, width), BF16),
            pltpu.VMEM((slots, padded), BF16),
            pltpu.VMEM((more, padded), F32),
            pltpu.VMEM((edges, depth + block), BF16),
            pltpu.VMEM((depth, edges), BF16),
            pltpu.VMEM((edges, width), BF16),
            pltpu.VMEM((edges, width), BF16),
            pltpu.VMEM((slots, width), F32),
            pltpu.VMEM((nodes, width), BF16),
            pltpu.VMEM((nodes, width), BF16),
            pltpu.VMEM((16, width), F32),
            pltpu.VMEM((grad_rows, width), F32),
        ],
        compiler_params=params,
        cost_estimate=pl.CostEstimate(
            flops=2 * edge_macs, bytes_accessed=8 * own * width, transcendentals=blocks * edges * width
        ),
        name="edge_rows",
    )(
        edge_count,
        edge_src,
        edge_dst,
        feat_in,
        feat,
        w_pad,
        w_src,
        w_out,
        b_hidden[None, :],
        latent,
        proj,
        near,
        back,
        mesh_latent,
        cotangent,
    )

    def swap(values, bits):
        return lax.ppermute(
            values, "dom", [(d, d ^ (1 << bits[d % 2])) for d in range(device_count)]
        )

    held = kept + swap(sent, (0, 0)).astype(F32)
    for bits in zip(first, second):
        cut = held.shape[0] // 2
        got = swap(held[cut:].astype(BF16), bits)
        held = held[:cut] + got.astype(F32)
    held = held.astype(BF16)
    got = swap(held, (last_bit, last_bit))
    held = (held.astype(F32) + got.astype(F32)).astype(BF16)
    for bits in zip(reversed(first), reversed(second)):
        held = jnp.concatenate([held, swap(held, bits)], axis=0)
    held = jnp.concatenate([held, swap(held, (0, 0))], axis=0)

    grad_embed, grad_src, grad_dst, grad_out, biases = pl.pallas_call(
        functools.partial(unpack_kernel, channels, device_count),
        out_shape=(
            shape((channels, width), F32),
            shape((width, width), F32),
            shape((width, width), F32),
            shape((width, width), F32),
            shape((2, width), F32),
        ),
        in_specs=[vmem],
        out_specs=(vmem,) * 5,
        compiler_params=params,
        name="unpack_grads",
    )(held)
    return mesh_out, grad_embed, grad_src, grad_dst, grad_out, biases


def solution(mesh):
    return jax.shard_map(
        shards,
        mesh=mesh,
        in_specs=(
            P(("ens", "dom"), None),
            P(("ens", "dom"), None),
            P(("ens", "dom"), None),
            P("dom"),
            P("dom", None),
            P("dom", None),
            P("dom"),
            P(),
            P(),
            P(),
            P(),
            P(),
            P(),
        ),
        out_specs=(
            P(("ens", "dom"), None),
            P("ens", None),
            P("ens", None),
            P("ens", None),
            P("ens", None),
            P("ens", None),
        ),
        check_vma=False,
    )
```

```python
import functools

import jax
import jax.numpy as jnp
from jax import lax
from jax.experimental import pallas as pl
from jax.experimental.pallas import tpu as pltpu
from jax.sharding import PartitionSpec as P

BF16 = jnp.bfloat16
F32 = jnp.float32


def mm(left, right, left_dim=1, right_dim=0):
    return lax.dot_general(
        left, right, (((left_dim,), (right_dim,)), ((), ())), preferred_element_type=F32
    )


def sigmoid(values):
    return 0.5 * jnp.tanh(0.5 * values) + 0.5


def round_up(value, step):
    return -(-value // step) * step


def pick_kernel(row_pack, feat_t, send):
    channels, own = feat_t.shape
    peers, peer_slots, padded = send.shape
    row = lax.broadcasted_iota(jnp.int32, (own, peers * peer_slots), 0)
    pick = jnp.where(row == row_pack[...], 1.0, 0.0).astype(BF16)
    rows = mm(pick, feat_t[...], 0, 1)
    last = padded - 128
    lane = lax.broadcasted_iota(jnp.int32, (peers * peer_slots, 128), 1) + last
    ones = jnp.where(lane == channels, 1.0, 0.0).astype(BF16)
    for j in range(peers):
        part = slice(j * peer_slots, (j + 1) * peer_slots)
        send[j, :, last:padded] = ones[part, :]
        send[j, :, 0:channels] = rows[part, :].astype(BF16)


def stage_bits(device_count):
    bits = device_count.bit_length() - 1
    first = list(range(1, bits - 1))
    second = first[1::-1] + first[2:]
    return first, second, bits - 1


def position_mask(me, order):
    mask = 0
    for i, bit in enumerate(order):
        mask = mask + (lax.rem(me // (1 << bit), 2) << (len(order) - 1 - i))
    return mask


def place(device_count):
    me = lax.axis_index("dom")
    first, second, _ = stage_bits(device_count)
    masks = position_mask(me, first), position_mask(me, second)
    return lax.rem(me, 2), masks, 1 << len(first)


def split_pieces(device_count, grads, kept, sent):
    core, masks, pieces = place(device_count)
    mine = jnp.where(core == 0, masks[0], masks[1])
    theirs = jnp.where(core == 0, masks[1], masks[0])
    piece = kept.shape[0] // pieces
    for p in range(pieces):
        at = pl.ds(pl.multiple_of((core * pieces + (mine ^ p)) * piece, 16), piece)
        kept[p * piece : (p + 1) * piece, :] = grads[at, :]
        at = pl.ds(pl.multiple_of(((1 - core) * pieces + (theirs ^ p)) * piece, 16), piece)
        sent[p * piece : (p + 1) * piece, :] = grads[at, :].astype(BF16)


def forward_kernel(
    device_count,
    count,
    src,
    dst,
    feat_in,
    feat_t,
    w_embed,
    biases,
    w_src,
    w_dst,
    w_out,
    mesh,
    cot,
    mesh_out,
    pgrad,
    latent,
    feat,
    w_pad,
    bias_sum,
    kept,
    sent,
    table,
    pair,
    wide,
    wide_t,
    incoming,
    one_hot,
    one_hot_t,
    hid,
    near,
    back,
    node_sum,
    hid_sum,
    grads,
):
    channels, own = feat_t.shape
    peers, peer_slots, padded = feat_in.shape
    more = peers * peer_slots
    slots = own + more
    blocks, edges = src.shape
    width = w_src.shape[0]
    nodes = mesh.shape[0]
    block = nodes // blocks
    depth = table.shape[0]
    step = 256

    last = padded - 32
    wide[last:padded, :] = jnp.zeros((32, width), F32)
    wide[0:channels, :] = w_embed[...].astype(F32)
    wide[channels : channels + 1, :] = biases[0:1, :].astype(F32)
    w_pad[...] = wide[...].astype(BF16)
    wide_t[last:padded, :] = jnp.zeros((32, own), F32)
    wide_t[0:channels, :] = feat_t[...].astype(F32)
    wide_t[channels : channels + 1, :] = jnp.ones((1, own), F32)
    feat[0:own, :] = jnp.transpose(wide_t[...]).astype(BF16)
    for j in range(peers):
        incoming[j * peer_slots : (j + 1) * peer_slots, :] = feat_in[j].astype(F32)
    feat[own:slots, :] = incoming[...].astype(BF16)
    for r in range(0, slots, step):
        end = min(r + step, slots)
        pre = mm(feat[r:end, :], w_pad[...])
        lat = (pre * sigmoid(pre)).astype(BF16)
        latent[r:end, :] = lat
        table[block + r : block + end, :] = mm(lat, w_src[...]).astype(BF16)
    near[...] = mm(mesh[...], w_dst[...]).astype(BF16)
    full = mm(cot[...], w_out[...], 1, 1)
    high = full.astype(BF16)
    back[0] = high
    back[1] = (full - high.astype(F32)).astype(BF16)
    tail = depth - slots - block
    tail_row = lax.broadcasted_iota(jnp.int32, (tail, width), 0)
    table[slots + block : depth, :] = jnp.where(
        tail_row == 0, jnp.broadcast_to(biases[1:2, :].astype(F32), (tail, width)), 0.0
    ).astype(BF16)

    edge_lane = lax.broadcasted_iota(jnp.int32, (blocks, edges), 1)
    block_row = lax.broadcasted_iota(jnp.int32, (blocks, 1), 0)
    counts = jnp.zeros((blocks, 1), jnp.int32)
    for b in range(blocks):
        counts = jnp.where(block_row == b, count[b], counts)
    src_all = src[...]
    dst_all = jnp.where(edge_lane < counts, dst[...], -1)
    columns = jnp.transpose(jnp.concatenate([src_all, dst_all], axis=0))
    bias_total = jnp.zeros((1, width), F32)

    for b in range(blocks):
        rows = slice(b * block, (b + 1) * block)
        table[0:block, :] = near[rows, :]
        pair[0:block, :] = back[0, rows, :]
        pair[block : 2 * block, :] = back[1, rows, :]
        dst_row = dst_all[b : b + 1, :]
        for e in range(0, edges, step):
            src_col = columns[e : e + step, b : b + 1]
            dst_col = columns[e : e + step, blocks + b : blocks + b + 1]
            lane = lax.broadcasted_iota(jnp.int32, (step, block), 1)
            near_hot = jnp.where(lane == dst_col, 1.0, 0.0).astype(BF16)
            one_hot[e : e + step, 0:block] = near_hot
            one_hot[e : e + step, block : 2 * block] = near_hot
            for k in range(0, depth - block, 128):
                lane = lax.broadcasted_iota(jnp.int32, (step, 128), 1) + k
                hot = lane == src_col
                if k <= slots < k + 128:
                    hot = hot | (lane == slots)
                hot = jnp.where(hot, 1.0, 0.0).astype(BF16)
                one_hot[e : e + step, 2 * block + k : 2 * block + k + 128] = hot
            pre = mm(one_hot[e : e + step, block : block + depth], table[...])
            grad = mm(one_hot[e : e + step, 0 : 2 * block], pair[...])
            sig = sigmoid(pre)
            act = pre * sig
            hid[e : e + step, :] = act.astype(BF16)
            at = slice(b * edges + e, b * edges + e + step)
            pgrad[at, :] = (grad * (sig + act * (1.0 - sig))).astype(BF16)
        sub = lax.broadcasted_iota(jnp.int32, (block, edges), 0)
        one_hot_t[...] = jnp.where(sub == dst_row, 1.0, 0.0).astype(BF16)
        node = mm(one_hot_t[...], pgrad[b * edges : (b + 1) * edges, :])
        bias_total = bias_total + jnp.sum(node, axis=0, keepdims=True)
        node_sum[rows, :] = node.astype(BF16)
        hid_sum[rows, :] = mm(one_hot_t[...], hid[...]).astype(BF16)

    bias_sum[...] = jnp.broadcast_to(bias_total, bias_sum.shape)
    total = hid_sum[...]
    mesh_out[...] = (mesh[...].astype(F32) + mm(total, w_out[...])).astype(BF16)
    grads[0:width, :] = mm(total, cot[...], 0, 0)
    grads[width : 2 * width, :] = mm(mesh[...], node_sum[...], 0, 0)
    split_pieces(device_count, grads, kept, sent)


def scatter_rows(src, pgrad, one_hot_t, first_block, block_count):
    edges = src.shape[1]
    slots = one_hot_t.shape[0]
    parts = []
    for b in range(first_block, first_block + block_count):
        at = slice((b - first_block) * edges, (b - first_block + 1) * edges)
        for r in range(0, slots, 128):
            size = min(128, slots - r)
            sub = lax.broadcasted_iota(jnp.int32, (size, edges), 0) + r
            hot = jnp.where(sub == src[b : b + 1, :], 1.0, 0.0).astype(BF16)
            one_hot_t[r : r + size, at] = hot
    rows = slice(first_block * edges, (first_block + block_count) * edges)
    return mm(one_hot_t[...], pgrad[rows, :])


def scatter_kernel(src, pgrad, slot_sum, one_hot_t):
    slot_sum[...] = scatter_rows(src, pgrad, one_hot_t, 0, src.shape[0] // 2)


def backward_kernel(
    channels,
    device_count,
    src,
    pgrad,
    slot_half,
    latent,
    feat,
    w_pad,
    w_src,
    bias_sum,
    kept,
    sent,
    one_hot_t,
    grads,
):
    width = w_src.shape[0]
    padded = feat.shape[1]
    half = src.shape[0] // 2
    rest = src.shape[0] - half
    slot_sum = slot_half[...] + scatter_rows(src, pgrad, one_hot_t, half, rest)
    slot_grad = slot_sum.astype(BF16)
    grads[0:width, :] = mm(latent[...], slot_grad, 0, 0)
    buffer_grad = mm(slot_grad, w_src[...], 1, 1)
    pre = mm(feat[...], w_pad[...])
    sig = sigmoid(pre)
    embed = (buffer_grad * (sig * (1.0 + pre * (1.0 - sig)))).astype(BF16)
    grads[width : width + padded, :] = mm(feat[...], embed, 0, 0)
    grads[width + channels + 1 : width + channels + 2, :] = bias_sum[0:1, :]
    if grads.shape[0] > width + padded:
        spare = grads.shape[0] - width - padded
        grads[width + padded :, :] = jnp.zeros((spare, width), F32)
    split_pieces(device_count, grads, kept, sent)


def unpack_kernel(device_count, bounds, held, got, *targets):
    core, masks, pieces = place(device_count)
    piece = held.shape[0] // pieces
    used = bounds[-1][1]
    for c in range(2 * pieces):
        half = c // pieces
        begin, end = c * piece, (c + 1) * piece
        if begin >= used:
            continue
        slot = (c % pieces) ^ masks[half]
        at = pl.ds(pl.multiple_of(slot * piece, 16), piece)
        values = jnp.where(core == half, held[at, :].astype(F32), got[at, :].astype(F32))
        for (low, high), target in zip(bounds, targets):
            lo, hi = max(low, begin), min(high, end)
            if lo < hi:
                target[lo - low : hi - low, :] = values[lo - begin : hi - begin, :]


def shards(
    grid_feat,
    mesh_latent,
    cotangent,
    row_pack,
    edge_src,
    edge_dst,
    edge_count,
    w_embed,
    b_embed,
    w_src,
    w_dst,
    b_hidden,
    w_out,
):
    device_count = lax.axis_size("dom")
    own, channels = grid_feat.shape
    width = w_src.shape[0]
    peer_slots = row_pack.shape[0] // device_count
    more = device_count * peer_slots
    slots = own + more
    blocks, edges = edge_src.shape
    nodes = mesh_latent.shape[0]
    block = nodes // blocks
    padded = round_up(channels + 2, 128)
    depth = block + round_up(slots + 16, 128)
    first, second, last_bit = stage_bits(device_count)
    pieces = 1 << len(first)
    mesh_rows = round_up(2 * width, 32 * pieces)
    grid_rows = round_up(width + padded, 32 * pieces)
    half_blocks = blocks // 2

    vmem = pl.BlockSpec(memory_space=pltpu.VMEM)
    smem = pl.BlockSpec(memory_space=pltpu.SMEM)
    shape = jax.ShapeDtypeStruct

    def limit(mib):
        return pltpu.CompilerParams(vmem_limit_bytes=mib * 1024 * 1024)

    feat_t = grid_feat.T
    send = pl.pallas_call(
        pick_kernel,
        out_shape=shape((device_count, peer_slots, padded), BF16),
        in_specs=[vmem] * 2,
        out_specs=vmem,
        compiler_params=limit(16),
        name="pick_rows",
    )(row_pack[None, :], feat_t)
    feat_in = lax.all_to_all(send, "dom", split_axis=0, concat_axis=0, tiled=True)
    bias_rows = jnp.stack([b_embed, b_hidden])

    forward_macs = (
        slots * width * (padded + width)
        + blocks * edges * width * (depth + 4 * block)
        + 5 * nodes * width * width
    )
    mesh_out, pgrad, latent, feat, w_pad, bias_sum, kept_mesh, sent_mesh = pl.pallas_call(
        functools.partial(forward_kernel, device_count),
        out_shape=(
            shape((nodes, width), BF16),
            shape((blocks * edges, width), BF16),
            shape((slots, width), BF16),
            shape((slots, padded), BF16),
            shape((padded, width), BF16),
            shape((8, width), F32),
            shape((mesh_rows // 2, width), F32),
            shape((mesh_rows // 2, width), BF16),
        ),
        in_specs=[smem] + [vmem] * 11,
        out_specs=(vmem,) * 8,
        scratch_shapes=[
            pltpu.VMEM((depth, width), BF16),
            pltpu.VMEM((2 * block, width), BF16),
            pltpu.VMEM((padded, width), F32),
            pltpu.VMEM((padded, own), F32),
            pltpu.VMEM((more, padded), F32),
            pltpu.VMEM((edges, depth + block), BF16),
            pltpu.VMEM((block, edges), BF16),
            pltpu.VMEM((edges, width), BF16),
            pltpu.VMEM((nodes, width), BF16),
            pltpu.VMEM((2, nodes, width), BF16),
            pltpu.VMEM((nodes, width), BF16),
            pltpu.VMEM((nodes, width), BF16),
            pltpu.VMEM((mesh_rows, width), F32),
        ],
        compiler_params=limit(40),
        cost_estimate=pl.CostEstimate(
            flops=2 * forward_macs,
            bytes_accessed=16 * own * width,
            transcendentals=blocks * edges * width,
        ),
        name="forward_rows",
    )(
        edge_count,
        edge_src,
        edge_dst,
        feat_in,
        feat_t,
        w_embed,
        bias_rows,
        w_src,
        w_dst,
        w_out,
        mesh_latent,
        cotangent,
    )

    def swap(values, bits):
        return lax.ppermute(
            values, "dom", [(d, d ^ (1 << bits[d % 2])) for d in range(device_count)]
        )

    def cut(held):
        middle = held.shape[0] // 2
        return held[:middle], held[middle:].astype(BF16)

    def pair_sum(kept, sent):
        return cut(kept + swap(sent, (0, 0)).astype(F32))

    def reduce_pieces(held, sent):
        stages = list(zip(first, second))
        for bits in stages[:-1]:
            held, sent = cut(held + swap(sent, bits).astype(F32))
        held = (held + swap(sent, stages[-1]).astype(F32)).astype(BF16)
        got = swap(held, (last_bit, last_bit))
        held = (held.astype(F32) + got.astype(F32)).astype(BF16)
        for bits in reversed(stages):
            held = jnp.concatenate([held, swap(held, bits)], axis=0)
        return held, swap(held, (0, 0))

    held_mesh, next_mesh = pair_sum(kept_mesh, sent_mesh)
    slot_half = pl.pallas_call(
        scatter_kernel,
        out_shape=shape((slots, width), F32),
        in_specs=[vmem] * 2,
        out_specs=vmem,
        scratch_shapes=[pltpu.VMEM((slots, half_blocks * edges), BF16)],
        compiler_params=limit(24),
        cost_estimate=pl.CostEstimate(
            flops=2 * half_blocks * edges * slots * width,
            bytes_accessed=half_blocks * edges * width * 2,
            transcendentals=0,
        ),
        name="scatter_rows",
    )(edge_src, pgrad)

    slot_half, held_mesh, next_mesh = lax.optimization_barrier((slot_half, held_mesh, next_mesh))
    kept_grid, sent_grid = pl.pallas_call(
        functools.partial(backward_kernel, channels, device_count),
        out_shape=(
            shape((grid_rows // 2, width), F32),
            shape((grid_rows // 2, width), BF16),
        ),
        in_specs=[vmem] * 8,
        out_specs=(vmem,) * 2,
        scratch_shapes=[
            pltpu.VMEM((slots, (blocks - half_blocks) * edges), BF16),
            pltpu.VMEM((grid_rows, width), F32),
        ],
        compiler_params=limit(40),
        cost_estimate=pl.CostEstimate(
            flops=2 * slots * width * (half_blocks * edges + 2 * width + 2 * padded),
            bytes_accessed=half_blocks * edges * width * 2,
            transcendentals=slots * width,
        ),
        name="backward_rows",
    )(edge_src, pgrad, slot_half, latent, feat, w_pad, w_src, bias_sum)

    def unpack(pair, bounds):
        return pl.pallas_call(
            functools.partial(unpack_kernel, device_count, bounds),
            out_shape=tuple(shape((high - low, width), F32) for low, high in bounds),
            in_specs=[vmem] * 2,
            out_specs=(vmem,) * len(bounds),
            compiler_params=limit(16),
            name="unpack_rows",
        )(*pair)

    mesh_pair = reduce_pieces(held_mesh, next_mesh)
    grid_pair = reduce_pieces(*pair_sum(kept_grid, sent_grid))
    grad_out, grad_dst = unpack(mesh_pair, ((0, width), (width, 2 * width)))
    end = width + channels
    grad_src, grad_embed, biases = unpack(grid_pair, ((0, width), (width, end), (end, end + 2)))
    return mesh_out, grad_embed, grad_src, grad_dst, grad_out, biases


def solution(mesh):
    return jax.shard_map(
        shards,
        mesh=mesh,
        in_specs=(
            P(("ens", "dom"), None),
            P(("ens", "dom"), None),
            P(("ens", "dom"), None),
            P("dom"),
            P("dom", None),
            P("dom", None),
            P("dom"),
            P(),
            P(),
            P(),
            P(),
            P(),
            P(),
        ),
        out_specs=(
            P(("ens", "dom"), None),
            P("ens", None),
            P("ens", None),
            P("ens", None),
            P("ens", None),
            P("ens", None),
        ),
        check_vma=False,
    )
```

```python
import functools

import jax
import jax.numpy as jnp
from jax import lax
from jax.experimental import pallas as pl
from jax.experimental.pallas import tpu as pltpu
from jax.sharding import PartitionSpec as P

BF16 = jnp.bfloat16
F32 = jnp.float32


def mm(left, right, left_dim=1, right_dim=0):
    return lax.dot_general(
        left, right, (((left_dim,), (right_dim,)), ((), ())), preferred_element_type=F32
    )


def sigmoid(values):
    return 0.5 * jnp.tanh(0.5 * values) + 0.5


def round_up(value, step):
    return -(-value // step) * step


def fetch(source, target, sems, index):
    copy = pltpu.make_async_copy(source, target, sems.at[index])
    copy.start()
    return copy


def pick_kernel(row_pack, feat_hbm, send, feat_t, sems):
    rows_copy = fetch(feat_hbm, feat_t, sems, 0)
    channels, own = feat_t.shape
    peers, peer_slots, padded = send.shape
    row = lax.broadcasted_iota(jnp.int32, (own, peers * peer_slots), 0)
    pick = jnp.where(row == row_pack[...], 1.0, 0.0).astype(BF16)
    last = padded - 128
    lane = lax.broadcasted_iota(jnp.int32, (peers * peer_slots, 128), 1) + last
    ones = jnp.where(lane == channels, 1.0, 0.0).astype(BF16)
    rows_copy.wait()
    rows = mm(pick, feat_t[...], 0, 1)
    for j in range(peers):
        part = slice(j * peer_slots, (j + 1) * peer_slots)
        send[j, :, last:padded] = ones[part, :]
        send[j, :, 0:channels] = rows[part, :].astype(BF16)


def stage_bits(device_count):
    bits = device_count.bit_length() - 1
    first = list(range(1, bits - 1))
    second = first[1::-1] + first[2:]
    return first, second, bits - 1


def position_mask(me, order):
    mask = 0
    for i, bit in enumerate(order):
        mask = mask + (lax.rem(me // (1 << bit), 2) << (len(order) - 1 - i))
    return mask


def place(device_count):
    me = lax.axis_index("dom")
    first, second, _ = stage_bits(device_count)
    masks = position_mask(me, first), position_mask(me, second)
    return lax.rem(me, 2), masks, 1 << len(first)


def split_pieces(device_count, grads, kept, sent):
    core, masks, pieces = place(device_count)
    mine = jnp.where(core == 0, masks[0], masks[1])
    theirs = jnp.where(core == 0, masks[1], masks[0])
    piece = kept.shape[0] // pieces
    for p in range(pieces):
        at = pl.ds(pl.multiple_of((core * pieces + (mine ^ p)) * piece, 16), piece)
        kept[p * piece : (p + 1) * piece, :] = grads[at, :]
        at = pl.ds(pl.multiple_of(((1 - core) * pieces + (theirs ^ p)) * piece, 16), piece)
        sent[p * piece : (p + 1) * piece, :] = grads[at, :].astype(BF16)


def own_kernel(
    feat_hbm,
    w_embed_hbm,
    w_src_hbm,
    w_dst_hbm,
    w_out_hbm,
    mesh_hbm,
    cot_hbm,
    b_embed,
    latent,
    feat,
    w_pad,
    proj,
    near,
    back,
    feat_t,
    w_embed,
    w_src,
    w_dst,
    w_out,
    mesh,
    cot,
    wide,
    wide_t,
    sems,
):
    feat_copy = fetch(feat_hbm, feat_t, sems, 0)
    embed_copy = fetch(w_embed_hbm, w_embed, sems, 1)
    src_copy = fetch(w_src_hbm, w_src, sems, 2)
    mesh_copy = fetch(mesh_hbm, mesh, sems, 3)
    dst_copy = fetch(w_dst_hbm, w_dst, sems, 4)
    cot_copy = fetch(cot_hbm, cot, sems, 5)
    out_copy = fetch(w_out_hbm, w_out, sems, 6)
    channels, own = feat_t.shape
    padded, width = w_pad.shape
    last = padded - 32
    step = 256
    wide[last:padded, :] = jnp.zeros((32, width), F32)
    wide_t[last:padded, :] = jnp.zeros((32, own), F32)
    embed_copy.wait()
    wide[0:channels, :] = w_embed[...].astype(F32)
    wide[channels : channels + 1, :] = b_embed[...].astype(F32).reshape(1, width)
    w_pad[...] = wide[...].astype(BF16)
    feat_copy.wait()
    wide_t[0:channels, :] = feat_t[...].astype(F32)
    wide_t[channels : channels + 1, :] = jnp.ones((1, own), F32)
    feat[...] = jnp.transpose(wide_t[...]).astype(BF16)
    src_copy.wait()
    for r in range(0, own, step):
        pre = mm(feat[r : r + step, :], w_pad[...])
        lat = (pre * sigmoid(pre)).astype(BF16)
        latent[r : r + step, :] = lat
        proj[r : r + step, :] = mm(lat, w_src[...]).astype(BF16)
    mesh_copy.wait()
    dst_copy.wait()
    near[...] = mm(mesh[...], w_dst[...]).astype(BF16)
    cot_copy.wait()
    out_copy.wait()
    full = mm(cot[...], w_out[...], 1, 1)
    high = full.astype(BF16)
    back[0] = high
    back[1] = (full - high.astype(F32)).astype(BF16)


def forward_kernel(
    device_count,
    count,
    src,
    dst,
    feat_in,
    b_hidden,
    latent_own,
    feat_own,
    w_pad,
    proj,
    near,
    back,
    w_src_hbm,
    w_out_hbm,
    mesh_hbm,
    cot_hbm,
    mesh_out,
    pgrad,
    latent_in,
    feat_rows,
    bias_sum,
    kept,
    sent,
    table,
    pair,
    incoming,
    one_hot,
    one_hot_t,
    hid,
    node_sum,
    hid_sum,
    grads,
    w_src,
    w_out,
    mesh,
    cot,
    sems,
):
    src_copy = fetch(w_src_hbm, w_src, sems, 0)
    mesh_copy = fetch(mesh_hbm, mesh, sems, 1)
    out_copy = fetch(w_out_hbm, w_out, sems, 2)
    cot_copy = fetch(cot_hbm, cot, sems, 3)
    own = latent_own.shape[0]
    peers, peer_slots, padded = feat_in.shape
    more = peers * peer_slots
    slots = own + more
    blocks, edges = src.shape
    width = w_src.shape[0]
    nodes = mesh.shape[0]
    block = nodes // blocks
    depth = table.shape[0]
    step = 256

    for j in range(peers):
        incoming[j * peer_slots : (j + 1) * peer_slots, :] = feat_in[j].astype(F32)
    feat_rows[...] = incoming[...].astype(BF16)
    pre_in = mm(feat_rows[...], w_pad[...])
    lat_in = (pre_in * sigmoid(pre_in)).astype(BF16)
    latent_in[...] = lat_in
    table[block : block + own, :] = proj[...]
    tail = depth - slots - block
    tail_row = lax.broadcasted_iota(jnp.int32, (tail, width), 0)
    bias_row = b_hidden[...].astype(F32).reshape(1, width)
    table[slots + block : depth, :] = jnp.where(
        tail_row == 0, jnp.broadcast_to(bias_row, (tail, width)), 0.0
    ).astype(BF16)
    src_copy.wait()
    table[block + own : block + slots, :] = mm(lat_in, w_src[...]).astype(BF16)

    edge_lane = lax.broadcasted_iota(jnp.int32, (blocks, edges), 1)
    block_row = lax.broadcasted_iota(jnp.int32, (blocks, 1), 0)
    counts = jnp.zeros((blocks, 1), jnp.int32)
    for b in range(blocks):
        counts = jnp.where(block_row == b, count[b], counts)
    src_all = src[...]
    dst_all = jnp.where(edge_lane < counts, dst[...], -1)
    columns = jnp.transpose(jnp.concatenate([src_all, dst_all], axis=0))
    bias_total = jnp.zeros((1, width), F32)

    for b in range(blocks):
        rows = slice(b * block, (b + 1) * block)
        table[0:block, :] = near[rows, :]
        pair[0:block, :] = back[0, rows, :]
        pair[block : 2 * block, :] = back[1, rows, :]
        dst_row = dst_all[b : b + 1, :]
        for e in range(0, edges, step):
            src_col = columns[e : e + step, b : b + 1]
            dst_col = columns[e : e + step, blocks + b : blocks + b + 1]
            lane = lax.broadcasted_iota(jnp.int32, (step, block), 1)
            near_hot = jnp.where(lane == dst_col, 1.0, 0.0).astype(BF16)
            one_hot[e : e + step, 0:block] = near_hot
            one_hot[e : e + step, block : 2 * block] = near_hot
            for k in range(0, depth - block, 128):
                lane = lax.broadcasted_iota(jnp.int32, (step, 128), 1) + k
                hot = lane == src_col
                if k <= slots < k + 128:
                    hot = hot | (lane == slots)
                hot = jnp.where(hot, 1.0, 0.0).astype(BF16)
                one_hot[e : e + step, 2 * block + k : 2 * block + k + 128] = hot
            pre = mm(one_hot[e : e + step, block : block + depth], table[...])
            grad = mm(one_hot[e : e + step, 0 : 2 * block], pair[...])
            sig = sigmoid(pre)
            act = pre * sig
            hid[e : e + step, :] = act.astype(BF16)
            at = slice(b * edges + e, b * edges + e + step)
            pgrad[at, :] = (grad * (sig + act * (1.0 - sig))).astype(BF16)
        sub = lax.broadcasted_iota(jnp.int32, (block, edges), 0)
        one_hot_t[...] = jnp.where(sub == dst_row, 1.0, 0.0).astype(BF16)
        node = mm(one_hot_t[...], pgrad[b * edges : (b + 1) * edges, :])
        bias_total = bias_total + jnp.sum(node, axis=0, keepdims=True)
        node_sum[rows, :] = node.astype(BF16)
        hid_sum[rows, :] = mm(one_hot_t[...], hid[...]).astype(BF16)

    bias_sum[...] = jnp.broadcast_to(bias_total, bias_sum.shape)
    total = hid_sum[...]
    mesh_copy.wait()
    out_copy.wait()
    cot_copy.wait()
    mesh_out[...] = (mesh[...].astype(F32) + mm(total, w_out[...])).astype(BF16)
    grads[0:width, :] = mm(total, cot[...], 0, 0)
    grads[width : 2 * width, :] = mm(mesh[...], node_sum[...], 0, 0)
    split_pieces(device_count, grads, kept, sent)


def scatter_rows(src, pgrad, one_hot_t, first_block, block_count):
    edges = src.shape[1]
    slots = one_hot_t.shape[0]
    parts = []
    for b in range(first_block, first_block + block_count):
        at = slice((b - first_block) * edges, (b - first_block + 1) * edges)
        for r in range(0, slots, 128):
            size = min(128, slots - r)
            sub = lax.broadcasted_iota(jnp.int32, (size, edges), 0) + r
            hot = jnp.where(sub == src[b : b + 1, :], 1.0, 0.0).astype(BF16)
            one_hot_t[r : r + size, at] = hot
    rows = slice(first_block * edges, (first_block + block_count) * edges)
    return mm(one_hot_t[...], pgrad[rows, :])


def scatter_kernel(src, pgrad, slot_sum, one_hot_t):
    slot_sum[...] = scatter_rows(src, pgrad, one_hot_t, 0, src.shape[0] // 2)


def scatter_rest_kernel(src, pgrad, slot_half, slot_grad, one_hot_t):
    half = src.shape[0] // 2
    rest = scatter_rows(src, pgrad, one_hot_t, half, src.shape[0] - half)
    slot_grad[...] = (slot_half[...] + rest).astype(BF16)


def backward_kernel(
    channels,
    device_count,
    slot_grad,
    latent_own,
    latent_in,
    feat_own,
    feat_in,
    w_pad,
    bias_sum,
    w_src_hbm,
    kept,
    sent,
    latent,
    feat,
    grads,
    w_src,
    sems,
):
    src_copy = fetch(w_src_hbm, w_src, sems, 0)
    own = latent_own.shape[0]
    slots = latent.shape[0]
    width = w_src.shape[0]
    padded = feat.shape[1]
    latent[0:own, :] = latent_own[...]
    latent[own:slots, :] = latent_in[...]
    feat[0:own, :] = feat_own[...]
    feat[own:slots, :] = feat_in[...]
    pre = mm(feat[...], w_pad[...])
    sig = sigmoid(pre)
    grads[0:width, :] = mm(latent[...], slot_grad[...], 0, 0)
    src_copy.wait()
    buffer_grad = mm(slot_grad[...], w_src[...], 1, 1)
    embed = (buffer_grad * (sig * (1.0 + pre * (1.0 - sig)))).astype(BF16)
    grads[width : width + padded, :] = mm(feat[...], embed, 0, 0)
    grads[width + channels + 1 : width + channels + 2, :] = bias_sum[0:1, :]
    if grads.shape[0] > width + padded:
        spare = grads.shape[0] - width - padded
        grads[width + padded :, :] = jnp.zeros((spare, width), F32)
    split_pieces(device_count, grads, kept, sent)


def unpack_kernel(device_count, bounds, held, got, *targets):
    core, masks, pieces = place(device_count)
    piece = held.shape[0] // pieces
    used = bounds[-1][1]
    for c in range(2 * pieces):
        half = c // pieces
        begin, end = c * piece, (c + 1) * piece
        if begin >= used:
            continue
        slot = (c % pieces) ^ masks[half]
        at = pl.ds(pl.multiple_of(slot * piece, 16), piece)
        values = jnp.where(core == half, held[at, :].astype(F32), got[at, :].astype(F32))
        for (low, high), target in zip(bounds, targets):
            lo, hi = max(low, begin), min(high, end)
            if lo < hi:
                target[lo - low : hi - low, :] = values[lo - begin : hi - begin, :]


def shards(
    grid_feat,
    mesh_latent,
    cotangent,
    row_pack,
    edge_src,
    edge_dst,
    edge_count,
    w_embed,
    b_embed,
    w_src,
    w_dst,
    b_hidden,
    w_out,
):
    device_count = lax.axis_size("dom")
    own, channels = grid_feat.shape
    width = w_src.shape[0]
    peer_slots = row_pack.shape[0] // device_count
    more = device_count * peer_slots
    slots = own + more
    blocks, edges = edge_src.shape
    nodes = mesh_latent.shape[0]
    block = nodes // blocks
    padded = round_up(channels + 2, 128)
    depth = block + round_up(slots + 16, 128)
    first, second, last_bit = stage_bits(device_count)
    pieces = 1 << len(first)
    mesh_rows = round_up(2 * width, 32 * pieces)
    grid_rows = round_up(width + padded, 32 * pieces)
    half_blocks = blocks // 2
    stages = list(zip(first, second))

    vmem = pl.BlockSpec(memory_space=pltpu.VMEM)
    smem = pl.BlockSpec(memory_space=pltpu.SMEM)
    hbm = pl.BlockSpec(memory_space=pltpu.HBM)
    shape = jax.ShapeDtypeStruct

    def limit(mib):
        return pltpu.CompilerParams(vmem_limit_bytes=mib * 1024 * 1024)

    feat_t = grid_feat.T
    dma = pltpu.SemaphoreType.DMA
    send = pl.pallas_call(
        pick_kernel,
        out_shape=shape((device_count, peer_slots, padded), BF16),
        in_specs=[vmem, hbm],
        out_specs=vmem,
        scratch_shapes=[pltpu.VMEM((channels, own), BF16), dma((1,))],
        compiler_params=limit(16),
        cost_estimate=pl.CostEstimate(
            flops=20_000_000_000, bytes_accessed=own * padded * 2, transcendentals=0
        ),
        name="pick_rows",
    )(row_pack[None, :], feat_t)
    feat_in = lax.all_to_all(send, "dom", split_axis=0, concat_axis=0, tiled=True)

    own_macs = own * width * (padded + width) + 2 * nodes * width * width
    latent_own, feat_own, w_pad, proj, near, back = pl.pallas_call(
        own_kernel,
        out_shape=(
            shape((own, width), BF16),
            shape((own, padded), BF16),
            shape((padded, width), BF16),
            shape((own, width), BF16),
            shape((nodes, width), BF16),
            shape((2, nodes, width), BF16),
        ),
        in_specs=[hbm] * 7 + [vmem],
        out_specs=(vmem,) * 6,
        scratch_shapes=[
            pltpu.VMEM((channels, own), BF16),
            pltpu.VMEM((channels, width), BF16),
            pltpu.VMEM((width, width), BF16),
            pltpu.VMEM((width, width), BF16),
            pltpu.VMEM((width, width), BF16),
            pltpu.VMEM((nodes, width), BF16),
            pltpu.VMEM((nodes, width), BF16),
            pltpu.VMEM((padded, width), F32),
            pltpu.VMEM((padded, own), F32),
            dma((7,)),
        ],
        compiler_params=limit(24),
        cost_estimate=pl.CostEstimate(
            flops=4 * own_macs, bytes_accessed=8 * own * width, transcendentals=own * width
        ),
        name="own_rows",
    )(feat_t, w_embed, w_src, w_dst, w_out, mesh_latent, cotangent, b_embed)

    forward_macs = blocks * edges * width * (depth + 4 * block) + 3 * nodes * width * width
    mesh_out, pgrad, latent_in, feat_rows, bias_sum, kept_mesh, sent_mesh = pl.pallas_call(
        functools.partial(forward_kernel, device_count),
        out_shape=(
            shape((nodes, width), BF16),
            shape((blocks * edges, width), BF16),
            shape((more, width), BF16),
            shape((more, padded), BF16),
            shape((8, width), F32),
            shape((mesh_rows // 2, width), F32),
            shape((mesh_rows // 2, width), BF16),
        ),
        in_specs=[smem] + [vmem] * 10 + [hbm] * 4,
        out_specs=(vmem,) * 7,
        scratch_shapes=[
            pltpu.VMEM((depth, width), BF16),
            pltpu.VMEM((2 * block, width), BF16),
            pltpu.VMEM((more, padded), F32),
            pltpu.VMEM((edges, depth + block), BF16),
            pltpu.VMEM((block, edges), BF16),
            pltpu.VMEM((edges, width), BF16),
            pltpu.VMEM((nodes, width), BF16),
            pltpu.VMEM((nodes, width), BF16),
            pltpu.VMEM((mesh_rows, width), F32),
            pltpu.VMEM((width, width), BF16),
            pltpu.VMEM((width, width), BF16),
            pltpu.VMEM((nodes, width), BF16),
            pltpu.VMEM((nodes, width), BF16),
            dma((4,)),
        ],
        compiler_params=limit(36),
        cost_estimate=pl.CostEstimate(
            flops=2 * forward_macs,
            bytes_accessed=16 * own * width,
            transcendentals=blocks * edges * width,
        ),
        name="forward_rows",
    )(
        edge_count,
        edge_src,
        edge_dst,
        feat_in,
        b_hidden,
        latent_own,
        feat_own,
        w_pad,
        proj,
        near,
        back,
        w_src,
        w_out,
        mesh_latent,
        cotangent,
    )

    def swap(values, bits):
        return lax.ppermute(
            values, "dom", [(d, d ^ (1 << bits[d % 2])) for d in range(device_count)]
        )

    def cut(held):
        middle = held.shape[0] // 2
        return held[:middle], held[middle:].astype(BF16)

    def pair_sum(kept, sent):
        return cut(kept + swap(sent, (0, 0)).astype(F32))

    def reduce_pieces(held, got):
        for bits in stages[1:]:
            held, sent = cut(held + got.astype(F32))
            got = swap(sent, bits)
        held = (held + got.astype(F32)).astype(BF16)
        got = swap(held, (last_bit, last_bit))
        held = (held.astype(F32) + got.astype(F32)).astype(BF16)
        for bits in reversed(stages):
            held = jnp.concatenate([held, swap(held, bits)], axis=0)
        return held, swap(held, (0, 0))

    held_mesh, next_mesh = pair_sum(kept_mesh, sent_mesh)
    slot_half = pl.pallas_call(
        scatter_kernel,
        out_shape=shape((slots, width), F32),
        in_specs=[vmem] * 2,
        out_specs=vmem,
        scratch_shapes=[pltpu.VMEM((slots, half_blocks * edges), BF16)],
        compiler_params=limit(24),
        cost_estimate=pl.CostEstimate(
            flops=2 * half_blocks * edges * slots * width,
            bytes_accessed=half_blocks * edges * width * 2,
            transcendentals=0,
        ),
        name="scatter_rows",
    )(edge_src, pgrad)
    slot_half, held_mesh, next_mesh = lax.optimization_barrier((slot_half, held_mesh, next_mesh))
    got_mesh = swap(next_mesh, stages[0])
    slot_grad = pl.pallas_call(
        scatter_rest_kernel,
        out_shape=shape((slots, width), BF16),
        in_specs=[vmem] * 3,
        out_specs=vmem,
        scratch_shapes=[pltpu.VMEM((slots, (blocks - half_blocks) * edges), BF16)],
        compiler_params=limit(24),
        cost_estimate=pl.CostEstimate(
            flops=4 * half_blocks * edges * slots * width,
            bytes_accessed=half_blocks * edges * width * 2,
            transcendentals=0,
        ),
        name="scatter_rest",
    )(edge_src, pgrad, slot_half)
    slot_grad, got_mesh = lax.optimization_barrier((slot_grad, got_mesh))

    kept_grid, sent_grid = pl.pallas_call(
        functools.partial(backward_kernel, channels, device_count),
        out_shape=(
            shape((grid_rows // 2, width), F32),
            shape((grid_rows // 2, width), BF16),
        ),
        in_specs=[vmem] * 7 + [hbm],
        out_specs=(vmem,) * 2,
        scratch_shapes=[
            pltpu.VMEM((slots, width), BF16),
            pltpu.VMEM((slots, padded), BF16),
            pltpu.VMEM((grid_rows, width), F32),
            pltpu.VMEM((width, width), BF16),
            dma((1,)),
        ],
        compiler_params=limit(24),
        cost_estimate=pl.CostEstimate(
            flops=4 * slots * width * (2 * width + 2 * padded),
            bytes_accessed=slots * width * 2,
            transcendentals=slots * width,
        ),
        name="backward_rows",
    )(slot_grad, latent_own, latent_in, feat_own, feat_rows, w_pad, bias_sum, w_src)

    def unpack(pair, bounds):
        return pl.pallas_call(
            functools.partial(unpack_kernel, device_count, bounds),
            out_shape=tuple(shape((high - low, width), F32) for low, high in bounds),
            in_specs=[vmem] * 2,
            out_specs=(vmem,) * len(bounds),
            compiler_params=limit(16),
            name="unpack_rows",
        )(*pair)

    mesh_pair = reduce_pieces(held_mesh, got_mesh)
    held_grid, next_grid = pair_sum(kept_grid, sent_grid)
    grid_pair = reduce_pieces(held_grid, swap(next_grid, stages[0]))
    grad_out, grad_dst = unpack(mesh_pair, ((0, width), (width, 2 * width)))
    end = width + channels
    grad_src, grad_embed, biases = unpack(grid_pair, ((0, width), (width, end), (end, end + 2)))
    return mesh_out, grad_embed, grad_src, grad_dst, grad_out, biases


def solution(mesh):
    return jax.shard_map(
        shards,
        mesh=mesh,
        in_specs=(
            P(("ens", "dom"), None),
            P(("ens", "dom"), None),
            P(("ens", "dom"), None),
            P("dom"),
            P("dom", None),
            P("dom", None),
            P("dom"),
            P(),
            P(),
            P(),
            P(),
            P(),
            P(),
        ),
        out_specs=(
            P(("ens", "dom"), None),
            P("ens", None),
            P("ens", None),
            P("ens", None),
            P("ens", None),
            P("ens", None),
        ),
        check_vma=False,
    )
```

```python
import functools

import jax
import jax.numpy as jnp
from jax import lax
from jax.experimental import pallas as pl
from jax.experimental.pallas import tpu as pltpu
from jax.sharding import PartitionSpec as P

BF16 = jnp.bfloat16
F32 = jnp.float32


def mm(left, right, left_dim=1, right_dim=0):
    return lax.dot_general(
        left, right, (((left_dim,), (right_dim,)), ((), ())), preferred_element_type=F32
    )


def sigmoid(values):
    return 0.5 * jnp.tanh(0.5 * values) + 0.5


def round_up(value, step):
    return -(-value // step) * step


def fetch(source, target, sems, index):
    copy = pltpu.make_async_copy(source, target, sems.at[index])
    copy.start()
    return copy


def pick_kernel(row_pack, feat_hbm, send, feat_t, sems):
    rows_copy = fetch(feat_hbm, feat_t, sems, 0)
    channels, own = feat_t.shape
    peers, peer_slots, padded = send.shape
    row = lax.broadcasted_iota(jnp.int32, (own, peers * peer_slots), 0)
    pick = jnp.where(row == row_pack[...], 1.0, 0.0).astype(BF16)
    last = padded - 128
    lane = lax.broadcasted_iota(jnp.int32, (peers * peer_slots, 128), 1) + last
    ones = jnp.where(lane == channels, 1.0, 0.0).astype(BF16)
    rows_copy.wait()
    rows = mm(pick, feat_t[...], 0, 1)
    for j in range(peers):
        part = slice(j * peer_slots, (j + 1) * peer_slots)
        send[j, :, last:padded] = ones[part, :]
        send[j, :, 0:channels] = rows[part, :].astype(BF16)


def stage_bits(device_count):
    bits = device_count.bit_length() - 1
    first = list(range(1, bits - 1))
    second = first[1::-1] + first[2:]
    return first, second, bits - 1


def position_mask(me, order):
    mask = 0
    for i, bit in enumerate(order):
        mask = mask + (lax.rem(me // (1 << bit), 2) << (len(order) - 1 - i))
    return mask


def place(device_count):
    me = lax.axis_index("dom")
    first, second, _ = stage_bits(device_count)
    masks = position_mask(me, first), position_mask(me, second)
    return lax.rem(me, 2), masks, 1 << len(first)


def split_pieces(device_count, grads, kept, sent):
    core, masks, pieces = place(device_count)
    mine = jnp.where(core == 0, masks[0], masks[1])
    theirs = jnp.where(core == 0, masks[1], masks[0])
    piece = kept.shape[0] // pieces
    for p in range(pieces):
        at = pl.ds(pl.multiple_of((core * pieces + (mine ^ p)) * piece, 16), piece)
        kept[p * piece : (p + 1) * piece, :] = grads[at, :]
        at = pl.ds(pl.multiple_of(((1 - core) * pieces + (theirs ^ p)) * piece, 16), piece)
        sent[p * piece : (p + 1) * piece, :] = grads[at, :].astype(BF16)


def forward_kernel(
    device_count,
    count,
    src,
    dst,
    feat_in,
    feat_t,
    w_embed,
    b_embed,
    b_hidden,
    w_src,
    w_dst,
    w_out,
    mesh,
    cot,
    mesh_out,
    pgrad,
    latent,
    feat,
    w_pad,
    bias_sum,
    kept,
    sent,
    table,
    pair,
    wide,
    wide_t,
    incoming,
    one_hot,
    one_hot_t,
    hid,
    near,
    back,
    node_sum,
    hid_sum,
    grads,
):
    channels, own = feat_t.shape
    peers, peer_slots, padded = feat_in.shape
    more = peers * peer_slots
    slots = own + more
    blocks, edges = src.shape
    width = w_src.shape[0]
    nodes = mesh.shape[0]
    block = nodes // blocks
    depth = table.shape[0]
    step = 256

    last = padded - 32
    wide[last:padded, :] = jnp.zeros((32, width), F32)
    wide[0:channels, :] = w_embed[...].astype(F32)
    wide[channels : channels + 1, :] = b_embed[...].astype(F32).reshape(1, width)
    w_pad[...] = wide[...].astype(BF16)
    wide_t[last:padded, :] = jnp.zeros((32, own), F32)
    wide_t[0:channels, :] = feat_t[...].astype(F32)
    wide_t[channels : channels + 1, :] = jnp.ones((1, own), F32)
    feat[0:own, :] = jnp.transpose(wide_t[...]).astype(BF16)
    for j in range(peers):
        incoming[j * peer_slots : (j + 1) * peer_slots, :] = feat_in[j].astype(F32)
    feat[own:slots, :] = incoming[...].astype(BF16)
    for r in range(0, slots, step):
        end = min(r + step, slots)
        pre = mm(feat[r:end, :], w_pad[...])
        lat = (pre * sigmoid(pre)).astype(BF16)
        latent[r:end, :] = lat
        table[block + r : block + end, :] = mm(lat, w_src[...]).astype(BF16)
    near[...] = mm(mesh[...], w_dst[...]).astype(BF16)
    full = mm(cot[...], w_out[...], 1, 1)
    high = full.astype(BF16)
    back[0] = high
    back[1] = (full - high.astype(F32)).astype(BF16)
    tail = depth - slots - block
    tail_row = lax.broadcasted_iota(jnp.int32, (tail, width), 0)
    bias_row = b_hidden[...].astype(F32).reshape(1, width)
    table[slots + block : depth, :] = jnp.where(
        tail_row == 0, jnp.broadcast_to(bias_row, (tail, width)), 0.0
    ).astype(BF16)

    edge_lane = lax.broadcasted_iota(jnp.int32, (blocks, edges), 1)
    block_row = lax.broadcasted_iota(jnp.int32, (blocks, 1), 0)
    counts = jnp.zeros((blocks, 1), jnp.int32)
    for b in range(blocks):
        counts = jnp.where(block_row == b, count[b], counts)
    src_all = src[...]
    dst_all = jnp.where(edge_lane < counts, dst[...], -1)
    columns = jnp.transpose(jnp.concatenate([src_all, dst_all], axis=0))
    bias_total = jnp.zeros((1, width), F32)

    for b in range(blocks):
        rows = slice(b * block, (b + 1) * block)
        table[0:block, :] = near[rows, :]
        pair[0:block, :] = back[0, rows, :]
        pair[block : 2 * block, :] = back[1, rows, :]
        dst_row = dst_all[b : b + 1, :]
        for e in range(0, edges, step):
            src_col = columns[e : e + step, b : b + 1]
            dst_col = columns[e : e + step, blocks + b : blocks + b + 1]
            lane = lax.broadcasted_iota(jnp.int32, (step, block), 1)
            near_hot = jnp.where(lane == dst_col, 1.0, 0.0).astype(BF16)
            one_hot[e : e + step, 0:block] = near_hot
            one_hot[e : e + step, block : 2 * block] = near_hot
            for k in range(0, depth - block, 128):
                lane = lax.broadcasted_iota(jnp.int32, (step, 128), 1) + k
                hot = lane == src_col
                if k <= slots < k + 128:
                    hot = hot | (lane == slots)
                hot = jnp.where(hot, 1.0, 0.0).astype(BF16)
                one_hot[e : e + step, 2 * block + k : 2 * block + k + 128] = hot
            pre = mm(one_hot[e : e + step, block : block + depth], table[...])
            grad = mm(one_hot[e : e + step, 0 : 2 * block], pair[...])
            sig = sigmoid(pre)
            act = pre * sig
            hid[e : e + step, :] = act.astype(BF16)
            at = slice(b * edges + e, b * edges + e + step)
            pgrad[at, :] = (grad * (sig + act * (1.0 - sig))).astype(BF16)
        sub = lax.broadcasted_iota(jnp.int32, (block, edges), 0)
        one_hot_t[...] = jnp.where(sub == dst_row, 1.0, 0.0).astype(BF16)
        node = mm(one_hot_t[...], pgrad[b * edges : (b + 1) * edges, :])
        bias_total = bias_total + jnp.sum(node, axis=0, keepdims=True)
        node_sum[rows, :] = node.astype(BF16)
        hid_sum[rows, :] = mm(one_hot_t[...], hid[...]).astype(BF16)

    bias_sum[...] = jnp.broadcast_to(bias_total, bias_sum.shape)
    total = hid_sum[...]
    mesh_out[...] = (mesh[...].astype(F32) + mm(total, w_out[...])).astype(BF16)
    grads[0:width, :] = mm(total, cot[...], 0, 0)
    grads[width : 2 * width, :] = mm(mesh[...], node_sum[...], 0, 0)
    split_pieces(device_count, grads, kept, sent)


def scatter_rows(src, pgrad, one_hot_t, first_block, block_count):
    edges = src.shape[1]
    slots = one_hot_t.shape[0]
    parts = []
    for b in range(first_block, first_block + block_count):
        at = slice((b - first_block) * edges, (b - first_block + 1) * edges)
        for r in range(0, slots, 128):
            size = min(128, slots - r)
            sub = lax.broadcasted_iota(jnp.int32, (size, edges), 0) + r
            hot = jnp.where(sub == src[b : b + 1, :], 1.0, 0.0).astype(BF16)
            one_hot_t[r : r + size, at] = hot
    rows = slice(first_block * edges, (first_block + block_count) * edges)
    return mm(one_hot_t[...], pgrad[rows, :])


def scatter_kernel(src, pgrad, slot_sum, one_hot_t):
    slot_sum[...] = scatter_rows(src, pgrad, one_hot_t, 0, src.shape[0] // 2)


def backward_kernel(
    channels,
    device_count,
    src,
    pgrad,
    slot_half,
    latent,
    feat,
    w_pad,
    w_src,
    bias_sum,
    kept,
    sent,
    one_hot_t,
    grads,
):
    width = w_src.shape[0]
    padded = feat.shape[1]
    half = src.shape[0] // 2
    rest = src.shape[0] - half
    slot_sum = slot_half[...] + scatter_rows(src, pgrad, one_hot_t, half, rest)
    slot_grad = slot_sum.astype(BF16)
    grads[0:width, :] = mm(latent[...], slot_grad, 0, 0)
    buffer_grad = mm(slot_grad, w_src[...], 1, 1)
    pre = mm(feat[...], w_pad[...])
    sig = sigmoid(pre)
    embed = (buffer_grad * (sig * (1.0 + pre * (1.0 - sig)))).astype(BF16)
    grads[width : width + padded, :] = mm(feat[...], embed, 0, 0)
    grads[width + channels + 1 : width + channels + 2, :] = bias_sum[0:1, :]
    if grads.shape[0] > width + padded:
        spare = grads.shape[0] - width - padded
        grads[width + padded :, :] = jnp.zeros((spare, width), F32)
    split_pieces(device_count, grads, kept, sent)


def unpack_kernel(device_count, bounds, held, got, *targets):
    core, masks, pieces = place(device_count)
    piece = held.shape[0] // pieces
    used = bounds[-1][1]
    for c in range(2 * pieces):
        half = c // pieces
        begin, end = c * piece, (c + 1) * piece
        if begin >= used:
            continue
        slot = (c % pieces) ^ masks[half]
        at = pl.ds(pl.multiple_of(slot * piece, 16), piece)
        values = jnp.where(core == half, held[at, :].astype(F32), got[at, :].astype(F32))
        for (low, high), target in zip(bounds, targets):
            lo, hi = max(low, begin), min(high, end)
            if lo < hi:
                target[lo - low : hi - low, :] = values[lo - begin : hi - begin, :]


def shards(
    grid_feat,
    mesh_latent,
    cotangent,
    row_pack,
    edge_src,
    edge_dst,
    edge_count,
    w_embed,
    b_embed,
    w_src,
    w_dst,
    b_hidden,
    w_out,
):
    device_count = lax.axis_size("dom")
    own, channels = grid_feat.shape
    width = w_src.shape[0]
    peer_slots = row_pack.shape[0] // device_count
    more = device_count * peer_slots
    slots = own + more
    blocks, edges = edge_src.shape
    nodes = mesh_latent.shape[0]
    block = nodes // blocks
    padded = round_up(channels + 2, 128)
    depth = block + round_up(slots + 16, 128)
    first, second, last_bit = stage_bits(device_count)
    pieces = 1 << len(first)
    mesh_rows = round_up(2 * width, 32 * pieces)
    grid_rows = round_up(width + padded, 32 * pieces)
    half_blocks = blocks // 2
    stages = list(zip(first, second))

    vmem = pl.BlockSpec(memory_space=pltpu.VMEM)
    smem = pl.BlockSpec(memory_space=pltpu.SMEM)
    hbm = pl.BlockSpec(memory_space=pltpu.HBM)
    shape = jax.ShapeDtypeStruct

    def limit(mib):
        return pltpu.CompilerParams(vmem_limit_bytes=mib * 1024 * 1024)

    feat_t = grid_feat.T
    dma = pltpu.SemaphoreType.DMA
    send = pl.pallas_call(
        pick_kernel,
        out_shape=shape((device_count, peer_slots, padded), BF16),
        in_specs=[vmem, hbm],
        out_specs=vmem,
        scratch_shapes=[pltpu.VMEM((channels, own), BF16), dma((1,))],
        compiler_params=limit(16),
        cost_estimate=pl.CostEstimate(
            flops=20_000_000_000, bytes_accessed=own * padded * 2, transcendentals=0
        ),
        name="pick_rows",
    )(row_pack[None, :], feat_t)
    feat_in = lax.all_to_all(send, "dom", split_axis=0, concat_axis=0, tiled=True)

    forward_macs = (
        slots * width * (padded + width)
        + blocks * edges * width * (depth + 4 * block)
        + 5 * nodes * width * width
    )
    mesh_out, pgrad, latent, feat, w_pad, bias_sum, kept_mesh, sent_mesh = pl.pallas_call(
        functools.partial(forward_kernel, device_count),
        out_shape=(
            shape((nodes, width), BF16),
            shape((blocks * edges, width), BF16),
            shape((slots, width), BF16),
            shape((slots, padded), BF16),
            shape((padded, width), BF16),
            shape((8, width), F32),
            shape((mesh_rows // 2, width), F32),
            shape((mesh_rows // 2, width), BF16),
        ),
        in_specs=[smem] + [vmem] * 12,
        out_specs=(vmem,) * 8,
        scratch_shapes=[
            pltpu.VMEM((depth, width), BF16),
            pltpu.VMEM((2 * block, width), BF16),
            pltpu.VMEM((padded, width), F32),
            pltpu.VMEM((padded, own), F32),
            pltpu.VMEM((more, padded), F32),
            pltpu.VMEM((edges, depth + block), BF16),
            pltpu.VMEM((block, edges), BF16),
            pltpu.VMEM((edges, width), BF16),
            pltpu.VMEM((nodes, width), BF16),
            pltpu.VMEM((2, nodes, width), BF16),
            pltpu.VMEM((nodes, width), BF16),
            pltpu.VMEM((nodes, width), BF16),
            pltpu.VMEM((mesh_rows, width), F32),
        ],
        compiler_params=limit(40),
        cost_estimate=pl.CostEstimate(
            flops=2 * forward_macs,
            bytes_accessed=16 * own * width,
            transcendentals=blocks * edges * width,
        ),
        name="forward_rows",
    )(
        edge_count,
        edge_src,
        edge_dst,
        feat_in,
        feat_t,
        w_embed,
        b_embed,
        b_hidden,
        w_src,
        w_dst,
        w_out,
        mesh_latent,
        cotangent,
    )

    def swap(values, bits):
        return lax.ppermute(
            values, "dom", [(d, d ^ (1 << bits[d % 2])) for d in range(device_count)]
        )

    def cut(held):
        middle = held.shape[0] // 2
        return held[:middle], held[middle:].astype(BF16)

    def pair_sum(kept, sent):
        return cut(kept + swap(sent, (0, 0)).astype(F32))

    def reduce_pieces(held, got):
        for bits in stages[1:]:
            held, sent = cut(held + got.astype(F32))
            got = swap(sent, bits)
        held = (held + got.astype(F32)).astype(BF16)
        got = swap(held, (last_bit, last_bit))
        held = (held.astype(F32) + got.astype(F32)).astype(BF16)
        for bits in reversed(stages):
            held = jnp.concatenate([held, swap(held, bits)], axis=0)
        return held, swap(held, (0, 0))

    held_mesh, next_mesh = pair_sum(kept_mesh, sent_mesh)
    slot_half = pl.pallas_call(
        scatter_kernel,
        out_shape=shape((slots, width), F32),
        in_specs=[vmem] * 2,
        out_specs=vmem,
        scratch_shapes=[pltpu.VMEM((slots, half_blocks * edges), BF16)],
        compiler_params=limit(24),
        cost_estimate=pl.CostEstimate(
            flops=2 * half_blocks * edges * slots * width,
            bytes_accessed=half_blocks * edges * width * 2,
            transcendentals=0,
        ),
        name="scatter_rows",
    )(edge_src, pgrad)

    slot_half, held_mesh, next_mesh = lax.optimization_barrier((slot_half, held_mesh, next_mesh))
    got_mesh = swap(next_mesh, stages[0])
    kept_grid, sent_grid = pl.pallas_call(
        functools.partial(backward_kernel, channels, device_count),
        out_shape=(
            shape((grid_rows // 2, width), F32),
            shape((grid_rows // 2, width), BF16),
        ),
        in_specs=[vmem] * 8,
        out_specs=(vmem,) * 2,
        scratch_shapes=[
            pltpu.VMEM((slots, (blocks - half_blocks) * edges), BF16),
            pltpu.VMEM((grid_rows, width), F32),
        ],
        compiler_params=limit(40),
        cost_estimate=pl.CostEstimate(
            flops=2 * slots * width * (half_blocks * edges + 2 * width + 2 * padded),
            bytes_accessed=half_blocks * edges * width * 2,
            transcendentals=slots * width,
        ),
        name="backward_rows",
    )(edge_src, pgrad, slot_half, latent, feat, w_pad, w_src, bias_sum)

    sent_grid, got_mesh = lax.optimization_barrier((sent_grid, got_mesh))

    def unpack(pair, bounds):
        return pl.pallas_call(
            functools.partial(unpack_kernel, device_count, bounds),
            out_shape=tuple(shape((high - low, width), F32) for low, high in bounds),
            in_specs=[vmem] * 2,
            out_specs=(vmem,) * len(bounds),
            compiler_params=limit(16),
            name="unpack_rows",
        )(*pair)

    mesh_pair = reduce_pieces(held_mesh, got_mesh)
    held_grid, next_grid = pair_sum(kept_grid, sent_grid)
    grid_pair = reduce_pieces(held_grid, swap(next_grid, stages[0]))
    grad_out, grad_dst = unpack(mesh_pair, ((0, width), (width, 2 * width)))
    end = width + channels
    grad_src, grad_embed, biases = unpack(grid_pair, ((0, width), (width, end), (end, end + 2)))
    return mesh_out, grad_embed, grad_src, grad_dst, grad_out, biases


def solution(mesh):
    return jax.shard_map(
        shards,
        mesh=mesh,
        in_specs=(
            P(("ens", "dom"), None),
            P(("ens", "dom"), None),
            P(("ens", "dom"), None),
            P("dom"),
            P("dom", None),
            P("dom", None),
            P("dom"),
            P(),
            P(),
            P(),
            P(),
            P(),
            P(),
        ),
        out_specs=(
            P(("ens", "dom"), None),
            P("ens", None),
            P("ens", None),
            P("ens", None),
            P("ens", None),
            P("ens", None),
        ),
        check_vma=False,
    )
```

```python
import functools

import jax
import jax.numpy as jnp
from jax import lax
from jax.experimental import pallas as pl
from jax.experimental.pallas import tpu as pltpu
from jax.sharding import PartitionSpec as P

BF16 = jnp.bfloat16
F32 = jnp.float32


def mm(left, right, left_dim=1, right_dim=0):
    return lax.dot_general(
        left, right, (((left_dim,), (right_dim,)), ((), ())), preferred_element_type=F32
    )


def sigmoid(values):
    return 0.5 * jnp.tanh(0.5 * values) + 0.5


def halved(values):
    return (0.5 * values.astype(F32)).astype(BF16)


def round_up(value, step):
    return -(-value // step) * step


def fetch(source, target, sems, index):
    copy = pltpu.make_async_copy(source, target, sems.at[index])
    copy.start()
    return copy


def pick_kernel(row_pack, feat_hbm, send, feat_t, sems):
    rows_copy = fetch(feat_hbm, feat_t, sems, 0)
    channels, own = feat_t.shape
    peers, peer_slots, padded = send.shape
    row = lax.broadcasted_iota(jnp.int32, (own, peers * peer_slots), 0)
    pick = jnp.where(row == row_pack[...], 1.0, 0.0).astype(BF16)
    last = padded - 128
    lane = lax.broadcasted_iota(jnp.int32, (peers * peer_slots, 128), 1) + last
    ones = jnp.where(lane == channels, 1.0, 0.0).astype(BF16)
    rows_copy.wait()
    rows = mm(pick, feat_t[...], 0, 1)
    for j in range(peers):
        part = slice(j * peer_slots, (j + 1) * peer_slots)
        send[j, :, last:padded] = ones[part, :]
        send[j, :, 0:channels] = rows[part, :].astype(BF16)


def stage_bits(device_count):
    bits = device_count.bit_length() - 1
    first = list(range(1, bits - 1))
    second = first[1::-1] + first[2:]
    return first, second, bits - 1


def position_mask(me, order):
    mask = 0
    for i, bit in enumerate(order):
        mask = mask + (lax.rem(me // (1 << bit), 2) << (len(order) - 1 - i))
    return mask


def place(device_count, turn):
    me = lax.axis_index("dom")
    orders = stage_bits(device_count)[:2]
    masks = position_mask(me, orders[turn]), position_mask(me, orders[1 - turn])
    return lax.rem(me, 2), masks, 1 << len(orders[0])


def split_pieces(device_count, turn, grads, kept, sent):
    core, masks, pieces = place(device_count, turn)
    mine = jnp.where(core == 0, masks[0], masks[1])
    theirs = jnp.where(core == 0, masks[1], masks[0])
    piece = kept.shape[0] // pieces
    for p in range(pieces):
        at = pl.ds(pl.multiple_of((core * pieces + (mine ^ p)) * piece, 16), piece)
        kept[p * piece : (p + 1) * piece, :] = grads[at, :]
        at = pl.ds(pl.multiple_of(((1 - core) * pieces + (theirs ^ p)) * piece, 16), piece)
        sent[p * piece : (p + 1) * piece, :] = grads[at, :].astype(BF16)


def forward_kernel(
    device_count,
    count,
    src,
    dst,
    feat_in,
    feat_t,
    w_embed,
    b_embed,
    b_hidden,
    w_src,
    w_dst,
    w_out,
    mesh,
    cot,
    hid_sum,
    pgrad,
    latent,
    feat,
    w_pad,
    bias_sum,
    kept,
    sent,
    table,
    pair,
    wide,
    wide_t,
    incoming,
    one_hot,
    one_hot_t,
    hid,
    near,
    back,
    node_sum,
    grads,
):
    channels, own = feat_t.shape
    peers, peer_slots, padded = feat_in.shape
    more = peers * peer_slots
    slots = own + more
    blocks, edges = src.shape
    width = w_src.shape[0]
    nodes = mesh.shape[0]
    block = nodes // blocks
    depth = table.shape[0]
    step = 256

    last = padded - 32
    wide[last:padded, :] = jnp.zeros((32, width), F32)
    wide[0:channels, :] = w_embed[...].astype(F32)
    wide[channels : channels + 1, :] = b_embed[...].astype(F32).reshape(1, width)
    w_pad[...] = wide[...].astype(BF16)
    wide_t[last:padded, :] = jnp.zeros((32, own), F32)
    wide_t[0:channels, :] = feat_t[...].astype(F32)
    wide_t[channels : channels + 1, :] = jnp.ones((1, own), F32)
    feat[0:own, :] = jnp.transpose(wide_t[...]).astype(BF16)
    for j in range(peers):
        incoming[j * peer_slots : (j + 1) * peer_slots, :] = feat_in[j].astype(F32)
    feat[own:slots, :] = incoming[...].astype(BF16)
    for r in range(0, slots, step):
        end = min(r + step, slots)
        pre = mm(feat[r:end, :], w_pad[...])
        lat = (pre * sigmoid(pre)).astype(BF16)
        latent[r:end, :] = lat
        table[block + r : block + end, :] = halved(mm(lat, w_src[...]).astype(BF16))
    near[...] = halved(mm(mesh[...], w_dst[...]).astype(BF16))
    full = 0.5 * mm(cot[...], w_out[...], 1, 1)
    high = full.astype(BF16)
    back[0] = high
    back[1] = (full - high.astype(F32)).astype(BF16)
    tail = depth - slots - block
    tail_row = lax.broadcasted_iota(jnp.int32, (tail, width), 0)
    bias_row = 0.5 * b_hidden[...].astype(F32).reshape(1, width)
    table[slots + block : depth, :] = jnp.where(
        tail_row == 0, jnp.broadcast_to(bias_row, (tail, width)), 0.0
    ).astype(BF16)

    edge_lane = lax.broadcasted_iota(jnp.int32, (blocks, edges), 1)
    block_row = lax.broadcasted_iota(jnp.int32, (blocks, 1), 0)
    counts = jnp.zeros((blocks, 1), jnp.int32)
    for b in range(blocks):
        counts = jnp.where(block_row == b, count[b], counts)
    src_all = src[...]
    dst_all = jnp.where(edge_lane < counts, dst[...], -1)
    columns = jnp.transpose(jnp.concatenate([src_all, dst_all], axis=0))
    bias_total = jnp.zeros((1, width), F32)
    one, none = jnp.ones((), BF16), jnp.zeros((), BF16)

    for b in range(blocks):
        rows = slice(b * block, (b + 1) * block)
        table[0:block, :] = near[rows, :]
        pair[0:block, :] = back[0, rows, :]
        pair[block : 2 * block, :] = back[1, rows, :]
        dst_row = dst_all[b : b + 1, :]
        for e in range(0, edges, step):
            src_col = columns[e : e + step, b : b + 1]
            dst_col = columns[e : e + step, blocks + b : blocks + b + 1]
            src_wide = jnp.broadcast_to(src_col, (step, 128)).astype(jnp.int16)
            dst_wide = jnp.broadcast_to(dst_col, (step, block)).astype(jnp.int16)
            lane = lax.broadcasted_iota(jnp.int16, (step, block), 1)
            near_hot = jnp.where(lane == dst_wide, one, none)
            one_hot[e : e + step, 0:block] = near_hot
            one_hot[e : e + step, block : 2 * block] = near_hot
            for k in range(0, depth - block, 128):
                lane = lax.broadcasted_iota(jnp.int16, (step, 128), 1) + jnp.int16(k)
                hot = lane == src_wide
                if k <= slots < k + 128:
                    hot = hot | (lane == jnp.int16(slots))
                hot = jnp.where(hot, one, none)
                one_hot[e : e + step, 2 * block + k : 2 * block + k + 128] = hot
            pre = mm(one_hot[e : e + step, block : block + depth], table[...])
            grad = mm(one_hot[e : e + step, 0 : 2 * block], pair[...])
            bent = jnp.tanh(pre)
            rise = 1.0 + bent
            act = pre * rise
            hid[e : e + step, :] = act.astype(BF16)
            at = slice(b * edges + e, b * edges + e + step)
            pgrad[at, :] = (grad * (rise + act * (1.0 - bent))).astype(BF16)
        sub = lax.broadcasted_iota(jnp.int32, (block, edges), 0)
        one_hot_t[...] = jnp.where(sub == dst_row, 1.0, 0.0).astype(BF16)
        node = mm(one_hot_t[...], pgrad[b * edges : (b + 1) * edges, :])
        bias_total = bias_total + jnp.sum(node, axis=0, keepdims=True)
        node_sum[rows, :] = node.astype(BF16)
        hid_sum[rows, :] = mm(one_hot_t[...], hid[...]).astype(BF16)

    bias_sum[...] = jnp.broadcast_to(bias_total, bias_sum.shape)
    grads[0:width, :] = mm(hid_sum[...], cot[...], 0, 0)
    grads[width : 2 * width, :] = mm(mesh[...], node_sum[...], 0, 0)
    split_pieces(device_count, 0, grads, kept, sent)


def mesh_kernel(mesh, hid_sum, w_out, mesh_out):
    mesh_out[...] = (mesh[...].astype(F32) + mm(hid_sum[...], w_out[...])).astype(BF16)


def scatter_rows(src, pgrad, one_hot_t, first_block, block_count):
    edges = src.shape[1]
    slots = one_hot_t.shape[0]
    one, none = jnp.ones((), BF16), jnp.zeros((), BF16)
    for b in range(first_block, first_block + block_count):
        at = slice((b - first_block) * edges, (b - first_block + 1) * edges)
        for r in range(0, slots, 128):
            size = min(128, slots - r)
            sub = lax.broadcasted_iota(jnp.int16, (size, edges), 0) + jnp.int16(r)
            row = jnp.broadcast_to(src[b : b + 1, :], (size, edges)).astype(jnp.int16)
            one_hot_t[r : r + size, at] = jnp.where(sub == row, one, none)
    rows = slice(first_block * edges, (first_block + block_count) * edges)
    return mm(one_hot_t[...], pgrad[rows, :])


def scatter_kernel(src, pgrad, slot_sum, one_hot_t):
    slot_sum[...] = scatter_rows(src, pgrad, one_hot_t, 0, src.shape[0] // 2)


def backward_kernel(
    channels,
    device_count,
    src,
    pgrad,
    slot_half,
    latent,
    feat,
    w_pad,
    w_src,
    bias_sum,
    kept,
    sent,
    one_hot_t,
    grads,
):
    width = w_src.shape[0]
    padded = feat.shape[1]
    half = src.shape[0] // 2
    rest = src.shape[0] - half
    slot_sum = slot_half[...] + scatter_rows(src, pgrad, one_hot_t, half, rest)
    slot_grad = slot_sum.astype(BF16)
    grads[0:width, :] = mm(latent[...], slot_grad, 0, 0)
    buffer_grad = mm(slot_grad, w_src[...], 1, 1)
    pre = mm(feat[...], w_pad[...])
    sig = sigmoid(pre)
    embed = (buffer_grad * (sig * (1.0 + pre * (1.0 - sig)))).astype(BF16)
    grads[width : width + padded, :] = mm(feat[...], embed, 0, 0)
    grads[width + channels + 1 : width + channels + 2, :] = bias_sum[0:1, :]
    if grads.shape[0] > width + padded:
        spare = grads.shape[0] - width - padded
        grads[width + padded :, :] = jnp.zeros((spare, width), F32)
    split_pieces(device_count, 1, grads, kept, sent)


def unpack_kernel(device_count, turn, bounds, held, got, *targets):
    core, masks, pieces = place(device_count, turn)
    piece = held.shape[0] // pieces
    used = bounds[-1][1]
    for c in range(2 * pieces):
        half = c // pieces
        begin, end = c * piece, (c + 1) * piece
        if begin >= used:
            continue
        slot = (c % pieces) ^ masks[half]
        at = pl.ds(pl.multiple_of(slot * piece, 16), piece)
        values = jnp.where(core == half, held[at, :].astype(F32), got[at, :].astype(F32))
        for (low, high), target in zip(bounds, targets):
            lo, hi = max(low, begin), min(high, end)
            if lo < hi:
                target[lo - low : hi - low, :] = values[lo - begin : hi - begin, :]


def shards(
    grid_feat,
    mesh_latent,
    cotangent,
    row_pack,
    edge_src,
    edge_dst,
    edge_count,
    w_embed,
    b_embed,
    w_src,
    w_dst,
    b_hidden,
    w_out,
):
    device_count = lax.axis_size("dom")
    own, channels = grid_feat.shape
    width = w_src.shape[0]
    peer_slots = row_pack.shape[0] // device_count
    more = device_count * peer_slots
    slots = own + more
    blocks, edges = edge_src.shape
    nodes = mesh_latent.shape[0]
    block = nodes // blocks
    padded = round_up(channels + 2, 128)
    depth = block + round_up(slots + 16, 128)
    first, second, last_bit = stage_bits(device_count)
    pieces = 1 << len(first)
    mesh_rows = round_up(2 * width, 32 * pieces)
    grid_rows = round_up(width + padded, 32 * pieces)
    half_blocks = blocks // 2
    stages = list(zip(first, second)), list(zip(second, first))

    vmem = pl.BlockSpec(memory_space=pltpu.VMEM)
    smem = pl.BlockSpec(memory_space=pltpu.SMEM)
    hbm = pl.BlockSpec(memory_space=pltpu.HBM)
    shape = jax.ShapeDtypeStruct

    def limit(mib):
        return pltpu.CompilerParams(vmem_limit_bytes=mib * 1024 * 1024)

    feat_t = grid_feat.T
    dma = pltpu.SemaphoreType.DMA
    send = pl.pallas_call(
        pick_kernel,
        out_shape=shape((device_count, peer_slots, padded), BF16),
        in_specs=[vmem, hbm],
        out_specs=vmem,
        scratch_shapes=[pltpu.VMEM((channels, own), BF16), dma((1,))],
        compiler_params=limit(16),
        cost_estimate=pl.CostEstimate(
            flops=20_000_000_000, bytes_accessed=own * padded * 2, transcendentals=0
        ),
        name="pick_rows",
    )(row_pack[None, :], feat_t)
    feat_in = lax.all_to_all(send, "dom", split_axis=0, concat_axis=0, tiled=True)

    forward_macs = (
        slots * width * (padded + width)
        + blocks * edges * width * (depth + 4 * block)
        + 5 * nodes * width * width
    )
    hid_sum, pgrad, latent, feat, w_pad, bias_sum, kept_mesh, sent_mesh = pl.pallas_call(
        functools.partial(forward_kernel, device_count),
        out_shape=(
            shape((nodes, width), BF16),
            shape((blocks * edges, width), BF16),
            shape((slots, width), BF16),
            shape((slots, padded), BF16),
            shape((padded, width), BF16),
            shape((8, width), F32),
            shape((mesh_rows // 2, width), F32),
            shape((mesh_rows // 2, width), BF16),
        ),
        in_specs=[smem] + [vmem] * 12,
        out_specs=(vmem,) * 8,
        scratch_shapes=[
            pltpu.VMEM((depth, width), BF16),
            pltpu.VMEM((2 * block, width), BF16),
            pltpu.VMEM((padded, width), F32),
            pltpu.VMEM((padded, own), F32),
            pltpu.VMEM((more, padded), F32),
            pltpu.VMEM((edges, depth + block), BF16),
            pltpu.VMEM((block, edges), BF16),
            pltpu.VMEM((edges, width), BF16),
            pltpu.VMEM((nodes, width), BF16),
            pltpu.VMEM((2, nodes, width), BF16),
            pltpu.VMEM((nodes, width), BF16),
            pltpu.VMEM((mesh_rows, width), F32),
        ],
        compiler_params=limit(40),
        cost_estimate=pl.CostEstimate(
            flops=2 * forward_macs,
            bytes_accessed=16 * own * width,
            transcendentals=blocks * edges * width,
        ),
        name="forward_rows",
    )(
        edge_count,
        edge_src,
        edge_dst,
        feat_in,
        feat_t,
        w_embed,
        b_embed,
        b_hidden,
        w_src,
        w_dst,
        w_out,
        mesh_latent,
        cotangent,
    )

    def swap(values, bits):
        return lax.ppermute(
            values, "dom", [(d, d ^ (1 << bits[d % 2])) for d in range(device_count)]
        )

    def cut(held):
        middle = held.shape[0] // 2
        return held[:middle], held[middle:].astype(BF16)

    def pair_sum(kept, sent):
        return cut(kept + swap(sent, (0, 0)).astype(F32))

    def reduce_pieces(turn, held, got, done=1):
        for bits in stages[turn][done:]:
            held, sent = cut(held + got.astype(F32))
            got = swap(sent, bits)
        held = (held + got.astype(F32)).astype(BF16)
        got = swap(held, (last_bit, last_bit))
        held = (held.astype(F32) + got.astype(F32)).astype(BF16)
        for bits in reversed(stages[turn]):
            held = jnp.concatenate([held, swap(held, bits)], axis=0)
        return held, swap(held, (0, 0))

    held_mesh, next_mesh = pair_sum(kept_mesh, sent_mesh)
    slot_half = pl.pallas_call(
        scatter_kernel,
        out_shape=shape((slots, width), F32),
        in_specs=[vmem] * 2,
        out_specs=vmem,
        scratch_shapes=[pltpu.VMEM((slots, half_blocks * edges), BF16)],
        compiler_params=limit(24),
        cost_estimate=pl.CostEstimate(
            flops=2 * half_blocks * edges * slots * width,
            bytes_accessed=half_blocks * edges * width * 2,
            transcendentals=0,
        ),
        name="scatter_rows",
    )(edge_src, pgrad)

    slot_half, held_mesh, next_mesh = lax.optimization_barrier((slot_half, held_mesh, next_mesh))
    got_mesh = swap(next_mesh, stages[0][0])
    kept_grid, sent_grid = pl.pallas_call(
        functools.partial(backward_kernel, channels, device_count),
        out_shape=(
            shape((grid_rows // 2, width), F32),
            shape((grid_rows // 2, width), BF16),
        ),
        in_specs=[vmem] * 8,
        out_specs=(vmem,) * 2,
        scratch_shapes=[
            pltpu.VMEM((slots, (blocks - half_blocks) * edges), BF16),
            pltpu.VMEM((grid_rows, width), F32),
        ],
        compiler_params=limit(40),
        cost_estimate=pl.CostEstimate(
            flops=2 * slots * width * (half_blocks * edges + 2 * width + 2 * padded),
            bytes_accessed=half_blocks * edges * width * 2,
            transcendentals=slots * width,
        ),
        name="backward_rows",
    )(edge_src, pgrad, slot_half, latent, feat, w_pad, w_src, bias_sum)

    sent_grid, got_mesh = lax.optimization_barrier((sent_grid, got_mesh))

    mesh_out = pl.pallas_call(
        mesh_kernel,
        out_shape=shape((nodes, width), BF16),
        in_specs=[vmem] * 3,
        out_specs=vmem,
        compiler_params=limit(16),
        cost_estimate=pl.CostEstimate(
            flops=2 * nodes * width * width, bytes_accessed=8 * nodes * width, transcendentals=0
        ),
        name="mesh_rows",
    )(mesh_latent, hid_sum, w_out)

    def unpack(turn, pair, bounds):
        return pl.pallas_call(
            functools.partial(unpack_kernel, device_count, turn, bounds),
            out_shape=tuple(shape((high - low, width), F32) for low, high in bounds),
            in_specs=[vmem] * 2,
            out_specs=(vmem,) * len(bounds),
            compiler_params=limit(16),
            name="unpack_rows",
        )(*pair)

    mesh_pair = reduce_pieces(0, held_mesh, got_mesh)
    held_grid, next_grid = pair_sum(kept_grid, sent_grid)
    mesh_out, next_grid = lax.optimization_barrier((mesh_out, next_grid))
    grid_pair = reduce_pieces(1, held_grid, swap(next_grid, stages[1][0]))
    grad_out, grad_dst = unpack(0, mesh_pair, ((0, width), (width, 2 * width)))
    end = width + channels
    grad_src, grad_embed, biases = unpack(1, grid_pair, ((0, width), (width, end), (end, end + 2)))
    return mesh_out, grad_embed, grad_src, grad_dst, grad_out, biases


def solution(mesh):
    return jax.shard_map(
        shards,
        mesh=mesh,
        in_specs=(
            P(("ens", "dom"), None),
            P(("ens", "dom"), None),
            P(("ens", "dom"), None),
            P("dom"),
            P("dom", None),
            P("dom", None),
            P("dom"),
            P(),
            P(),
            P(),
            P(),
            P(),
            P(),
        ),
        out_specs=(
            P(("ens", "dom"), None),
            P("ens", None),
            P("ens", None),
            P("ens", None),
            P("ens", None),
            P("ens", None),
        ),
        check_vma=False,
    )
```

```python
import functools

import jax
import jax.numpy as jnp
from jax import lax
from jax.experimental import pallas as pl
from jax.experimental.pallas import tpu as pltpu
from jax.sharding import PartitionSpec as P

BF16 = jnp.bfloat16
F32 = jnp.float32


def mm(left, right, left_dim=1, right_dim=0):
    return lax.dot_general(
        left, right, (((left_dim,), (right_dim,)), ((), ())), preferred_element_type=F32
    )


def sigmoid(values):
    return 0.5 * jnp.tanh(0.5 * values) + 0.5


def halved(values):
    return (0.5 * values.astype(F32)).astype(BF16)


def round_up(value, step):
    return -(-value // step) * step


def fetch(source, target, sems, index):
    copy = pltpu.make_async_copy(source, target, sems.at[index])
    copy.start()
    return copy


def pick_kernel(row_pack, feat_hbm, send, feat_t, sems):
    rows_copy = fetch(feat_hbm, feat_t, sems, 0)
    channels, own = feat_t.shape
    peers, peer_slots, padded = send.shape
    row = lax.broadcasted_iota(jnp.int32, (own, peers * peer_slots), 0)
    pick = jnp.where(row == row_pack[...], 1.0, 0.0).astype(BF16)
    last = padded - 128
    lane = lax.broadcasted_iota(jnp.int32, (peers * peer_slots, 128), 1) + last
    ones = jnp.where(lane == channels, 1.0, 0.0).astype(BF16)
    rows_copy.wait()
    rows = mm(pick, feat_t[...], 0, 1)
    for j in range(peers):
        part = slice(j * peer_slots, (j + 1) * peer_slots)
        send[j, :, last:padded] = ones[part, :]
        send[j, :, 0:channels] = rows[part, :].astype(BF16)


def stage_bits(device_count):
    bits = device_count.bit_length() - 1
    first = list(range(1, bits - 1))
    second = first[1::-1] + first[2:]
    return first, second, bits - 1


def position_mask(me, order):
    mask = 0
    for i, bit in enumerate(order):
        mask = mask + (lax.rem(me // (1 << bit), 2) << (len(order) - 1 - i))
    return mask


def place(device_count, turn):
    me = lax.axis_index("dom")
    orders = stage_bits(device_count)[:2]
    masks = position_mask(me, orders[turn]), position_mask(me, orders[1 - turn])
    return lax.rem(me, 2), masks, 1 << len(orders[0])


def split_pieces(device_count, turn, grads, kept, sent):
    core, masks, pieces = place(device_count, turn)
    mine = jnp.where(core == 0, masks[0], masks[1])
    theirs = jnp.where(core == 0, masks[1], masks[0])
    piece = kept.shape[0] // pieces
    for p in range(pieces):
        at = pl.ds(pl.multiple_of((core * pieces + (mine ^ p)) * piece, 16), piece)
        kept[p * piece : (p + 1) * piece, :] = grads[at, :]
        at = pl.ds(pl.multiple_of(((1 - core) * pieces + (theirs ^ p)) * piece, 16), piece)
        sent[p * piece : (p + 1) * piece, :] = grads[at, :].astype(BF16)


def forward_kernel(
    device_count,
    count,
    src,
    dst,
    feat_in,
    feat_t,
    w_embed,
    b_embed,
    b_hidden,
    w_src,
    w_dst,
    w_out,
    mesh,
    cot,
    hid_sum,
    pgrad,
    latent,
    feat,
    slope,
    bias_sum,
    kept,
    sent,
    w_pad,
    table,
    pair,
    wide,
    wide_t,
    incoming,
    one_hot,
    one_hot_t,
    hid,
    near,
    back,
    node_sum,
    grads,
):
    channels, own = feat_t.shape
    peers, peer_slots, padded = feat_in.shape
    more = peers * peer_slots
    slots = own + more
    blocks, edges = src.shape
    width = w_src.shape[0]
    nodes = mesh.shape[0]
    block = nodes // blocks
    depth = table.shape[0]
    step = 256

    last = padded - 32
    wide[last:padded, :] = jnp.zeros((32, width), F32)
    wide[0:channels, :] = w_embed[...].astype(F32)
    wide[channels : channels + 1, :] = b_embed[...].astype(F32).reshape(1, width)
    w_pad[...] = wide[...].astype(BF16)
    wide_t[last:padded, :] = jnp.zeros((32, own), F32)
    wide_t[0:channels, :] = feat_t[...].astype(F32)
    wide_t[channels : channels + 1, :] = jnp.ones((1, own), F32)
    feat[0:own, :] = jnp.transpose(wide_t[...]).astype(BF16)
    for j in range(peers):
        incoming[j * peer_slots : (j + 1) * peer_slots, :] = feat_in[j].astype(F32)
    feat[own:slots, :] = incoming[...].astype(BF16)
    for r in range(0, slots, step):
        end = min(r + step, slots)
        pre = mm(feat[r:end, :], w_pad[...])
        sig = sigmoid(pre)
        lat = (pre * sig).astype(BF16)
        latent[r:end, :] = lat
        slope[r:end, :] = sig * (1.0 + pre * (1.0 - sig))
        table[block + r : block + end, :] = halved(mm(lat, w_src[...]).astype(BF16))
    near[...] = halved(mm(mesh[...], w_dst[...]).astype(BF16))
    full = 0.5 * mm(cot[...], w_out[...], 1, 1)
    high = full.astype(BF16)
    back[0] = high
    back[1] = (full - high.astype(F32)).astype(BF16)
    tail = depth - slots - block
    tail_row = lax.broadcasted_iota(jnp.int32, (tail, width), 0)
    bias_row = 0.5 * b_hidden[...].astype(F32).reshape(1, width)
    table[slots + block : depth, :] = jnp.where(
        tail_row == 0, jnp.broadcast_to(bias_row, (tail, width)), 0.0
    ).astype(BF16)

    edge_lane = lax.broadcasted_iota(jnp.int32, (blocks, edges), 1)
    block_row = lax.broadcasted_iota(jnp.int32, (blocks, 1), 0)
    counts = jnp.zeros((blocks, 1), jnp.int32)
    for b in range(blocks):
        counts = jnp.where(block_row == b, count[b], counts)
    src_all = src[...]
    dst_all = jnp.where(edge_lane < counts, dst[...], -1)
    columns = jnp.transpose(jnp.concatenate([src_all, dst_all], axis=0))
    bias_total = jnp.zeros((1, width), F32)
    one, none = jnp.ones((), BF16), jnp.zeros((), BF16)

    for b in range(blocks):
        rows = slice(b * block, (b + 1) * block)
        table[0:block, :] = near[rows, :]
        pair[0:block, :] = back[0, rows, :]
        pair[block : 2 * block, :] = back[1, rows, :]
        dst_row = dst_all[b : b + 1, :]
        for e in range(0, edges, step):
            src_col = columns[e : e + step, b : b + 1]
            dst_col = columns[e : e + step, blocks + b : blocks + b + 1]
            src_wide = jnp.broadcast_to(src_col, (step, 128)).astype(jnp.int16)
            dst_wide = jnp.broadcast_to(dst_col, (step, block)).astype(jnp.int16)
            lane = lax.broadcasted_iota(jnp.int16, (step, block), 1)
            near_hot = jnp.where(lane == dst_wide, one, none)
            one_hot[e : e + step, 0:block] = near_hot
            one_hot[e : e + step, block : 2 * block] = near_hot
            for k in range(0, depth - block, 128):
                lane = lax.broadcasted_iota(jnp.int16, (step, 128), 1) + jnp.int16(k)
                hot = lane == src_wide
                if k <= slots < k + 128:
                    hot = hot | (lane == jnp.int16(slots))
                hot = jnp.where(hot, one, none)
                one_hot[e : e + step, 2 * block + k : 2 * block + k + 128] = hot
            pre = mm(one_hot[e : e + step, block : block + depth], table[...])
            grad = mm(one_hot[e : e + step, 0 : 2 * block], pair[...])
            bent = jnp.tanh(pre)
            rise = 1.0 + bent
            act = pre * rise
            hid[e : e + step, :] = act.astype(BF16)
            at = slice(b * edges + e, b * edges + e + step)
            pgrad[at, :] = (grad * (rise + act * (1.0 - bent))).astype(BF16)
        sub = lax.broadcasted_iota(jnp.int32, (block, edges), 0)
        one_hot_t[...] = jnp.where(sub == dst_row, 1.0, 0.0).astype(BF16)
        node = mm(one_hot_t[...], pgrad[b * edges : (b + 1) * edges, :])
        bias_total = bias_total + jnp.sum(node, axis=0, keepdims=True)
        node_sum[rows, :] = node.astype(BF16)
        hid_sum[rows, :] = mm(one_hot_t[...], hid[...]).astype(BF16)

    bias_sum[...] = jnp.broadcast_to(bias_total, bias_sum.shape)
    grads[0:width, :] = mm(hid_sum[...], cot[...], 0, 0)
    grads[width : 2 * width, :] = mm(mesh[...], node_sum[...], 0, 0)
    split_pieces(device_count, 0, grads, kept, sent)


def mesh_kernel(mesh, hid_sum, w_out, mesh_out):
    mesh_out[...] = (mesh[...].astype(F32) + mm(hid_sum[...], w_out[...])).astype(BF16)


def scatter_rows(src, pgrad, one_hot_t, first_block, block_count):
    edges = src.shape[1]
    slots = one_hot_t.shape[0]
    one, none = jnp.ones((), BF16), jnp.zeros((), BF16)
    for b in range(first_block, first_block + block_count):
        at = slice((b - first_block) * edges, (b - first_block + 1) * edges)
        for r in range(0, slots, 128):
            size = min(128, slots - r)
            sub = lax.broadcasted_iota(jnp.int16, (size, edges), 0) + jnp.int16(r)
            row = jnp.broadcast_to(src[b : b + 1, :], (size, edges)).astype(jnp.int16)
            one_hot_t[r : r + size, at] = jnp.where(sub == row, one, none)
    rows = slice(first_block * edges, (first_block + block_count) * edges)
    return mm(one_hot_t[...], pgrad[rows, :])


def scatter_kernel(src, pgrad, slot_sum, one_hot_t):
    slot_sum[...] = scatter_rows(src, pgrad, one_hot_t, 0, src.shape[0] // 2)


def backward_kernel(
    channels,
    device_count,
    src,
    pgrad,
    slot_half,
    latent,
    feat,
    slope,
    w_src,
    bias_sum,
    kept,
    sent,
    one_hot_t,
    grads,
):
    width = w_src.shape[0]
    padded = feat.shape[1]
    half = src.shape[0] // 2
    rest = src.shape[0] - half
    slot_sum = slot_half[...] + scatter_rows(src, pgrad, one_hot_t, half, rest)
    slot_grad = slot_sum.astype(BF16)
    grads[0:width, :] = mm(latent[...], slot_grad, 0, 0)
    buffer_grad = mm(slot_grad, w_src[...], 1, 1)
    embed = (buffer_grad * slope[...]).astype(BF16)
    grads[width : width + padded, :] = mm(feat[...], embed, 0, 0)
    grads[width + channels + 1 : width + channels + 2, :] = bias_sum[0:1, :]
    if grads.shape[0] > width + padded:
        spare = grads.shape[0] - width - padded
        grads[width + padded :, :] = jnp.zeros((spare, width), F32)
    split_pieces(device_count, 1, grads, kept, sent)


def segments(bounds, half_rows):
    found = []
    for half in range(2):
        for index, (low, high) in enumerate(bounds):
            begin, end = max(low, half * half_rows), min(high, (half + 1) * half_rows)
            if begin < end:
                found.append((half, index, begin, end))
    return found


def unpack_kernel(device_count, chains, own_half, *refs):
    count = sum(len(bounds) for _, bounds in chains)
    chain_rows, refs = refs[0 : len(chains)], refs[len(chains) :]
    targets = refs[0:count] if own_half else refs[count : 2 * count]
    buffers, sems = refs[count if own_half else 2 * count : -1], refs[-1]

    def move(half, turn, bounds, rows, base, skip):
        _, masks, pieces = place(device_count, turn)
        parts = segments(bounds, rows.shape[0])
        piece = rows.shape[0] // pieces
        for p in range(pieces):
            begin = half * rows.shape[0] + p * piece
            at = pl.ds(pl.multiple_of((p ^ masks[half]) * piece, 16), piece)
            values = rows[at, :].astype(F32)
            for k, (owner, _, low, high) in enumerate(parts):
                lo, hi = max(low, begin), min(high, begin + piece)
                if owner == half and lo < hi:
                    buffers[skip + k][lo - low : hi - low, :] = values[lo - begin : hi - begin, :]
        copies = []
        for k, (owner, index, low, high) in enumerate(parts):
            if owner == half:
                target = targets[base + index]
                if high - low < target.shape[0]:
                    first = low - bounds[index][0]
                    target = target.at[first : first + high - low, :]
                copies.append(fetch(buffers[skip + k], target, sems, skip + k))
        return copies

    def move_all(half):
        base, skip, copies = 0, 0, []
        for (turn, bounds), rows in zip(chains, chain_rows):
            copies += move(half, turn, bounds, rows, base, skip)
            base += len(bounds)
            skip += len(segments(bounds, rows.shape[0]))
        for copy in copies:
            copy.wait()

    core = lax.rem(lax.axis_index("dom"), 2)
    which = core if own_half else 1 - core
    for half in range(2):
        pl.when(which == half)(functools.partial(move_all, half))


def shards(
    grid_feat,
    mesh_latent,
    cotangent,
    row_pack,
    edge_src,
    edge_dst,
    edge_count,
    w_embed,
    b_embed,
    w_src,
    w_dst,
    b_hidden,
    w_out,
):
    device_count = lax.axis_size("dom")
    own, channels = grid_feat.shape
    width = w_src.shape[0]
    peer_slots = row_pack.shape[0] // device_count
    more = device_count * peer_slots
    slots = own + more
    blocks, edges = edge_src.shape
    nodes = mesh_latent.shape[0]
    block = nodes // blocks
    padded = round_up(channels + 2, 128)
    depth = block + round_up(slots + 16, 128)
    first, second, last_bit = stage_bits(device_count)
    pieces = 1 << len(first)
    mesh_rows = round_up(2 * width, 32 * pieces)
    grid_rows = round_up(width + padded, 32 * pieces)
    half_blocks = blocks // 2
    stages = list(zip(first, second)), list(zip(second, first))

    vmem = pl.BlockSpec(memory_space=pltpu.VMEM)
    smem = pl.BlockSpec(memory_space=pltpu.SMEM)
    hbm = pl.BlockSpec(memory_space=pltpu.HBM)
    shape = jax.ShapeDtypeStruct

    def limit(mib):
        return pltpu.CompilerParams(vmem_limit_bytes=mib * 1024 * 1024)

    feat_t = grid_feat.T
    dma = pltpu.SemaphoreType.DMA
    send = pl.pallas_call(
        pick_kernel,
        out_shape=shape((device_count, peer_slots, padded), BF16),
        in_specs=[vmem, hbm],
        out_specs=vmem,
        scratch_shapes=[pltpu.VMEM((channels, own), BF16), dma((1,))],
        compiler_params=limit(16),
        cost_estimate=pl.CostEstimate(
            flops=20_000_000_000, bytes_accessed=own * padded * 2, transcendentals=0
        ),
        name="pick_rows",
    )(row_pack[None, :], feat_t)
    feat_in = lax.all_to_all(send, "dom", split_axis=0, concat_axis=0, tiled=True)

    forward_macs = (
        slots * width * (padded + width)
        + blocks * edges * width * (depth + 4 * block)
        + 5 * nodes * width * width
    )
    hid_sum, pgrad, latent, feat, slope, bias_sum, kept_mesh, sent_mesh = pl.pallas_call(
        functools.partial(forward_kernel, device_count),
        out_shape=(
            shape((nodes, width), BF16),
            shape((blocks * edges, width), BF16),
            shape((slots, width), BF16),
            shape((slots, padded), BF16),
            shape((slots, width), F32),
            shape((8, width), F32),
            shape((mesh_rows // 2, width), F32),
            shape((mesh_rows // 2, width), BF16),
        ),
        in_specs=[smem] + [vmem] * 12,
        out_specs=(vmem,) * 8,
        scratch_shapes=[
            pltpu.VMEM((padded, width), BF16),
            pltpu.VMEM((depth, width), BF16),
            pltpu.VMEM((2 * block, width), BF16),
            pltpu.VMEM((padded, width), F32),
            pltpu.VMEM((padded, own), F32),
            pltpu.VMEM((more, padded), F32),
            pltpu.VMEM((edges, depth + block), BF16),
            pltpu.VMEM((block, edges), BF16),
            pltpu.VMEM((edges, width), BF16),
            pltpu.VMEM((nodes, width), BF16),
            pltpu.VMEM((2, nodes, width), BF16),
            pltpu.VMEM((nodes, width), BF16),
            pltpu.VMEM((mesh_rows, width), F32),
        ],
        compiler_params=limit(40),
        cost_estimate=pl.CostEstimate(
            flops=2 * forward_macs,
            bytes_accessed=16 * own * width,
            transcendentals=blocks * edges * width,
        ),
        name="forward_rows",
    )(
        edge_count,
        edge_src,
        edge_dst,
        feat_in,
        feat_t,
        w_embed,
        b_embed,
        b_hidden,
        w_src,
        w_dst,
        w_out,
        mesh_latent,
        cotangent,
    )

    def swap(values, bits):
        return lax.ppermute(
            values, "dom", [(d, d ^ (1 << bits[d % 2])) for d in range(device_count)]
        )

    def cut(held):
        middle = held.shape[0] // 2
        return held[:middle], held[middle:].astype(BF16)

    def pair_sum(kept, sent):
        return cut(kept + swap(sent, (0, 0)).astype(F32))

    def reduce_pieces(turn, held, got, done=1):
        for bits in stages[turn][done:]:
            held, sent = cut(held + got.astype(F32))
            got = swap(sent, bits)
        held = (held + got.astype(F32)).astype(BF16)
        got = swap(held, (last_bit, last_bit))
        held = (held.astype(F32) + got.astype(F32)).astype(BF16)
        for bits in reversed(stages[turn]):
            held = jnp.concatenate([held, swap(held, bits)], axis=0)
        return held, swap(held, (0, 0))

    held_mesh, next_mesh = pair_sum(kept_mesh, sent_mesh)
    slot_half = pl.pallas_call(
        scatter_kernel,
        out_shape=shape((slots, width), F32),
        in_specs=[vmem] * 2,
        out_specs=vmem,
        scratch_shapes=[pltpu.VMEM((slots, half_blocks * edges), BF16)],
        compiler_params=limit(24),
        cost_estimate=pl.CostEstimate(
            flops=2 * half_blocks * edges * slots * width,
            bytes_accessed=half_blocks * edges * width * 2,
            transcendentals=0,
        ),
        name="scatter_rows",
    )(edge_src, pgrad)

    slot_half, held_mesh, next_mesh = lax.optimization_barrier((slot_half, held_mesh, next_mesh))
    got_mesh = swap(next_mesh, stages[0][0])
    kept_grid, sent_grid = pl.pallas_call(
        functools.partial(backward_kernel, channels, device_count),
        out_shape=(
            shape((grid_rows // 2, width), F32),
            shape((grid_rows // 2, width), BF16),
        ),
        in_specs=[vmem] * 8,
        out_specs=(vmem,) * 2,
        scratch_shapes=[
            pltpu.VMEM((slots, (blocks - half_blocks) * edges), BF16),
            pltpu.VMEM((grid_rows, width), F32),
        ],
        compiler_params=limit(40),
        cost_estimate=pl.CostEstimate(
            flops=2 * slots * width * (half_blocks * edges + 2 * width + 2 * padded),
            bytes_accessed=half_blocks * edges * width * 2,
            transcendentals=slots * width,
        ),
        name="backward_rows",
    )(edge_src, pgrad, slot_half, latent, feat, slope, w_src, bias_sum)


    mesh_out = pl.pallas_call(
        mesh_kernel,
        out_shape=shape((nodes, width), BF16),
        in_specs=[vmem] * 3,
        out_specs=vmem,
        compiler_params=limit(16),
        cost_estimate=pl.CostEstimate(
            flops=2 * nodes * width * width, bytes_accessed=8 * nodes * width, transcendentals=0
        ),
        name="mesh_rows",
    )(mesh_latent, hid_sum, w_out)

    def unpack(chains, pairs):
        sizes = [high - low for _, bounds in chains for low, high in bounds]
        parts = [
            high - low
            for (_, bounds), (rows, _) in zip(chains, pairs)
            for _, _, low, high in segments(bounds, rows.shape[0])
        ]
        targets = ()
        for own_half, chain_rows in zip((True, False), zip(*pairs)):
            targets = pl.pallas_call(
                functools.partial(unpack_kernel, device_count, chains, own_half),
                out_shape=tuple(shape((size, width), F32) for size in sizes),
                in_specs=[vmem] * len(chains) + [hbm] * len(targets),
                out_specs=(hbm,) * len(sizes),
                scratch_shapes=[pltpu.VMEM((size, width), F32) for size in parts]
                + [dma((len(parts),))],
                input_output_aliases={len(chains) + k: k for k in range(len(targets))},
                compiler_params=limit(12),
                name="unpack_rows",
            )(*chain_rows, *targets)
        return targets

    mesh_out, got_mesh = lax.optimization_barrier((mesh_out, got_mesh))
    held_mesh, next_mesh = cut(held_mesh + got_mesh.astype(F32))
    held_grid, next_grid = pair_sum(kept_grid, sent_grid)
    next_grid, next_mesh = lax.optimization_barrier((next_grid, next_mesh))
    got_mesh = swap(next_mesh, stages[0][1])
    mesh_pair = reduce_pieces(0, held_mesh, got_mesh, 2)
    grid_pair = reduce_pieces(1, held_grid, swap(next_grid, stages[1][0]))
    end = width + channels
    mesh_bounds = ((0, width), (width, 2 * width))
    grid_bounds = ((0, width), (width, end), (end, end + 2))
    grad_out, grad_dst, grad_src, grad_embed, biases = unpack(
        ((0, mesh_bounds), (1, grid_bounds)), (mesh_pair, grid_pair)
    )
    return mesh_out, grad_embed, grad_src, grad_dst, grad_out, biases


def solution(mesh):
    return jax.shard_map(
        shards,
        mesh=mesh,
        in_specs=(
            P(("ens", "dom"), None),
            P(("ens", "dom"), None),
            P(("ens", "dom"), None),
            P("dom"),
            P("dom", None),
            P("dom", None),
            P("dom"),
            P(),
            P(),
            P(),
            P(),
            P(),
            P(),
        ),
        out_specs=(
            P(("ens", "dom"), None),
            P("ens", None),
            P("ens", None),
            P("ens", None),
            P("ens", None),
            P("ens", None),
        ),
        check_vma=False,
    )
```

```python
import functools

import jax
import jax.numpy as jnp
from jax import lax
from jax.experimental import pallas as pl
from jax.experimental.pallas import tpu as pltpu
from jax.sharding import PartitionSpec as P

BF16 = jnp.bfloat16
F32 = jnp.float32


def mm(left, right, left_dim=1, right_dim=0):
    return lax.dot_general(
        left, right, (((left_dim,), (right_dim,)), ((), ())), preferred_element_type=F32
    )


def sigmoid(values):
    return 0.5 * jnp.tanh(0.5 * values) + 0.5


def halved(values):
    return (0.5 * values.astype(F32)).astype(BF16)


def round_up(value, step):
    return -(-value // step) * step


def fetch(source, target, sems, index):
    copy = pltpu.make_async_copy(source, target, sems.at[index])
    copy.start()
    return copy


def begin_kernel(flag):
    flag[...] = jnp.zeros_like(flag)


def pick_kernel(flag, row_pack, feat_t, send):
    channels, own = feat_t.shape
    peers, peer_slots, padded = send.shape
    row = lax.broadcasted_iota(jnp.int32, (own, peers * peer_slots), 0)
    pick = jnp.where(row == row_pack[...], 1.0, 0.0).astype(BF16)
    last = padded - 128
    lane = lax.broadcasted_iota(jnp.int32, (peers * peer_slots, 128), 1) + last
    ones = jnp.where(lane == channels, 1.0, 0.0).astype(BF16)
    rows = mm(pick, feat_t[...], 0, 1)
    for j in range(peers):
        part = slice(j * peer_slots, (j + 1) * peer_slots)
        send[j, :, last:padded] = ones[part, :]
        send[j, :, 0:channels] = rows[part, :].astype(BF16)


def stage_bits(device_count):
    bits = device_count.bit_length() - 1
    first = list(range(1, bits - 1))
    second = first[1::-1] + first[2:]
    return first, second, bits - 1


def position_mask(me, order):
    mask = 0
    for i, bit in enumerate(order):
        mask = mask + (lax.rem(me // (1 << bit), 2) << (len(order) - 1 - i))
    return mask


def place(device_count, turn):
    me = lax.axis_index("dom")
    orders = stage_bits(device_count)[:2]
    masks = position_mask(me, orders[turn]), position_mask(me, orders[1 - turn])
    return lax.rem(me, 2), masks, 1 << len(orders[0])


def split_pieces(device_count, turn, grads, kept, sent):
    core, masks, pieces = place(device_count, turn)
    mine = jnp.where(core == 0, masks[0], masks[1])
    theirs = jnp.where(core == 0, masks[1], masks[0])
    piece = kept.shape[0] // pieces
    for p in range(pieces):
        at = pl.ds(pl.multiple_of((core * pieces + (mine ^ p)) * piece, 16), piece)
        kept[p * piece : (p + 1) * piece, :] = grads[at, :]
        at = pl.ds(pl.multiple_of(((1 - core) * pieces + (theirs ^ p)) * piece, 16), piece)
        sent[p * piece : (p + 1) * piece, :] = grads[at, :].astype(BF16)


def forward_kernel(
    device_count,
    count,
    src,
    dst,
    feat_in,
    feat_t,
    w_embed,
    b_embed,
    b_hidden,
    w_src,
    w_dst,
    w_out,
    mesh,
    cot,
    hid_sum,
    pgrad,
    latent,
    feat,
    slope,
    bias_sum,
    kept,
    sent,
    w_pad,
    table,
    pair,
    wide,
    wide_t,
    incoming,
    one_hot,
    one_hot_t,
    hid,
    near,
    back,
    node_sum,
    grads,
):
    channels, own = feat_t.shape
    peers, peer_slots, padded = feat_in.shape
    more = peers * peer_slots
    slots = own + more
    blocks, edges = src.shape
    width = w_src.shape[0]
    nodes = mesh.shape[0]
    block = nodes // blocks
    depth = table.shape[0]
    step = 256

    last = padded - 32
    wide[last:padded, :] = jnp.zeros((32, width), F32)
    wide[0:channels, :] = w_embed[...].astype(F32)
    wide[channels : channels + 1, :] = b_embed[...].astype(F32).reshape(1, width)
    w_pad[...] = wide[...].astype(BF16)
    wide_t[last:padded, :] = jnp.zeros((32, own), F32)
    wide_t[0:channels, :] = feat_t[...].astype(F32)
    wide_t[channels : channels + 1, :] = jnp.ones((1, own), F32)
    feat[0:own, :] = jnp.transpose(wide_t[...]).astype(BF16)
    for j in range(peers):
        incoming[j * peer_slots : (j + 1) * peer_slots, :] = feat_in[j].astype(F32)
    feat[own:slots, :] = incoming[...].astype(BF16)
    for r in range(0, slots, step):
        end = min(r + step, slots)
        pre = mm(feat[r:end, :], w_pad[...])
        sig = sigmoid(pre)
        lat = (pre * sig).astype(BF16)
        latent[r:end, :] = lat
        slope[r:end, :] = sig * (1.0 + pre * (1.0 - sig))
        table[block + r : block + end, :] = halved(mm(lat, w_src[...]).astype(BF16))
    near[...] = halved(mm(mesh[...], w_dst[...]).astype(BF16))
    full = 0.5 * mm(cot[...], w_out[...], 1, 1)
    high = full.astype(BF16)
    back[0] = high
    back[1] = (full - high.astype(F32)).astype(BF16)
    tail = depth - slots - block
    tail_row = lax.broadcasted_iota(jnp.int32, (tail, width), 0)
    bias_row = 0.5 * b_hidden[...].astype(F32).reshape(1, width)
    table[slots + block : depth, :] = jnp.where(
        tail_row == 0, jnp.broadcast_to(bias_row, (tail, width)), 0.0
    ).astype(BF16)

    edge_lane = lax.broadcasted_iota(jnp.int32, (blocks, edges), 1)
    block_row = lax.broadcasted_iota(jnp.int32, (blocks, 1), 0)
    counts = jnp.zeros((blocks, 1), jnp.int32)
    for b in range(blocks):
        counts = jnp.where(block_row == b, count[b], counts)
    src_all = src[...]
    dst_all = jnp.where(edge_lane < counts, dst[...], -1)
    columns = jnp.transpose(jnp.concatenate([src_all, dst_all], axis=0))
    bias_total = jnp.zeros((1, width), F32)
    one, none = jnp.ones((), BF16), jnp.zeros((), BF16)

    for b in range(blocks):
        rows = slice(b * block, (b + 1) * block)
        table[0:block, :] = near[rows, :]
        pair[0:block, :] = back[0, rows, :]
        pair[block : 2 * block, :] = back[1, rows, :]
        dst_row = dst_all[b : b + 1, :]
        for e in range(0, edges, step):
            src_col = columns[e : e + step, b : b + 1]
            dst_col = columns[e : e + step, blocks + b : blocks + b + 1]
            src_wide = jnp.broadcast_to(src_col, (step, 128)).astype(jnp.int16)
            dst_wide = jnp.broadcast_to(dst_col, (step, block)).astype(jnp.int16)
            lane = lax.broadcasted_iota(jnp.int16, (step, block), 1)
            near_hot = jnp.where(lane == dst_wide, one, none)
            one_hot[e : e + step, 0:block] = near_hot
            one_hot[e : e + step, block : 2 * block] = near_hot
            for k in range(0, depth - block, 128):
                lane = lax.broadcasted_iota(jnp.int16, (step, 128), 1) + jnp.int16(k)
                hot = lane == src_wide
                if k <= slots < k + 128:
                    hot = hot | (lane == jnp.int16(slots))
                hot = jnp.where(hot, one, none)
                one_hot[e : e + step, 2 * block + k : 2 * block + k + 128] = hot
            pre = mm(one_hot[e : e + step, block : block + depth], table[...])
            grad = mm(one_hot[e : e + step, 0 : 2 * block], pair[...])
            bent = jnp.tanh(pre)
            rise = 1.0 + bent
            act = pre * rise
            hid[e : e + step, :] = act.astype(BF16)
            at = slice(b * edges + e, b * edges + e + step)
            pgrad[at, :] = (grad * (rise + act * (1.0 - bent))).astype(BF16)
        sub = lax.broadcasted_iota(jnp.int32, (block, edges), 0)
        one_hot_t[...] = jnp.where(sub == dst_row, 1.0, 0.0).astype(BF16)
        node = mm(one_hot_t[...], pgrad[b * edges : (b + 1) * edges, :])
        bias_total = bias_total + jnp.sum(node, axis=0, keepdims=True)
        node_sum[rows, :] = node.astype(BF16)
        hid_sum[rows, :] = mm(one_hot_t[...], hid[...]).astype(BF16)

    bias_sum[...] = jnp.broadcast_to(bias_total, bias_sum.shape)
    grads[0:width, :] = mm(hid_sum[...], cot[...], 0, 0)
    grads[width : 2 * width, :] = mm(mesh[...], node_sum[...], 0, 0)
    split_pieces(device_count, 0, grads, kept, sent)


def mesh_kernel(mesh, hid_sum, w_out, mesh_out):
    mesh_out[...] = (mesh[...].astype(F32) + mm(hid_sum[...], w_out[...])).astype(BF16)


def scatter_rows(src, pgrad, one_hot_t, first_block, block_count):
    edges = src.shape[1]
    slots = one_hot_t.shape[0]
    one, none = jnp.ones((), BF16), jnp.zeros((), BF16)
    for b in range(first_block, first_block + block_count):
        at = slice((b - first_block) * edges, (b - first_block + 1) * edges)
        for r in range(0, slots, 128):
            size = min(128, slots - r)
            sub = lax.broadcasted_iota(jnp.int16, (size, edges), 0) + jnp.int16(r)
            row = jnp.broadcast_to(src[b : b + 1, :], (size, edges)).astype(jnp.int16)
            one_hot_t[r : r + size, at] = jnp.where(sub == row, one, none)
    rows = slice(first_block * edges, (first_block + block_count) * edges)
    return mm(one_hot_t[...], pgrad[rows, :])


def scatter_kernel(src, pgrad, slot_sum, one_hot_t):
    slot_sum[...] = scatter_rows(src, pgrad, one_hot_t, 0, src.shape[0] // 2)


def backward_kernel(
    channels,
    device_count,
    src,
    pgrad,
    slot_half,
    latent,
    feat,
    slope,
    w_src,
    bias_sum,
    kept,
    sent,
    one_hot_t,
    grads,
):
    width = w_src.shape[0]
    padded = feat.shape[1]
    half = src.shape[0] // 2
    rest = src.shape[0] - half
    slot_sum = slot_half[...] + scatter_rows(src, pgrad, one_hot_t, half, rest)
    slot_grad = slot_sum.astype(BF16)
    grads[0:width, :] = mm(latent[...], slot_grad, 0, 0)
    buffer_grad = mm(slot_grad, w_src[...], 1, 1)
    embed = (buffer_grad * slope[...]).astype(BF16)
    grads[width : width + padded, :] = mm(feat[...], embed, 0, 0)
    grads[width + channels + 1 : width + channels + 2, :] = bias_sum[0:1, :]
    if grads.shape[0] > width + padded:
        spare = grads.shape[0] - width - padded
        grads[width + padded :, :] = jnp.zeros((spare, width), F32)
    split_pieces(device_count, 1, grads, kept, sent)


def segments(bounds, half_rows):
    found = []
    for half in range(2):
        for index, (low, high) in enumerate(bounds):
            begin, end = max(low, half * half_rows), min(high, (half + 1) * half_rows)
            if begin < end:
                found.append((half, index, begin, end))
    return found


def unpack_kernel(device_count, chains, own_half, *refs):
    count = sum(len(bounds) for _, bounds in chains)
    chain_rows, refs = refs[0 : len(chains)], refs[len(chains) :]
    targets = refs[0:count] if own_half else refs[count : 2 * count]
    buffers, sems = refs[count if own_half else 2 * count : -1], refs[-1]

    def move(half, turn, bounds, rows, base, skip):
        _, masks, pieces = place(device_count, turn)
        parts = segments(bounds, rows.shape[0])
        piece = rows.shape[0] // pieces
        for p in range(pieces):
            begin = half * rows.shape[0] + p * piece
            at = pl.ds(pl.multiple_of((p ^ masks[half]) * piece, 16), piece)
            values = rows[at, :].astype(F32)
            for k, (owner, _, low, high) in enumerate(parts):
                lo, hi = max(low, begin), min(high, begin + piece)
                if owner == half and lo < hi:
                    buffers[skip + k][lo - low : hi - low, :] = values[lo - begin : hi - begin, :]
        copies = []
        for k, (owner, index, low, high) in enumerate(parts):
            if owner == half:
                target = targets[base + index]
                if high - low < target.shape[0]:
                    first = low - bounds[index][0]
                    target = target.at[first : first + high - low, :]
                copies.append(fetch(buffers[skip + k], target, sems, skip + k))
        return copies

    def move_all(half):
        base, skip, copies = 0, 0, []
        for (turn, bounds), rows in zip(chains, chain_rows):
            copies += move(half, turn, bounds, rows, base, skip)
            base += len(bounds)
            skip += len(segments(bounds, rows.shape[0]))
        for copy in copies:
            copy.wait()

    core = lax.rem(lax.axis_index("dom"), 2)
    which = core if own_half else 1 - core
    for half in range(2):
        pl.when(which == half)(functools.partial(move_all, half))


def shards(
    grid_feat,
    mesh_latent,
    cotangent,
    row_pack,
    edge_src,
    edge_dst,
    edge_count,
    w_embed,
    b_embed,
    w_src,
    w_dst,
    b_hidden,
    w_out,
):
    device_count = lax.axis_size("dom")
    own, channels = grid_feat.shape
    width = w_src.shape[0]
    peer_slots = row_pack.shape[0] // device_count
    more = device_count * peer_slots
    slots = own + more
    blocks, edges = edge_src.shape
    nodes = mesh_latent.shape[0]
    block = nodes // blocks
    padded = round_up(channels + 2, 128)
    depth = block + round_up(slots + 16, 128)
    first, second, last_bit = stage_bits(device_count)
    pieces = 1 << len(first)
    mesh_rows = round_up(2 * width, 32 * pieces)
    grid_rows = round_up(width + padded, 32 * pieces)
    half_blocks = blocks // 2
    stages = list(zip(first, second)), list(zip(second, first))

    vmem = pl.BlockSpec(memory_space=pltpu.VMEM)
    smem = pl.BlockSpec(memory_space=pltpu.SMEM)
    hbm = pl.BlockSpec(memory_space=pltpu.HBM)
    shape = jax.ShapeDtypeStruct

    def limit(mib):
        return pltpu.CompilerParams(vmem_limit_bytes=mib * 1024 * 1024)

    feat_t = grid_feat.T
    dma = pltpu.SemaphoreType.DMA
    flag = pl.pallas_call(
        begin_kernel,
        out_shape=shape((8, 128), F32),
        out_specs=vmem,
        compiler_params=limit(1),
        cost_estimate=pl.CostEstimate(
            flops=20_000_000_000, bytes_accessed=own * padded * 2, transcendentals=0
        ),
        name="begin",
    )()
    send = pl.pallas_call(
        pick_kernel,
        out_shape=shape((device_count, peer_slots, padded), BF16),
        in_specs=[vmem] * 3,
        out_specs=vmem,
        compiler_params=limit(16),
        cost_estimate=pl.CostEstimate(
            flops=20_000_000_000, bytes_accessed=own * padded * 2, transcendentals=0
        ),
        name="pick_rows",
    )(flag, row_pack[None, :], feat_t)
    feat_in = lax.all_to_all(send, "dom", split_axis=0, concat_axis=0, tiled=True)

    forward_macs = (
        slots * width * (padded + width)
        + blocks * edges * width * (depth + 4 * block)
        + 5 * nodes * width * width
    )
    hid_sum, pgrad, latent, feat, slope, bias_sum, kept_mesh, sent_mesh = pl.pallas_call(
        functools.partial(forward_kernel, device_count),
        out_shape=(
            shape((nodes, width), BF16),
            shape((blocks * edges, width), BF16),
            shape((slots, width), BF16),
            shape((slots, padded), BF16),
            shape((slots, width), F32),
            shape((8, width), F32),
            shape((mesh_rows // 2, width), F32),
            shape((mesh_rows // 2, width), BF16),
        ),
        in_specs=[smem] + [vmem] * 12,
        out_specs=(vmem,) * 8,
        scratch_shapes=[
            pltpu.VMEM((padded, width), BF16),
            pltpu.VMEM((depth, width), BF16),
            pltpu.VMEM((2 * block, width), BF16),
            pltpu.VMEM((padded, width), F32),
            pltpu.VMEM((padded, own), F32),
            pltpu.VMEM((more, padded), F32),
            pltpu.VMEM((edges, depth + block), BF16),
            pltpu.VMEM((block, edges), BF16),
            pltpu.VMEM((edges, width), BF16),
            pltpu.VMEM((nodes, width), BF16),
            pltpu.VMEM((2, nodes, width), BF16),
            pltpu.VMEM((nodes, width), BF16),
            pltpu.VMEM((mesh_rows, width), F32),
        ],
        compiler_params=limit(40),
        cost_estimate=pl.CostEstimate(
            flops=2 * forward_macs,
            bytes_accessed=16 * own * width,
            transcendentals=blocks * edges * width,
        ),
        name="forward_rows",
    )(
        edge_count,
        edge_src,
        edge_dst,
        feat_in,
        feat_t,
        w_embed,
        b_embed,
        b_hidden,
        w_src,
        w_dst,
        w_out,
        mesh_latent,
        cotangent,
    )

    def swap(values, bits):
        return lax.ppermute(
            values, "dom", [(d, d ^ (1 << bits[d % 2])) for d in range(device_count)]
        )

    def cut(held):
        middle = held.shape[0] // 2
        return held[:middle], held[middle:].astype(BF16)

    def pair_sum(kept, sent):
        return cut(kept + swap(sent, (0, 0)).astype(F32))

    def reduce_pieces(turn, held, got, done=1):
        for bits in stages[turn][done:]:
            held, sent = cut(held + got.astype(F32))
            got = swap(sent, bits)
        held = (held + got.astype(F32)).astype(BF16)
        got = swap(held, (last_bit, last_bit))
        held = (held.astype(F32) + got.astype(F32)).astype(BF16)
        for bits in reversed(stages[turn]):
            held = jnp.concatenate([held, swap(held, bits)], axis=0)
        return held, swap(held, (0, 0))

    held_mesh, next_mesh = pair_sum(kept_mesh, sent_mesh)
    slot_half = pl.pallas_call(
        scatter_kernel,
        out_shape=shape((slots, width), F32),
        in_specs=[vmem] * 2,
        out_specs=vmem,
        scratch_shapes=[pltpu.VMEM((slots, half_blocks * edges), BF16)],
        compiler_params=limit(24),
        cost_estimate=pl.CostEstimate(
            flops=2 * half_blocks * edges * slots * width,
            bytes_accessed=half_blocks * edges * width * 2,
            transcendentals=0,
        ),
        name="scatter_rows",
    )(edge_src, pgrad)

    slot_half, held_mesh, next_mesh = lax.optimization_barrier((slot_half, held_mesh, next_mesh))
    got_mesh = swap(next_mesh, stages[0][0])
    kept_grid, sent_grid = pl.pallas_call(
        functools.partial(backward_kernel, channels, device_count),
        out_shape=(
            shape((grid_rows // 2, width), F32),
            shape((grid_rows // 2, width), BF16),
        ),
        in_specs=[vmem] * 8,
        out_specs=(vmem,) * 2,
        scratch_shapes=[
            pltpu.VMEM((slots, (blocks - half_blocks) * edges), BF16),
            pltpu.VMEM((grid_rows, width), F32),
        ],
        compiler_params=limit(40),
        cost_estimate=pl.CostEstimate(
            flops=2 * slots * width * (half_blocks * edges + 2 * width + 2 * padded),
            bytes_accessed=half_blocks * edges * width * 2,
            transcendentals=slots * width,
        ),
        name="backward_rows",
    )(edge_src, pgrad, slot_half, latent, feat, slope, w_src, bias_sum)


    mesh_out = pl.pallas_call(
        mesh_kernel,
        out_shape=shape((nodes, width), BF16),
        in_specs=[vmem] * 3,
        out_specs=vmem,
        compiler_params=limit(16),
        cost_estimate=pl.CostEstimate(
            flops=2 * nodes * width * width, bytes_accessed=8 * nodes * width, transcendentals=0
        ),
        name="mesh_rows",
    )(mesh_latent, hid_sum, w_out)

    def unpack(chains, pairs):
        sizes = [high - low for _, bounds in chains for low, high in bounds]
        parts = [
            high - low
            for (_, bounds), (rows, _) in zip(chains, pairs)
            for _, _, low, high in segments(bounds, rows.shape[0])
        ]
        targets = ()
        for own_half, chain_rows in zip((True, False), zip(*pairs)):
            targets = pl.pallas_call(
                functools.partial(unpack_kernel, device_count, chains, own_half),
                out_shape=tuple(shape((size, width), F32) for size in sizes),
                in_specs=[vmem] * len(chains) + [hbm] * len(targets),
                out_specs=(hbm,) * len(sizes),
                scratch_shapes=[pltpu.VMEM((size, width), F32) for size in parts]
                + [dma((len(parts),))],
                input_output_aliases={len(chains) + k: k for k in range(len(targets))},
                compiler_params=limit(12),
                name="unpack_rows",
            )(*chain_rows, *targets)
        return targets

    mesh_out, got_mesh = lax.optimization_barrier((mesh_out, got_mesh))
    held_mesh, next_mesh = cut(held_mesh + got_mesh.astype(F32))
    held_grid, next_grid = pair_sum(kept_grid, sent_grid)
    next_grid, next_mesh = lax.optimization_barrier((next_grid, next_mesh))
    got_mesh = swap(next_mesh, stages[0][1])
    mesh_pair = reduce_pieces(0, held_mesh, got_mesh, 2)
    grid_pair = reduce_pieces(1, held_grid, swap(next_grid, stages[1][0]))
    end = width + channels
    mesh_bounds = ((0, width), (width, 2 * width))
    grid_bounds = ((0, width), (width, end), (end, end + 2))
    grad_out, grad_dst, grad_src, grad_embed, biases = unpack(
        ((0, mesh_bounds), (1, grid_bounds)), (mesh_pair, grid_pair)
    )
    return mesh_out, grad_embed, grad_src, grad_dst, grad_out, biases


def solution(mesh):
    return jax.shard_map(
        shards,
        mesh=mesh,
        in_specs=(
            P(("ens", "dom"), None),
            P(("ens", "dom"), None),
            P(("ens", "dom"), None),
            P("dom"),
            P("dom", None),
            P("dom", None),
            P("dom"),
            P(),
            P(),
            P(),
            P(),
            P(),
            P(),
        ),
        out_specs=(
            P(("ens", "dom"), None),
            P("ens", None),
            P("ens", None),
            P("ens", None),
            P("ens", None),
            P("ens", None),
        ),
        check_vma=False,
    )
```

```python
import functools

import jax
import jax.numpy as jnp
from jax import lax
from jax.experimental import pallas as pl
from jax.experimental.pallas import tpu as pltpu
from jax.sharding import PartitionSpec as P

BF16 = jnp.bfloat16
F32 = jnp.float32


def mm(left, right, left_dim=1, right_dim=0):
    return lax.dot_general(
        left, right, (((left_dim,), (right_dim,)), ((), ())), preferred_element_type=F32
    )


def sigmoid(values):
    return 0.5 * jnp.tanh(0.5 * values) + 0.5


def halved(values):
    return (0.5 * values.astype(F32)).astype(BF16)


def round_up(value, step):
    return -(-value // step) * step


def fetch(source, target, sems, index):
    copy = pltpu.make_async_copy(source, target, sems.at[index])
    copy.start()
    return copy


def begin_kernel(flag):
    flag[...] = jnp.zeros_like(flag)


def pick_kernel(flag, row_pack, feat_t, send):
    channels, own = feat_t.shape
    peers, peer_slots, padded = send.shape
    row = lax.broadcasted_iota(jnp.int32, (own, peers * peer_slots), 0)
    pick = jnp.where(row == row_pack[...], 1.0, 0.0).astype(BF16)
    last = padded - 128
    lane = lax.broadcasted_iota(jnp.int32, (peers * peer_slots, 128), 1) + last
    ones = jnp.where(lane == channels, 1.0, 0.0).astype(BF16)
    rows = mm(pick, feat_t[...], 0, 1)
    for j in range(peers):
        part = slice(j * peer_slots, (j + 1) * peer_slots)
        send[j, :, last:padded] = ones[part, :]
        send[j, :, 0:channels] = rows[part, :].astype(BF16)


def stage_bits(device_count):
    bits = device_count.bit_length() - 1
    first = list(range(1, bits - 1))
    second = first[1::-1] + first[2:]
    return first, second, bits - 1


def position_mask(me, order):
    mask = 0
    for i, bit in enumerate(order):
        mask = mask + (lax.rem(me // (1 << bit), 2) << (len(order) - 1 - i))
    return mask


def place(device_count, turn):
    me = lax.axis_index("dom")
    orders = stage_bits(device_count)[:2]
    masks = position_mask(me, orders[turn]), position_mask(me, orders[1 - turn])
    return lax.rem(me, 2), masks, 1 << len(orders[0])


def split_pieces(device_count, turn, grads, kept, sent):
    core, masks, pieces = place(device_count, turn)
    mine = jnp.where(core == 0, masks[0], masks[1])
    theirs = jnp.where(core == 0, masks[1], masks[0])
    piece = kept.shape[0] // pieces
    for p in range(pieces):
        at = pl.ds(pl.multiple_of((core * pieces + (mine ^ p)) * piece, 16), piece)
        kept[p * piece : (p + 1) * piece, :] = grads[at, :]
        at = pl.ds(pl.multiple_of(((1 - core) * pieces + (theirs ^ p)) * piece, 16), piece)
        sent[p * piece : (p + 1) * piece, :] = grads[at, :].astype(BF16)


def forward_kernel(
    device_count,
    count,
    src,
    dst,
    feat_in,
    feat_t,
    w_embed,
    b_embed,
    b_hidden,
    w_src,
    w_dst,
    w_out,
    mesh,
    cot,
    hid_sum,
    pgrad,
    latent,
    feat,
    slope,
    bias_sum,
    kept,
    sent,
    w_pad,
    table,
    pair,
    wide,
    incoming,
    one_hot,
    one_hot_t,
    hid,
    near,
    back,
    node_sum,
    grads,
):
    channels, own = feat_t.shape
    peers, peer_slots, padded = feat_in.shape
    more = peers * peer_slots
    slots = own + more
    blocks, edges = src.shape
    width = w_src.shape[0]
    nodes = mesh.shape[0]
    block = nodes // blocks
    depth = table.shape[0]
    step = 512

    last = padded - 32
    wide[last:padded, :] = jnp.zeros((32, width), F32)
    wide[0:channels, :] = w_embed[...].astype(F32)
    wide[channels : channels + 1, :] = b_embed[...].astype(F32).reshape(1, width)
    w_pad[...] = wide[...].astype(BF16)
    lane = lax.broadcasted_iota(jnp.int32, (own, 128), 1) + (padded - 128)
    feat[0:own, padded - 128 : padded] = jnp.where(lane == channels, 1.0, 0.0).astype(BF16)
    feat[0:own, 0:channels] = jnp.transpose(feat_t[...])
    for j in range(peers):
        incoming[j * peer_slots : (j + 1) * peer_slots, :] = feat_in[j].astype(F32)
    feat[own:slots, :] = incoming[...].astype(BF16)
    for r in range(0, slots, step):
        end = min(r + step, slots)
        pre = mm(feat[r:end, :], w_pad[...])
        sig = sigmoid(pre)
        lat = (pre * sig).astype(BF16)
        latent[r:end, :] = lat
        slope[r:end, :] = sig * (1.0 + pre * (1.0 - sig))
        table[block + r : block + end, :] = halved(mm(lat, w_src[...]).astype(BF16))
    near[...] = halved(mm(mesh[...], w_dst[...]).astype(BF16))
    full = 0.5 * mm(cot[...], w_out[...], 1, 1)
    high = full.astype(BF16)
    back[0] = high
    back[1] = (full - high.astype(F32)).astype(BF16)
    tail = depth - slots - block
    tail_row = lax.broadcasted_iota(jnp.int32, (tail, width), 0)
    bias_row = 0.5 * b_hidden[...].astype(F32).reshape(1, width)
    table[slots + block : depth, :] = jnp.where(
        tail_row == 0, jnp.broadcast_to(bias_row, (tail, width)), 0.0
    ).astype(BF16)

    edge_lane = lax.broadcasted_iota(jnp.int32, (blocks, edges), 1)
    block_row = lax.broadcasted_iota(jnp.int32, (blocks, 1), 0)
    counts = jnp.zeros((blocks, 1), jnp.int32)
    for b in range(blocks):
        counts = jnp.where(block_row == b, count[b], counts)
    src_all = src[...]
    dst_all = jnp.where(edge_lane < counts, dst[...], -1)
    columns = jnp.transpose(jnp.concatenate([src_all, dst_all], axis=0))
    bias_total = jnp.zeros((1, width), F32)
    one, none = jnp.ones((), BF16), jnp.zeros((), BF16)

    for b in range(blocks):
        rows = slice(b * block, (b + 1) * block)
        table[0:block, :] = near[rows, :]
        pair[0:block, :] = back[0, rows, :]
        pair[block : 2 * block, :] = back[1, rows, :]
        dst_row = dst_all[b : b + 1, :]
        for e in range(0, edges, step):
            src_col = columns[e : e + step, b : b + 1]
            dst_col = columns[e : e + step, blocks + b : blocks + b + 1]
            src_wide = jnp.broadcast_to(src_col, (step, 128)).astype(jnp.int16)
            dst_wide = jnp.broadcast_to(dst_col, (step, block)).astype(jnp.int16)
            lane = lax.broadcasted_iota(jnp.int16, (step, block), 1)
            near_hot = jnp.where(lane == dst_wide, one, none)
            one_hot[e : e + step, 0:block] = near_hot
            one_hot[e : e + step, block : 2 * block] = near_hot
            for k in range(0, depth - block, 128):
                lane = lax.broadcasted_iota(jnp.int16, (step, 128), 1) + jnp.int16(k)
                hot = lane == src_wide
                if k <= slots < k + 128:
                    hot = hot | (lane == jnp.int16(slots))
                hot = jnp.where(hot, one, none)
                one_hot[e : e + step, 2 * block + k : 2 * block + k + 128] = hot
            pre = mm(one_hot[e : e + step, block : block + depth], table[...])
            grad = mm(one_hot[e : e + step, 0 : 2 * block], pair[...])
            bent = jnp.tanh(pre)
            rise = 1.0 + bent
            act = pre * rise
            hid[e : e + step, :] = act.astype(BF16)
            at = slice(b * edges + e, b * edges + e + step)
            pgrad[at, :] = (grad * (rise + act * (1.0 - bent))).astype(BF16)
        sub = lax.broadcasted_iota(jnp.int32, (block, edges), 0)
        one_hot_t[...] = jnp.where(sub == dst_row, 1.0, 0.0).astype(BF16)
        node = mm(one_hot_t[...], pgrad[b * edges : (b + 1) * edges, :])
        bias_total = bias_total + jnp.sum(node, axis=0, keepdims=True)
        node_sum[rows, :] = node.astype(BF16)
        hid_sum[rows, :] = mm(one_hot_t[...], hid[...]).astype(BF16)

    bias_sum[...] = jnp.broadcast_to(bias_total, bias_sum.shape)
    grads[0:width, :] = mm(hid_sum[...], cot[...], 0, 0)
    grads[width : 2 * width, :] = mm(mesh[...], node_sum[...], 0, 0)
    split_pieces(device_count, 0, grads, kept, sent)


def mesh_kernel(mesh, hid_sum, w_out, mesh_out):
    mesh_out[...] = (mesh[...].astype(F32) + mm(hid_sum[...], w_out[...])).astype(BF16)


def scatter_rows(src, pgrad, one_hot_t, first_block, block_count):
    edges = src.shape[1]
    slots = one_hot_t.shape[0]
    one, none = jnp.ones((), BF16), jnp.zeros((), BF16)
    for b in range(first_block, first_block + block_count):
        at = slice((b - first_block) * edges, (b - first_block + 1) * edges)
        for r in range(0, slots, 128):
            size = min(128, slots - r)
            sub = lax.broadcasted_iota(jnp.int16, (size, edges), 0) + jnp.int16(r)
            row = jnp.broadcast_to(src[b : b + 1, :], (size, edges)).astype(jnp.int16)
            one_hot_t[r : r + size, at] = jnp.where(sub == row, one, none)
    rows = slice(first_block * edges, (first_block + block_count) * edges)
    return mm(one_hot_t[...], pgrad[rows, :])


def scatter_kernel(src, pgrad, slot_sum, one_hot_t):
    slot_sum[...] = scatter_rows(src, pgrad, one_hot_t, 0, src.shape[0] // 2)


def backward_kernel(
    channels,
    device_count,
    src,
    pgrad,
    slot_half,
    latent,
    feat,
    slope,
    w_src,
    bias_sum,
    kept,
    sent,
    one_hot_t,
    grads,
):
    width = w_src.shape[0]
    padded = feat.shape[1]
    half = src.shape[0] // 2
    rest = src.shape[0] - half
    slot_sum = slot_half[...] + scatter_rows(src, pgrad, one_hot_t, half, rest)
    slot_grad = slot_sum.astype(BF16)
    grads[0:width, :] = mm(latent[...], slot_grad, 0, 0)
    buffer_grad = mm(slot_grad, w_src[...], 1, 1)
    embed = (buffer_grad * slope[...]).astype(BF16)
    grads[width : width + padded, :] = mm(feat[...], embed, 0, 0)
    grads[width + channels + 1 : width + channels + 2, :] = bias_sum[0:1, :]
    if grads.shape[0] > width + padded:
        spare = grads.shape[0] - width - padded
        grads[width + padded :, :] = jnp.zeros((spare, width), F32)
    split_pieces(device_count, 1, grads, kept, sent)


def segments(bounds, half_rows):
    found = []
    for half in range(2):
        for index, (low, high) in enumerate(bounds):
            begin, end = max(low, half * half_rows), min(high, (half + 1) * half_rows)
            if begin < end:
                found.append((half, index, begin, end))
    return found


def unpack_kernel(device_count, chains, own_half, *refs):
    count = sum(len(bounds) for _, bounds in chains)
    chain_rows, refs = refs[0 : len(chains)], refs[len(chains) :]
    targets = refs[0:count] if own_half else refs[count : 2 * count]
    buffers, sems = refs[count if own_half else 2 * count : -1], refs[-1]

    def move(half, turn, bounds, rows, base, skip):
        _, masks, pieces = place(device_count, turn)
        parts = segments(bounds, rows.shape[0])
        piece = rows.shape[0] // pieces
        for p in range(pieces):
            begin = half * rows.shape[0] + p * piece
            at = pl.ds(pl.multiple_of((p ^ masks[half]) * piece, 16), piece)
            values = rows[at, :].astype(F32)
            for k, (owner, _, low, high) in enumerate(parts):
                lo, hi = max(low, begin), min(high, begin + piece)
                if owner == half and lo < hi:
                    buffers[skip + k][lo - low : hi - low, :] = values[lo - begin : hi - begin, :]
        copies = []
        for k, (owner, index, low, high) in enumerate(parts):
            if owner == half:
                target = targets[base + index]
                if high - low < target.shape[0]:
                    first = low - bounds[index][0]
                    target = target.at[first : first + high - low, :]
                copies.append(fetch(buffers[skip + k], target, sems, skip + k))
        return copies

    def move_all(half):
        base, skip, copies = 0, 0, []
        for (turn, bounds), rows in zip(chains, chain_rows):
            copies += move(half, turn, bounds, rows, base, skip)
            base += len(bounds)
            skip += len(segments(bounds, rows.shape[0]))
        for copy in copies:
            copy.wait()

    core = lax.rem(lax.axis_index("dom"), 2)
    which = core if own_half else 1 - core
    for half in range(2):
        pl.when(which == half)(functools.partial(move_all, half))


def shards(
    grid_feat,
    mesh_latent,
    cotangent,
    row_pack,
    edge_src,
    edge_dst,
    edge_count,
    w_embed,
    b_embed,
    w_src,
    w_dst,
    b_hidden,
    w_out,
):
    device_count = lax.axis_size("dom")
    own, channels = grid_feat.shape
    width = w_src.shape[0]
    peer_slots = row_pack.shape[0] // device_count
    more = device_count * peer_slots
    slots = own + more
    blocks, edges = edge_src.shape
    nodes = mesh_latent.shape[0]
    block = nodes // blocks
    padded = round_up(channels + 2, 128)
    depth = block + round_up(slots + 16, 128)
    first, second, last_bit = stage_bits(device_count)
    pieces = 1 << len(first)
    mesh_rows = round_up(2 * width, 32 * pieces)
    grid_rows = round_up(width + padded, 32 * pieces)
    half_blocks = blocks // 2
    stages = list(zip(first, second)), list(zip(second, first))

    vmem = pl.BlockSpec(memory_space=pltpu.VMEM)
    smem = pl.BlockSpec(memory_space=pltpu.SMEM)
    hbm = pl.BlockSpec(memory_space=pltpu.HBM)
    shape = jax.ShapeDtypeStruct

    def limit(mib):
        return pltpu.CompilerParams(vmem_limit_bytes=mib * 1024 * 1024)

    feat_t = grid_feat.T
    dma = pltpu.SemaphoreType.DMA
    flag = pl.pallas_call(
        begin_kernel,
        out_shape=shape((8, 128), F32),
        out_specs=vmem,
        compiler_params=limit(1),
        cost_estimate=pl.CostEstimate(
            flops=20_000_000_000, bytes_accessed=own * padded * 2, transcendentals=0
        ),
        name="begin",
    )()
    send = pl.pallas_call(
        pick_kernel,
        out_shape=shape((device_count, peer_slots, padded), BF16),
        in_specs=[vmem] * 3,
        out_specs=vmem,
        compiler_params=limit(16),
        cost_estimate=pl.CostEstimate(
            flops=20_000_000_000, bytes_accessed=own * padded * 2, transcendentals=0
        ),
        name="pick_rows",
    )(flag, row_pack[None, :], feat_t)
    feat_in = lax.all_to_all(send, "dom", split_axis=0, concat_axis=0, tiled=True)

    forward_macs = (
        slots * width * (padded + width)
        + blocks * edges * width * (depth + 4 * block)
        + 5 * nodes * width * width
    )
    hid_sum, pgrad, latent, feat, slope, bias_sum, kept_mesh, sent_mesh = pl.pallas_call(
        functools.partial(forward_kernel, device_count),
        out_shape=(
            shape((nodes, width), BF16),
            shape((blocks * edges, width), BF16),
            shape((slots, width), BF16),
            shape((slots, padded), BF16),
            shape((slots, width), F32),
            shape((8, width), F32),
            shape((mesh_rows // 2, width), F32),
            shape((mesh_rows // 2, width), BF16),
        ),
        in_specs=[smem] + [vmem] * 12,
        out_specs=(vmem,) * 8,
        scratch_shapes=[
            pltpu.VMEM((padded, width), BF16),
            pltpu.VMEM((depth, width), BF16),
            pltpu.VMEM((2 * block, width), BF16),
            pltpu.VMEM((padded, width), F32),
            pltpu.VMEM((more, padded), F32),
            pltpu.VMEM((edges, depth + block), BF16),
            pltpu.VMEM((block, edges), BF16),
            pltpu.VMEM((edges, width), BF16),
            pltpu.VMEM((nodes, width), BF16),
            pltpu.VMEM((2, nodes, width), BF16),
            pltpu.VMEM((nodes, width), BF16),
            pltpu.VMEM((mesh_rows, width), F32),
        ],
        compiler_params=limit(40),
        cost_estimate=pl.CostEstimate(
            flops=2 * forward_macs,
            bytes_accessed=16 * own * width,
            transcendentals=blocks * edges * width,
        ),
        name="forward_rows",
    )(
        edge_count,
        edge_src,
        edge_dst,
        feat_in,
        feat_t,
        w_embed,
        b_embed,
        b_hidden,
        w_src,
        w_dst,
        w_out,
        mesh_latent,
        cotangent,
    )

    def swap(values, bits):
        return lax.ppermute(
            values, "dom", [(d, d ^ (1 << bits[d % 2])) for d in range(device_count)]
        )

    def cut(held):
        middle = held.shape[0] // 2
        return held[:middle], held[middle:].astype(BF16)

    def pair_sum(kept, sent):
        return cut(kept + swap(sent, (0, 0)).astype(F32))

    def reduce_pieces(turn, held, got, done=1):
        for bits in stages[turn][done:]:
            held, sent = cut(held + got.astype(F32))
            got = swap(sent, bits)
        held = (held + got.astype(F32)).astype(BF16)
        got = swap(held, (last_bit, last_bit))
        held = (held.astype(F32) + got.astype(F32)).astype(BF16)
        for bits in reversed(stages[turn]):
            held = jnp.concatenate([held, swap(held, bits)], axis=0)
        return held, swap(held, (0, 0))

    held_mesh, next_mesh = pair_sum(kept_mesh, sent_mesh)
    slot_half = pl.pallas_call(
        scatter_kernel,
        out_shape=shape((slots, width), F32),
        in_specs=[vmem] * 2,
        out_specs=vmem,
        scratch_shapes=[pltpu.VMEM((slots, half_blocks * edges), BF16)],
        compiler_params=limit(24),
        cost_estimate=pl.CostEstimate(
            flops=2 * half_blocks * edges * slots * width,
            bytes_accessed=half_blocks * edges * width * 2,
            transcendentals=0,
        ),
        name="scatter_rows",
    )(edge_src, pgrad)

    slot_half, held_mesh, next_mesh = lax.optimization_barrier((slot_half, held_mesh, next_mesh))
    got_mesh = swap(next_mesh, stages[0][0])
    kept_grid, sent_grid = pl.pallas_call(
        functools.partial(backward_kernel, channels, device_count),
        out_shape=(
            shape((grid_rows // 2, width), F32),
            shape((grid_rows // 2, width), BF16),
        ),
        in_specs=[vmem] * 8,
        out_specs=(vmem,) * 2,
        scratch_shapes=[
            pltpu.VMEM((slots, (blocks - half_blocks) * edges), BF16),
            pltpu.VMEM((grid_rows, width), F32),
        ],
        compiler_params=limit(40),
        cost_estimate=pl.CostEstimate(
            flops=2 * slots * width * (half_blocks * edges + 2 * width + 2 * padded),
            bytes_accessed=half_blocks * edges * width * 2,
            transcendentals=slots * width,
        ),
        name="backward_rows",
    )(edge_src, pgrad, slot_half, latent, feat, slope, w_src, bias_sum)


    mesh_out = pl.pallas_call(
        mesh_kernel,
        out_shape=shape((nodes, width), BF16),
        in_specs=[vmem] * 3,
        out_specs=vmem,
        compiler_params=limit(16),
        cost_estimate=pl.CostEstimate(
            flops=2 * nodes * width * width, bytes_accessed=8 * nodes * width, transcendentals=0
        ),
        name="mesh_rows",
    )(mesh_latent, hid_sum, w_out)

    def unpack(chains, pairs):
        sizes = [high - low for _, bounds in chains for low, high in bounds]
        parts = [
            high - low
            for (_, bounds), (rows, _) in zip(chains, pairs)
            for _, _, low, high in segments(bounds, rows.shape[0])
        ]
        targets = ()
        for own_half, chain_rows in zip((True, False), zip(*pairs)):
            targets = pl.pallas_call(
                functools.partial(unpack_kernel, device_count, chains, own_half),
                out_shape=tuple(shape((size, width), F32) for size in sizes),
                in_specs=[vmem] * len(chains) + [hbm] * len(targets),
                out_specs=(hbm,) * len(sizes),
                scratch_shapes=[pltpu.VMEM((size, width), F32) for size in parts]
                + [dma((len(parts),))],
                input_output_aliases={len(chains) + k: k for k in range(len(targets))},
                compiler_params=limit(12),
                name="unpack_rows",
            )(*chain_rows, *targets)
        return targets

    mesh_out, got_mesh = lax.optimization_barrier((mesh_out, got_mesh))
    held_mesh, next_mesh = cut(held_mesh + got_mesh.astype(F32))
    held_grid, next_grid = pair_sum(kept_grid, sent_grid)
    next_grid, next_mesh = lax.optimization_barrier((next_grid, next_mesh))
    got_mesh = swap(next_mesh, stages[0][1])
    mesh_pair = reduce_pieces(0, held_mesh, got_mesh, 2)
    grid_pair = reduce_pieces(1, held_grid, swap(next_grid, stages[1][0]))
    end = width + channels
    mesh_bounds = ((0, width), (width, 2 * width))
    grid_bounds = ((0, width), (width, end), (end, end + 2))
    grad_out, grad_dst, grad_src, grad_embed, biases = unpack(
        ((0, mesh_bounds), (1, grid_bounds)), (mesh_pair, grid_pair)
    )
    return mesh_out, grad_embed, grad_src, grad_dst, grad_out, biases


def solution(mesh):
    return jax.shard_map(
        shards,
        mesh=mesh,
        in_specs=(
            P(("ens", "dom"), None),
            P(("ens", "dom"), None),
            P(("ens", "dom"), None),
            P("dom"),
            P("dom", None),
            P("dom", None),
            P("dom"),
            P(),
            P(),
            P(),
            P(),
            P(),
            P(),
        ),
        out_specs=(
            P(("ens", "dom"), None),
            P("ens", None),
            P("ens", None),
            P("ens", None),
            P("ens", None),
            P("ens", None),
        ),
        check_vma=False,
    )
```

```python
import functools

import jax
import jax.numpy as jnp
from jax import lax
from jax.experimental import pallas as pl
from jax.experimental.pallas import tpu as pltpu
from jax.sharding import PartitionSpec as P

BF16 = jnp.bfloat16
F32 = jnp.float32


def mm(left, right, left_dim=1, right_dim=0):
    return lax.dot_general(
        left, right, (((left_dim,), (right_dim,)), ((), ())), preferred_element_type=F32
    )


def sigmoid(values):
    return 0.5 * jnp.tanh(0.5 * values) + 0.5


def halved(values):
    return (0.5 * values.astype(F32)).astype(BF16)


def round_up(value, step):
    return -(-value // step) * step


def fetch(source, target, sems, index):
    copy = pltpu.make_async_copy(source, target, sems.at[index])
    copy.start()
    return copy


def begin_kernel(flag):
    flag[...] = jnp.zeros_like(flag)


def pick_kernel(flag, row_pack, feat_t, send):
    channels, own = feat_t.shape
    peers, peer_slots, padded = send.shape
    row = lax.broadcasted_iota(jnp.int32, (own, peers * peer_slots), 0)
    pick = jnp.where(row == row_pack[...], 1.0, 0.0).astype(BF16)
    last = padded - 128
    lane = lax.broadcasted_iota(jnp.int32, (peers * peer_slots, 128), 1) + last
    ones = jnp.where(lane == channels, 1.0, 0.0).astype(BF16)
    rows = mm(pick, feat_t[...], 0, 1)
    for j in range(peers):
        part = slice(j * peer_slots, (j + 1) * peer_slots)
        send[j, :, last:padded] = ones[part, :]
        send[j, :, 0:channels] = rows[part, :].astype(BF16)


def stage_bits(device_count):
    bits = device_count.bit_length() - 1
    first = list(range(1, bits - 1))
    second = first[1::-1] + first[2:]
    return first, second, bits - 1


def position_mask(me, order):
    mask = 0
    for i, bit in enumerate(order):
        mask = mask + (lax.rem(me // (1 << bit), 2) << (len(order) - 1 - i))
    return mask


def place(device_count, turn):
    me = lax.axis_index("dom")
    orders = stage_bits(device_count)[:2]
    masks = position_mask(me, orders[turn]), position_mask(me, orders[1 - turn])
    return lax.rem(me, 2), masks, 1 << len(orders[0])


def split_pieces(device_count, turn, grads, kept, sent):
    core, masks, pieces = place(device_count, turn)
    mine = jnp.where(core == 0, masks[0], masks[1])
    theirs = jnp.where(core == 0, masks[1], masks[0])
    piece = kept.shape[0] // pieces
    for p in range(pieces):
        at = pl.ds(pl.multiple_of((core * pieces + (mine ^ p)) * piece, 16), piece)
        kept[p * piece : (p + 1) * piece, :] = grads[at, :]
        at = pl.ds(pl.multiple_of(((1 - core) * pieces + (theirs ^ p)) * piece, 16), piece)
        sent[p * piece : (p + 1) * piece, :] = grads[at, :].astype(BF16)


def forward_kernel(
    device_count,
    count,
    src,
    dst,
    feat_in,
    feat_t,
    w_embed,
    b_embed,
    b_hidden,
    w_src,
    w_dst,
    w_out,
    mesh,
    cot,
    hid_sum,
    pgrad,
    latent,
    feat,
    slope,
    bias_sum,
    kept,
    sent,
    w_pad,
    table,
    pair,
    wide,
    incoming,
    one_hot,
    one_hot_t,
    hid,
    near,
    back,
    node_sum,
    grads,
):
    channels, own = feat_t.shape
    peers, peer_slots, padded = feat_in.shape
    more = peers * peer_slots
    slots = own + more
    blocks, edges = src.shape
    width = w_src.shape[0]
    nodes = mesh.shape[0]
    block = nodes // blocks
    depth = table.shape[0]
    step = 512

    last = padded - 32
    wide[last:padded, :] = jnp.zeros((32, width), F32)
    wide[0:channels, :] = w_embed[...].astype(F32)
    wide[channels : channels + 1, :] = b_embed[...].astype(F32).reshape(1, width)
    w_pad[...] = wide[...].astype(BF16)
    lane = lax.broadcasted_iota(jnp.int32, (own, 128), 1) + (padded - 128)
    feat[0:own, padded - 128 : padded] = jnp.where(lane == channels, 1.0, 0.0).astype(BF16)
    feat[0:own, 0:channels] = jnp.transpose(feat_t[...])
    for j in range(peers):
        incoming[j * peer_slots : (j + 1) * peer_slots, :] = feat_in[j].astype(F32)
    feat[own:slots, :] = incoming[...].astype(BF16)
    for r in range(0, slots, step):
        end = min(r + step, slots)
        pre = mm(feat[r:end, :], w_pad[...])
        sig = sigmoid(pre)
        lat = (pre * sig).astype(BF16)
        latent[:, r:end] = jnp.transpose(lat)
        slope[r:end, :] = sig * (1.0 + pre * (1.0 - sig))
        table[block + r : block + end, :] = halved(mm(lat, w_src[...]).astype(BF16))
    near[...] = halved(mm(mesh[...], w_dst[...]).astype(BF16))
    full = 0.5 * mm(cot[...], w_out[...], 1, 1)
    high = full.astype(BF16)
    back[0] = high
    back[1] = (full - high.astype(F32)).astype(BF16)
    tail = depth - slots - block
    tail_row = lax.broadcasted_iota(jnp.int32, (tail, width), 0)
    bias_row = 0.5 * b_hidden[...].astype(F32).reshape(1, width)
    table[slots + block : depth, :] = jnp.where(
        tail_row == 0, jnp.broadcast_to(bias_row, (tail, width)), 0.0
    ).astype(BF16)

    edge_lane = lax.broadcasted_iota(jnp.int32, (blocks, edges), 1)
    block_row = lax.broadcasted_iota(jnp.int32, (blocks, 1), 0)
    counts = jnp.zeros((blocks, 1), jnp.int32)
    for b in range(blocks):
        counts = jnp.where(block_row == b, count[b], counts)
    src_all = src[...]
    dst_all = jnp.where(edge_lane < counts, dst[...], -1)
    columns = jnp.transpose(jnp.concatenate([src_all, dst_all], axis=0))
    bias_total = jnp.zeros((1, width), F32)
    one, none = jnp.ones((), BF16), jnp.zeros((), BF16)

    for b in range(blocks):
        rows = slice(b * block, (b + 1) * block)
        table[0:block, :] = near[rows, :]
        pair[0:block, :] = back[0, rows, :]
        pair[block : 2 * block, :] = back[1, rows, :]
        dst_row = dst_all[b : b + 1, :]
        for e in range(0, edges, step):
            src_col = columns[e : e + step, b : b + 1]
            dst_col = columns[e : e + step, blocks + b : blocks + b + 1]
            src_wide = jnp.broadcast_to(src_col, (step, 128)).astype(jnp.int16)
            dst_wide = jnp.broadcast_to(dst_col, (step, block)).astype(jnp.int16)
            lane = lax.broadcasted_iota(jnp.int16, (step, block), 1)
            near_hot = jnp.where(lane == dst_wide, one, none)
            one_hot[e : e + step, 0:block] = near_hot
            one_hot[e : e + step, block : 2 * block] = near_hot
            for k in range(0, depth - block, 128):
                lane = lax.broadcasted_iota(jnp.int16, (step, 128), 1) + jnp.int16(k)
                hot = lane == src_wide
                if k <= slots < k + 128:
                    hot = hot | (lane == jnp.int16(slots))
                hot = jnp.where(hot, one, none)
                one_hot[e : e + step, 2 * block + k : 2 * block + k + 128] = hot
            pre = mm(one_hot[e : e + step, block : block + depth], table[...])
            grad = mm(one_hot[e : e + step, 0 : 2 * block], pair[...])
            bent = jnp.tanh(pre)
            rise = 1.0 + bent
            act = pre * rise
            hid[e : e + step, :] = act.astype(BF16)
            at = slice(b * edges + e, b * edges + e + step)
            pgrad[at, :] = (grad * (rise + act * (1.0 - bent))).astype(BF16)
        sub = lax.broadcasted_iota(jnp.int32, (block, edges), 0)
        one_hot_t[...] = jnp.where(sub == dst_row, 1.0, 0.0).astype(BF16)
        node = mm(one_hot_t[...], pgrad[b * edges : (b + 1) * edges, :])
        bias_total = bias_total + jnp.sum(node, axis=0, keepdims=True)
        node_sum[rows, :] = node.astype(BF16)
        hid_sum[rows, :] = mm(one_hot_t[...], hid[...]).astype(BF16)

    bias_sum[...] = jnp.broadcast_to(bias_total, bias_sum.shape)
    grads[0:width, :] = mm(hid_sum[...], cot[...], 0, 0)
    grads[width : 2 * width, :] = mm(mesh[...], node_sum[...], 0, 0)
    split_pieces(device_count, 0, grads, kept, sent)


def mesh_kernel(mesh, hid_sum, w_out, mesh_out):
    mesh_out[...] = (mesh[...].astype(F32) + mm(hid_sum[...], w_out[...])).astype(BF16)


def scatter_rows(src, pgrad, one_hot_t, first_block, block_count):
    edges = src.shape[1]
    slots = one_hot_t.shape[0]
    one, none = jnp.ones((), BF16), jnp.zeros((), BF16)
    for b in range(first_block, first_block + block_count):
        at = slice((b - first_block) * edges, (b - first_block + 1) * edges)
        for r in range(0, slots, 128):
            size = min(128, slots - r)
            sub = lax.broadcasted_iota(jnp.int16, (size, edges), 0) + jnp.int16(r)
            row = jnp.broadcast_to(src[b : b + 1, :], (size, edges)).astype(jnp.int16)
            one_hot_t[r : r + size, at] = jnp.where(sub == row, one, none)
    rows = slice(first_block * edges, (first_block + block_count) * edges)
    return mm(one_hot_t[...], pgrad[rows, :])


def scatter_kernel(src, pgrad, slot_sum, one_hot_t):
    slot_sum[...] = scatter_rows(src, pgrad, one_hot_t, 0, src.shape[0] // 2)


def backward_kernel(
    channels,
    device_count,
    src,
    pgrad,
    slot_half,
    latent,
    feat,
    slope,
    w_src,
    bias_sum,
    kept,
    sent,
    one_hot_t,
    grads,
):
    width = w_src.shape[0]
    padded = feat.shape[1]
    half = src.shape[0] // 2
    rest = src.shape[0] - half
    slot_sum = slot_half[...] + scatter_rows(src, pgrad, one_hot_t, half, rest)
    slot_grad = slot_sum.astype(BF16)
    grads[0:width, :] = mm(latent[...], slot_grad)
    buffer_grad = mm(slot_grad, w_src[...], 1, 1)
    embed = (buffer_grad * slope[...]).astype(BF16)
    grads[width : width + padded, :] = mm(feat[...], embed, 0, 0)
    grads[width + channels + 1 : width + channels + 2, :] = bias_sum[0:1, :]
    if grads.shape[0] > width + padded:
        spare = grads.shape[0] - width - padded
        grads[width + padded :, :] = jnp.zeros((spare, width), F32)
    split_pieces(device_count, 1, grads, kept, sent)


def segments(bounds, half_rows):
    found = []
    for half in range(2):
        for index, (low, high) in enumerate(bounds):
            begin, end = max(low, half * half_rows), min(high, (half + 1) * half_rows)
            if begin < end:
                found.append((half, index, begin, end))
    return found


def unpack_kernel(device_count, chains, own_half, *refs):
    count = sum(len(bounds) for _, bounds in chains)
    chain_rows, refs = refs[0 : len(chains)], refs[len(chains) :]
    targets = refs[0:count] if own_half else refs[count : 2 * count]
    buffers, sems = refs[count if own_half else 2 * count : -1], refs[-1]

    def move(half, turn, bounds, rows, base, skip):
        _, masks, pieces = place(device_count, turn)
        parts = segments(bounds, rows.shape[0])
        piece = rows.shape[0] // pieces
        for p in range(pieces):
            begin = half * rows.shape[0] + p * piece
            at = pl.ds(pl.multiple_of((p ^ masks[half]) * piece, 16), piece)
            values = rows[at, :].astype(F32)
            for k, (owner, _, low, high) in enumerate(parts):
                lo, hi = max(low, begin), min(high, begin + piece)
                if owner == half and lo < hi:
                    buffers[skip + k][lo - low : hi - low, :] = values[lo - begin : hi - begin, :]
        copies = []
        for k, (owner, index, low, high) in enumerate(parts):
            if owner == half:
                target = targets[base + index]
                if high - low < target.shape[0]:
                    first = low - bounds[index][0]
                    target = target.at[first : first + high - low, :]
                copies.append(fetch(buffers[skip + k], target, sems, skip + k))
        return copies

    def move_all(half):
        base, skip, copies = 0, 0, []
        for (turn, bounds), rows in zip(chains, chain_rows):
            copies += move(half, turn, bounds, rows, base, skip)
            base += len(bounds)
            skip += len(segments(bounds, rows.shape[0]))
        for copy in copies:
            copy.wait()

    core = lax.rem(lax.axis_index("dom"), 2)
    which = core if own_half else 1 - core
    for half in range(2):
        pl.when(which == half)(functools.partial(move_all, half))


def shards(
    grid_feat,
    mesh_latent,
    cotangent,
    row_pack,
    edge_src,
    edge_dst,
    edge_count,
    w_embed,
    b_embed,
    w_src,
    w_dst,
    b_hidden,
    w_out,
):
    device_count = lax.axis_size("dom")
    own, channels = grid_feat.shape
    width = w_src.shape[0]
    peer_slots = row_pack.shape[0] // device_count
    more = device_count * peer_slots
    slots = own + more
    blocks, edges = edge_src.shape
    nodes = mesh_latent.shape[0]
    block = nodes // blocks
    padded = round_up(channels + 2, 128)
    depth = block + round_up(slots + 16, 128)
    first, second, last_bit = stage_bits(device_count)
    pieces = 1 << len(first)
    mesh_rows = round_up(2 * width, 32 * pieces)
    grid_rows = round_up(width + padded, 32 * pieces)
    half_blocks = blocks // 2
    stages = list(zip(first, second)), list(zip(second, first))

    vmem = pl.BlockSpec(memory_space=pltpu.VMEM)
    smem = pl.BlockSpec(memory_space=pltpu.SMEM)
    hbm = pl.BlockSpec(memory_space=pltpu.HBM)
    shape = jax.ShapeDtypeStruct

    def limit(mib):
        return pltpu.CompilerParams(vmem_limit_bytes=mib * 1024 * 1024)

    feat_t = grid_feat.T
    dma = pltpu.SemaphoreType.DMA
    flag = pl.pallas_call(
        begin_kernel,
        out_shape=shape((8, 128), F32),
        out_specs=vmem,
        compiler_params=limit(1),
        cost_estimate=pl.CostEstimate(
            flops=20_000_000_000, bytes_accessed=own * padded * 2, transcendentals=0
        ),
        name="begin",
    )()
    send = pl.pallas_call(
        pick_kernel,
        out_shape=shape((device_count, peer_slots, padded), BF16),
        in_specs=[vmem] * 3,
        out_specs=vmem,
        compiler_params=limit(16),
        cost_estimate=pl.CostEstimate(
            flops=20_000_000_000, bytes_accessed=own * padded * 2, transcendentals=0
        ),
        name="pick_rows",
    )(flag, row_pack[None, :], feat_t)
    feat_in = lax.all_to_all(send, "dom", split_axis=0, concat_axis=0, tiled=True)

    forward_macs = (
        slots * width * (padded + width)
        + blocks * edges * width * (depth + 4 * block)
        + 5 * nodes * width * width
    )
    hid_sum, pgrad, latent, feat, slope, bias_sum, kept_mesh, sent_mesh = pl.pallas_call(
        functools.partial(forward_kernel, device_count),
        out_shape=(
            shape((nodes, width), BF16),
            shape((blocks * edges, width), BF16),
            shape((width, slots), BF16),
            shape((slots, padded), BF16),
            shape((slots, width), F32),
            shape((8, width), F32),
            shape((mesh_rows // 2, width), F32),
            shape((mesh_rows // 2, width), BF16),
        ),
        in_specs=[smem] + [vmem] * 12,
        out_specs=(vmem,) * 8,
        scratch_shapes=[
            pltpu.VMEM((padded, width), BF16),
            pltpu.VMEM((depth, width), BF16),
            pltpu.VMEM((2 * block, width), BF16),
            pltpu.VMEM((padded, width), F32),
            pltpu.VMEM((more, padded), F32),
            pltpu.VMEM((edges, depth + block), BF16),
            pltpu.VMEM((block, edges), BF16),
            pltpu.VMEM((edges, width), BF16),
            pltpu.VMEM((nodes, width), BF16),
            pltpu.VMEM((2, nodes, width), BF16),
            pltpu.VMEM((nodes, width), BF16),
            pltpu.VMEM((mesh_rows, width), F32),
        ],
        compiler_params=limit(40),
        cost_estimate=pl.CostEstimate(
            flops=2 * forward_macs,
            bytes_accessed=16 * own * width,
            transcendentals=blocks * edges * width,
        ),
        name="forward_rows",
    )(
        edge_count,
        edge_src,
        edge_dst,
        feat_in,
        feat_t,
        w_embed,
        b_embed,
        b_hidden,
        w_src,
        w_dst,
        w_out,
        mesh_latent,
        cotangent,
    )

    def swap(values, bits):
        return lax.ppermute(
            values, "dom", [(d, d ^ (1 << bits[d % 2])) for d in range(device_count)]
        )

    def cut(held):
        middle = held.shape[0] // 2
        return held[:middle], held[middle:].astype(BF16)

    def pair_sum(kept, sent):
        return cut(kept + swap(sent, (0, 0)).astype(F32))

    def reduce_pieces(turn, held, got, done=1):
        for bits in stages[turn][done:]:
            held, sent = cut(held + got.astype(F32))
            got = swap(sent, bits)
        held = (held + got.astype(F32)).astype(BF16)
        got = swap(held, (last_bit, last_bit))
        held = (held.astype(F32) + got.astype(F32)).astype(BF16)
        for bits in reversed(stages[turn]):
            held = jnp.concatenate([held, swap(held, bits)], axis=0)
        return held, swap(held, (0, 0))

    held_mesh, next_mesh = pair_sum(kept_mesh, sent_mesh)
    slot_half = pl.pallas_call(
        scatter_kernel,
        out_shape=shape((slots, width), F32),
        in_specs=[vmem] * 2,
        out_specs=vmem,
        scratch_shapes=[pltpu.VMEM((slots, half_blocks * edges), BF16)],
        compiler_params=limit(24),
        cost_estimate=pl.CostEstimate(
            flops=2 * half_blocks * edges * slots * width,
            bytes_accessed=half_blocks * edges * width * 2,
            transcendentals=0,
        ),
        name="scatter_rows",
    )(edge_src, pgrad)

    slot_half, held_mesh, next_mesh = lax.optimization_barrier((slot_half, held_mesh, next_mesh))
    got_mesh = swap(next_mesh, stages[0][0])
    kept_grid, sent_grid = pl.pallas_call(
        functools.partial(backward_kernel, channels, device_count),
        out_shape=(
            shape((grid_rows // 2, width), F32),
            shape((grid_rows // 2, width), BF16),
        ),
        in_specs=[vmem] * 8,
        out_specs=(vmem,) * 2,
        scratch_shapes=[
            pltpu.VMEM((slots, (blocks - half_blocks) * edges), BF16),
            pltpu.VMEM((grid_rows, width), F32),
        ],
        compiler_params=limit(40),
        cost_estimate=pl.CostEstimate(
            flops=2 * slots * width * (half_blocks * edges + 2 * width + 2 * padded),
            bytes_accessed=half_blocks * edges * width * 2,
            transcendentals=slots * width,
        ),
        name="backward_rows",
    )(edge_src, pgrad, slot_half, latent, feat, slope, w_src, bias_sum)


    mesh_out = pl.pallas_call(
        mesh_kernel,
        out_shape=shape((nodes, width), BF16),
        in_specs=[vmem] * 3,
        out_specs=vmem,
        compiler_params=limit(16),
        cost_estimate=pl.CostEstimate(
            flops=2 * nodes * width * width, bytes_accessed=8 * nodes * width, transcendentals=0
        ),
        name="mesh_rows",
    )(mesh_latent, hid_sum, w_out)

    def unpack(chains, pairs):
        sizes = [high - low for _, bounds in chains for low, high in bounds]
        parts = [
            high - low
            for (_, bounds), (rows, _) in zip(chains, pairs)
            for _, _, low, high in segments(bounds, rows.shape[0])
        ]
        targets = ()
        for own_half, chain_rows in zip((True, False), zip(*pairs)):
            targets = pl.pallas_call(
                functools.partial(unpack_kernel, device_count, chains, own_half),
                out_shape=tuple(shape((size, width), F32) for size in sizes),
                in_specs=[vmem] * len(chains) + [hbm] * len(targets),
                out_specs=(hbm,) * len(sizes),
                scratch_shapes=[pltpu.VMEM((size, width), F32) for size in parts]
                + [dma((len(parts),))],
                input_output_aliases={len(chains) + k: k for k in range(len(targets))},
                compiler_params=limit(12),
                name="unpack_rows",
            )(*chain_rows, *targets)
        return targets

    mesh_out, got_mesh = lax.optimization_barrier((mesh_out, got_mesh))
    held_mesh, next_mesh = cut(held_mesh + got_mesh.astype(F32))
    held_grid, next_grid = pair_sum(kept_grid, sent_grid)
    next_grid, next_mesh = lax.optimization_barrier((next_grid, next_mesh))
    got_mesh = swap(next_mesh, stages[0][1])
    mesh_pair = reduce_pieces(0, held_mesh, got_mesh, 2)
    grid_pair = reduce_pieces(1, held_grid, swap(next_grid, stages[1][0]))
    end = width + channels
    mesh_bounds = ((0, width), (width, 2 * width))
    grid_bounds = ((0, width), (width, end), (end, end + 2))
    grad_out, grad_dst, grad_src, grad_embed, biases = unpack(
        ((0, mesh_bounds), (1, grid_bounds)), (mesh_pair, grid_pair)
    )
    return mesh_out, grad_embed, grad_src, grad_dst, grad_out, biases


def solution(mesh):
    return jax.shard_map(
        shards,
        mesh=mesh,
        in_specs=(
            P(("ens", "dom"), None),
            P(("ens", "dom"), None),
            P(("ens", "dom"), None),
            P("dom"),
            P("dom", None),
            P("dom", None),
            P("dom"),
            P(),
            P(),
            P(),
            P(),
            P(),
            P(),
        ),
        out_specs=(
            P(("ens", "dom"), None),
            P("ens", None),
            P("ens", None),
            P("ens", None),
            P("ens", None),
            P("ens", None),
        ),
        check_vma=False,
    )
```
